128 devices in a mesh: leaf: 32 (over z, y, core), sub: 4 (over x).
Axes of the slice: x: 4, y: 4, z: 4, core: 2. Of those that a mesh axis runs over, the one named last changes fastest.
Arguments:
- volume_fraction: float32 [256, 64, 1024], P('leaf', 'sub'), may hold values from 0 to 1
- interface_mask: int32 [256, 64, 1024], P('leaf', 'sub'), may hold values 0 or 1
Outputs:
- pressure: float32 [256, 64, 1024], P('leaf', 'sub')
- residual: float32 [256, 64, 1024], P('leaf', 'sub')
The draws below stay inside these ranges and needn't reach their ends.
All inputs are finite; a program needn't handle non-finite values. No bound on the sum of `interface_mask` on one device may be relied on, other than what follows from the above.
Results may differ from the reference program's by a relative error of at most 0.0003.
Values sent between devices are 32-bit elements; how exact they have to be, the bound alone decides.
No kernel may reach another device: no remote copies, remote signals or barrier semaphores. Data moves between devices by JAX's collectives and lax.ppermute only.
A program may use at most 128 MiB of HBM per device.

```python
import jax
import jax.numpy as jnp

CZ = 1024
LEV = 3
NU = 2
COARSE = 8
NX = 256
NY = 64


def set_ends(array, key, smallest, largest):
    extent = array.shape
    place = [jax.random.randint(jax.random.fold_in(key, axis), (), 0, extent[axis]) for axis in range(len(extent))]
    array = array.at[tuple(place)].set(smallest)
    longest = extent.index(max(extent))
    place[longest] = (place[longest] + 1) % extent[longest]
    return array.at[tuple(place)].set(largest)


def levels(stream_key, extent, cuts, low, top_value):
    factor_of = 1.0
    for dim, blocks in cuts:
        steps = jax.random.uniform(jax.random.fold_in(jax.random.fold_in(stream_key, 6), dim), (blocks,), jnp.float32, low / len(cuts), top_value / len(cuts))
        factor_of = factor_of * jnp.repeat(jnp.exp(steps), extent[dim] // blocks).reshape((-1,) + (1,) * (len(extent) - 1 - dim))
    return factor_of


def setup_inputs(seed: int = 0) -> dict:
    streams_of = jax.random.split(jax.random.key(seed), 3)
    volume_fraction = jnp.clip(1.0 * jax.random.uniform(streams_of[0], (NX, NY, CZ), jnp.float32) ** levels(streams_of[0], (NX, NY, CZ), ((0, 32), (1, 4)), -0.2, 0.2), 0.0, 1.0)
    interface_mask = set_ends((jax.random.randint(streams_of[1], (NX, NY, CZ), 0, 2) < 1).astype(jnp.int32), jax.random.fold_in(streams_of[1], 1), 0, 1)
    return {"volume_fraction": volume_fraction, "interface_mask": interface_mask}


damping = 0.8 / 6.0

def neighbours(padded):
    total = padded[2:, 1:-1, 1:-1] + padded[:-2, 1:-1, 1:-1]
    total = total + padded[1:-1, 2:, 1:-1] + padded[1:-1, :-2, 1:-1]
    total = total + padded[1:-1, 1:-1, 2:] + padded[1:-1, 1:-1, :-2]
    return total

def apply_op(field):
    return 6.0 * field - neighbours(jnp.pad(field, 1))

def sweep(field, rhs):
    return field + damping * (rhs - apply_op(field))

def restrict(field):
    nx, ny, nz = field.shape
    return 0.5 * field.reshape(nx // 2, 2, ny // 2, 2, nz // 2, 2).sum(axis=(1, 3, 5))

def prolong(field):
    return jnp.repeat(jnp.repeat(jnp.repeat(field, 2, 0), 2, 1), 2, 2)

def curvature_source(volume_fraction, interface_mask):
    depth = volume_fraction.shape[2]
    column = jnp.pad(volume_fraction, ((0, 0), (0, 0), (3, 3)))
    heights = column[:, :, 0:depth]
    for shift in range(1, 7):
        heights = heights + column[:, :, shift:shift + depth]
    padded = jnp.pad(heights, ((1, 1), (1, 1), (0, 0)))
    upper_x = padded[2:, 1:-1]
    lower_x = padded[:-2, 1:-1]
    upper_y = padded[1:-1, 2:]
    lower_y = padded[1:-1, :-2]
    slope_x = 0.5 * (upper_x - lower_x)
    slope_y = 0.5 * (upper_y - lower_y)
    bend = upper_x - 2.0 * heights + lower_x + (upper_y - 2.0 * heights + lower_y)
    factor = 1.0 + slope_x * slope_x + slope_y * slope_y
    curvature = bend / (factor * jnp.sqrt(factor))
    grad_z = 0.5 * (column[:, :, 4:depth + 4] - column[:, :, 2:depth + 2])
    return interface_mask.astype(jnp.float32) * curvature * grad_z

def reference(volume_fraction, interface_mask):
    source = curvature_source(volume_fraction, interface_mask)
    rhs = source
    stored = []
    rights = []
    for level in range(LEV):
        field = jnp.zeros_like(rhs)
        for step in range(NU):
            field = sweep(field, rhs)
        remain = rhs - apply_op(field)
        stored.append(field)
        rights.append(rhs)
        rhs = restrict(remain)
    field = jnp.zeros_like(rhs)
    for step in range(COARSE):
        field = sweep(field, rhs)
    for level in range(LEV - 1, -1, -1):
        field = stored[level] + prolong(field)
        for step in range(NU):
            field = sweep(field, rights[level])
    return (field, source - apply_op(field))
```

```python
import functools

import jax
import jax.numpy as jnp
from jax import lax
from jax.experimental import pallas as pl
from jax.experimental.pallas import tpu as pltpu
from jax.sharding import PartitionSpec as P

D = 0.8 / 6.0
C1 = 2.0 * D - 6.0 * D * D
C2 = D * D
C0 = 1.0 - 6.0 * D
NX, NY = 8, 16
LANES = 128
AXES = ("leaf", "sub")
f32 = jnp.float32


def lanes(rows):
    return lax.broadcasted_iota(jnp.int32, (rows, LANES), 1)


def rows_of(rows):
    return lax.broadcasted_iota(jnp.int32, (rows, LANES), 0)


def along_z(cols):
    lane = lanes(cols[0].shape[0])
    first, last = lane == 0, lane == LANES - 1
    right = [pltpu.roll(c, 1, 1) for c in cols]
    left = [pltpu.roll(c, LANES - 1, 1) for c in cols]
    n = len(cols)
    before = [jnp.where(first, right[k - 1] if k else 0.0, right[k]) for k in range(n)]
    after = [jnp.where(last, left[k + 1] if k < n - 1 else 0.0, left[k]) for k in range(n)]
    return before, after


def around(ref, x, whole=False):
    n, rows = ref.shape[1], ref.shape[2]
    cols = [ref[x, k] for k in range(n)]
    before, after = along_z(cols)
    out = []
    for k, c in enumerate(cols):
        up, down = pltpu.roll(c, rows - 1, 0), pltpu.roll(c, 1, 0)
        if whole:
            row = rows_of(rows)
            up, down = jnp.where(row == rows - 1, 0.0, up), jnp.where(row == 0, 0.0, down)
        out.append((ref[x + 1, k] + ref[x - 1, k]) + (up + down) + (before[k] + after[k]))
    return cols, out


def pairs_z(even, odd):
    lane = lanes(even.shape[0])
    take = (lane * 2) % LANES
    got = [
        jnp.take_along_axis(c + pltpu.roll(c, LANES - 1, 1), take, axis=1, mode="promise_in_bounds") for c in (even, odd)
    ]
    return jnp.where(lane < LANES // 2, got[0], got[1])


def twice_z(col):
    lane = lanes(col.shape[0])
    return [jnp.take_along_axis(col, lane // 2 + h * (LANES // 2), axis=1, mode="promise_in_bounds") for h in (0, 1)]


def restricted(tmp, rows):
    sums = [tmp[k, pl.ds(0, rows, 2), :] + tmp[k, pl.ds(1, rows, 2), :] for k in range(tmp.shape[0])]
    return [0.5 * pairs_z(sums[2 * m], sums[2 * m + 1]) for m in range(tmp.shape[0] // 2)]


def prolonged(tmp, cols, rows, at=0):
    for m, c in enumerate(cols):
        for h, e in enumerate(twice_z(c)):
            tmp[2 * m + h, pl.ds(at, rows, 2), :] = e
            tmp[2 * m + h, pl.ds(at + 1, rows, 2), :] = e


def inside(pos, count):
    return jnp.logical_and(pos >= 0, pos < count)


def row_mask(rows, start, count):
    pos = rows_of(rows) + start
    return jnp.where(inside(pos, count), 1.0, 0.0).astype(f32)


def plane_mask(mask, x, count):
    return mask * jnp.where(inside(x, count), 1.0, 0.0).astype(f32)


def each(lo, hi, body):
    def step(x, carry):
        body(x)
        return carry

    lax.fori_loop(lo, hi, step, 0)


def taps(cols):
    lane = lanes(cols[0].shape[0])
    before, after = along_z(cols)
    n = len(cols)
    three = [before[k] + cols[k] + after[k] for k in range(n)]
    right = [pltpu.roll(c, 2, 1) for c in three]
    left = [pltpu.roll(c, LANES - 2, 1) for c in three]
    out = []
    for k in range(n):
        lo = right[k - 1] if k else jnp.where(lane == 1, before[0], 0.0)
        hi = left[k + 1] if k < n - 1 else jnp.where(lane == LANES - 2, after[n - 1], 0.0)
        out.append(cols[k] + jnp.where(lane < 2, lo, right[k]) + jnp.where(lane >= LANES - 2, hi, left[k]))
    return out, before, after


def split(value):
    return [value[:, k * LANES : (k + 1) * LANES] for k in range(value.shape[1] // LANES)]


def place(leaves, subs):
    i, j = lax.axis_index("leaf"), lax.axis_index("sub")
    odd_i, odd_j = i % 2 == 1, j % 2 == 1
    far_i = jnp.where(odd_i, i < leaves - 1, i > 0)
    far_j = jnp.where(odd_j, j < subs - 1, j > 0)
    return i, j, odd_i, odd_j, far_i, far_j


def descent(dims, vf, mask, ra, rb, rs1, rs2, src, big_a, big_b, c1_out, c2_out, m2a, m2b, own2, F1c, H, F0, U0, T0, F1, U1, T1):
    leaves, subs = dims
    i, j, odd_i, odd_j, far_i, far_j = place(leaves, subs)
    nz = vf.shape[2] // LANES
    zero = jnp.zeros((16, LANES), f32)

    def level0(x):
        h, before, after = taps(split(vf[x]))
        m = mask[x].astype(f32)
        for k in range(nz):
            H[x + 1, k] = h[k]
            U0[x, k, 0:16, :] = (after[k] - before[k]) * (0.5 * m[:, k * LANES : (k + 1) * LANES])

    each(0, NX, level0)
    far_x = jnp.where(far_i, 1.0, 0.0).astype(f32)
    far_y = jnp.where(far_j, 1.0, 0.0).astype(f32)
    ha, _, _ = taps(split(ra[0]))
    hb, _, _ = taps(split(rb[0]))
    hs1, _, _ = taps(split(rs1[...]))
    hs2, _, _ = taps(split(rs2[...]))
    for k in range(nz):
        b = hb[k] * far_x
        H[0, k] = jnp.where(odd_i, ha[k], b)
        H[NX + 1, k] = jnp.where(odd_i, b, ha[k])
    row = rows_of(16)
    low = [jnp.where(odd_j, hs1[k], hs2[k] * far_y) for k in range(nz)]
    high = [jnp.where(odd_j, hs2[k] * far_y, hs1[k]) for k in range(nz)]

    zero24 = jnp.zeros((24, LANES), f32)
    for x in (0, 1, 2, 3, 12, 13, 14, 15):
        for k in range(nz):
            F0[x, k] = zero24
    for x in range(NX):
        for k in range(nz):
            h = H[x + 1, k]
            up = jnp.where(row == 15, high[k][x : x + 1, :], pltpu.roll(h, 15, 0))
            down = jnp.where(row == 0, low[k][x : x + 1, :], pltpu.roll(h, 1, 0))
            ahead, behind = H[x + 2, k], H[x, k]
            sx, sy = 0.5 * (ahead - behind), 0.5 * (up - down)
            bend = ahead - 2.0 * h + behind + (up - 2.0 * h + down)
            inv = lax.rsqrt(1.0 + sx * sx + sy * sy)
            f = U0[x, k, 0:16, :] * (bend * (inv * inv * inv))
            src[x, :, k * LANES : (k + 1) * LANES] = f
            F0[x + 4, k, 0:4, :] = zero24[0:4]
            F0[x + 4, k, 4:20, :] = f
            F0[x + 4, k, 20:24, :] = zero24[0:4]

    count_x, count_y = leaves * NX, subs * NY
    my0 = row_mask(24, j * NY - 4, count_y)
    for x in (1, 2, 13, 14):
        for k in range(nz):
            U0[x, k] = zero24

    def smooth0(x):
        m = plane_mask(my0, i * NX + x - 4, count_x)
        f, around_f = around(F0, x)
        for k in range(nz):
            U0[x, k] = (C1 * f[k] + C2 * around_f[k]) * m

    each(3, 13, smooth0)

    for x in range(0, 14):
        if x < 4 or x >= 10:
            for k in range(nz // 2):
                F1[x, k] = zero

    def restrict0(c):
        total = [zero24] * nz
        for p in (0, 1):
            x = 2 * c + p
            m = plane_mask(my0, i * NX + x - 4, count_x)
            u, around_u = around(U0, x)
            total = [total[k] + (F0[x, k] - 6.0 * u[k] + around_u[k]) * m for k in range(nz)]
        for k in range(nz):
            T0[k] = total[k]
        for k, v in enumerate(restricted(T0, 12)):
            F1[c + 3, k, 0:2, :] = zero[0:2]
            F1[c + 3, k, 2:14, :] = v
            F1[c + 3, k, 14:16, :] = zero[0:2]

    each(1, 7, restrict0)

    n1 = nz // 2
    my1 = row_mask(16, j * (NY // 2) - 4, count_y // 2)
    for x in (0, 1, 2, 11, 12, 13):
        for k in range(n1):
            U1[x, k] = zero

    def smooth1(x):
        m = plane_mask(my1, i * (NX // 2) + x - 5, count_x // 2)
        f, around_f = around(F1, x)
        for k in range(n1):
            U1[x, k] = (C1 * f[k] + C2 * around_f[k]) * m

    each(3, 11, smooth1)

    def restrict1(c):
        total = [zero] * n1
        for p in (0, 1):
            x = 2 * c + 1 + p
            m = plane_mask(my1, i * (NX // 2) + x - 5, count_x // 2)
            u, around_u = around(U1, x)
            total = [total[k] + (F1[x, k] - 6.0 * u[k] + around_u[k]) * m for k in range(n1)]
        for k in range(n1):
            T1[k] = total[k]
        for k, v in enumerate(restricted(T1, 8)):
            F1c[c, :, k * LANES : (k + 1) * LANES] = v

    each(0, 6, restrict1)

    at = jnp.where(odd_i, 0, 4)
    m2a[...] = F1c[pl.ds(at, 2)]
    m2b[...] = F1c[pl.ds(4 - at, 2)]
    own2[...] = F1c[2:4]
    for x in range(4):
        big_a[x] = src[at + x]
        big_b[x] = src[4 - at + x]
    for p in range(3):
        for k in range(n1):
            for h in (0, 1):
                v = F1[4 + p + 3 * h, k]
                big_a[4 + p, :, (h * n1 + k) * LANES : (h * n1 + k + 1) * LANES] = v
                big_b[4 + p, :, (h * n1 + k) * LANES : (h * n1 + k + 1) * LANES] = v
    odd_c = (i // 2) % 2 == 1
    first = jnp.where(odd_c, 4, 8)
    for k in range(n1):
        for h in (0, 1):
            s = slice((h * n1 + k) * LANES, (h * n1 + k + 1) * LANES)
            c1_out[0, :, s] = F1[first + h, k]
            c2_out[0, :, s] = F1[12 - first + h, k]


def sum2(dims, own2, ra, rb, out):
    far = place(*dims)[4]
    v = own2[...] + ra[...] + jnp.where(far, rb[...], 0.0)
    for k in range(out.shape[0]):
        out[k] = v


def chip2(dims, got, out):
    odd_i = place(*dims)[2]
    half = got.shape[3] // 2
    row = lax.broadcasted_iota(jnp.int32, (8, half), 0)
    for c in (0, 1):
        for x in (0, 1):
            t = [jnp.where(odd_i, got[4 * c + j, x, :, half:], got[4 * c + j, x, :, :half]) for j in range(4)]
            one, two = pltpu.roll(t[1], 2, 0), pltpu.roll(t[2], 6, 0)
            lo = jnp.where(row < 6, pltpu.roll(t[0], 6, 0), two) + jnp.where(row >= 2, one, 0.0)
            hi = jnp.where(row >= 2, pltpu.roll(t[3], 2, 0), one) + jnp.where(row < 6, two, 0.0)
            for k in range(out.shape[0]):
                out[k, 2 * c + x, 0:8, :] = lo
                out[k, 2 * c + x, 8:16, :] = hi


def rows_out(dims, src, F1own, ra, rb, rc1, rc2, f1x, s1, s2):
    leaves, subs = dims
    i, j, odd_i, odd_j, far_i, far_j = place(leaves, subs)
    odd_c = (i // 2) % 2 == 1
    chips = leaves // 2
    c = i // 2
    far_c = jnp.where(odd_c, c < chips - 1, c > 0)
    n = src.shape[2] // 2

    def halves(ref, at, p):
        return ref[at + p % 3, :, (p // 3) * n : (p // 3 + 1) * n]

    a = [halves(ra, 4, p) for p in range(6)]
    b = [jnp.where(far_i, halves(rb, 4, p), 0.0) for p in range(6)]
    before = [jnp.where(odd_i, a[p], b[p]) for p in range(6)]
    after = [jnp.where(odd_i, b[p], a[p]) for p in range(6)]
    d1 = [rc1[0, :, h * n : (h + 1) * n] for h in (0, 1)]
    d2 = [jnp.where(far_c, rc2[0, :, h * n : (h + 1) * n], 0.0) for h in (0, 1)]
    before2 = [jnp.where(odd_c, d1[h], d2[h]) for h in (0, 1)]
    after2 = [jnp.where(odd_c, d2[h], d1[h]) for h in (0, 1)]
    own = [halves(F1own, 4, p) for p in range(6)]
    planes = {}

    def add(x, v):
        planes[x] = planes[x] + v if x in planes else v

    for p in range(6):
        add(p - 1, own[p])
        add(p - 5, before[p])
        add(p + 3, after[p])
    for h in (0, 1):
        add(-5 + h, before2[h])
        add(7 + h, after2[h])
    for x in range(14):
        f1x[x] = planes[x - 5]

    def fine(x):
        if 4 <= x < 12:
            return src[x - 4]
        if x < 4:
            return jnp.where(odd_i, ra[x], jnp.where(far_i, rb[x], 0.0))
        return jnp.where(odd_i, jnp.where(far_i, rb[x - 12], 0.0), ra[x - 12])

    for x in range(8):
        u, v = fine(x), fine(x + 8)
        for out, up in ((s1, odd_j == False), (s2, odd_j)):
            out[x, 0:4, :] = jnp.where(up, u[12:16], u[0:4])
            out[x, 4:8, :] = jnp.where(up, v[12:16], v[0:4])
    for x in range(14):
        v = planes[x - 5]
        s = slice((x // 7) * n, (x // 7 + 1) * n)
        last, first = v[5:13], v[3:11]
        s1[8 + x % 7, :, s] = jnp.where(odd_j, first, last)
        s2[8 + x % 7, :, s] = jnp.where(odd_j, last, first)


def ascent(dims, mine, other, src, ra, rb, f1x, rs1, rs2, press, resid, F2, U2, T2, G3, U3, V3, W2, X2, T1, F1, V1, X1, T0, F0, V0, X0):
    leaves, subs = dims
    i, j, odd_i, odd_j, far_i, far_j = place(leaves, subs)
    count_x, count_y = leaves * NX, subs * NY
    nz = src.shape[2] // LANES
    n1, n2 = nz // 2, nz // 4
    x2 = count_x // 4
    zero = jnp.zeros((24, LANES), f32)

    for x in list(range(5)) + list(range(x2 + 5, x2 + 10)):
        for k in range(n2):
            F2[x, k] = zero[0:16]
            U2[x, k] = zero[0:16]
    h2 = n2 // 2

    def fill2(x):
        a, b = mine[x], other[x]
        for k in range(h2):
            s = slice(k * LANES, (k + 1) * LANES)
            F2[x + 5, k] = jnp.where(odd_i, b[:, s], a[:, s])
            F2[x + 5, h2 + k] = jnp.where(odd_i, a[:, s], b[:, s])

    each(0, x2, fill2)

    def smooth2(x):
        f, around_f = around(F2, x, True)
        for k in range(n2):
            U2[x, k] = C1 * f[k] + C2 * around_f[k]

    each(5, x2 + 5, smooth2)

    x3 = x2 // 2

    def restrict2(c):
        total = [zero[0:16]] * n2
        for p in (0, 1):
            x = 5 + 2 * c + p
            u, around_u = around(U2, x, True)
            total = [total[k] + (F2[x, k] - 6.0 * u[k] + around_u[k]) for k in range(n2)]
        for k in range(n2):
            T2[k] = total[k]
        for k, v in enumerate(restricted(T2, 8)):
            G3[c + 2, k] = v
            U3[c + 2, k] = D * v

    each(0, x3, restrict2)
    n3 = n2 // 2
    for x in (0, 1, x3 + 2, x3 + 3):
        for k in range(n3):
            G3[x, k] = zero[0:8]
            U3[x, k] = zero[0:8]
            V3[x, k] = zero[0:8]

    def sweep3(old, new):
        def body(x):
            u, around_u = around(old, x, True)
            for k in range(n3):
                new[x, k] = C0 * u[k] + D * (G3[x, k] + around_u[k])

        each(2, x3 + 2, body)

    for _ in range(3):
        sweep3(U3, V3)
        sweep3(V3, U3)
    sweep3(U3, V3)

    def window2(c):
        x = c // 2
        prolonged(T2, [V3[i + x, k] for k in range(n3)], 8)
        for p in (0, 1):
            w = c + p
            for k in range(n2):
                W2[w, k] = U2[2 * i + 1 + w, k] + T2[k]

    for c in range(0, 10, 2):
        window2(c)
    m2 = jnp.ones((16, LANES), f32)

    def sweep2(old, new, lo, hi):
        for w in range(lo, hi):
            m = plane_mask(m2, 2 * i + w - 4, x2)
            u, around_u = around(old, w, True)
            for k in range(n2):
                new[w, k] = (C0 * u[k] + D * (F2[2 * i + 1 + w, k] + around_u[k])) * m

    for w in range(10):
        m = plane_mask(m2, 2 * i + w - 4, x2)
        for k in range(n2):
            W2[w, k] = W2[w, k] * m
    sweep2(W2, X2, 1, 9)
    sweep2(X2, W2, 2, 8)

    for k in range(n1):
        T1[k] = zero
    low_j = jnp.where(j > 0, 1.0, 0.0).astype(f32)
    high_j = jnp.where(j < subs - 1, 1.0, 0.0).astype(f32)

    def fill1(x):
        part, at = x // 7, 8 + x % 7
        for k in range(n1):
            s = slice(k * LANES, (k + 1) * LANES)
            F1[x, k] = zero
            F1[x, k, 4:20, :] = f1x[x, :, s]
            s = slice((part * n1 + k) * LANES, (part * n1 + k + 1) * LANES)
            lo = jnp.where(odd_j, rs1[at, :, s], rs2[at, :, s]) * low_j
            hi = jnp.where(odd_j, rs2[at, :, s], rs1[at, :, s]) * high_j
            F1[x, k, 1:9, :] = F1[x, k, 1:9, :] + lo
            F1[x, k, 15:23, :] = F1[x, k, 15:23, :] + hi

    for x in range(14):
        fill1(x)
    my1 = row_mask(24, j * (NY // 2) - 8, count_y // 2)

    for c in range(6):
        cols = [pltpu.roll(W2[c + 2, k], (18 - 4 * j) % 16, 0)[0:8] for k in range(n2)]
        prolonged(T1, cols, 8, 4)
        for p in (0, 1):
            x = 2 * c + p + 1
            m = plane_mask(my1, i * (NX // 2) + x - 5, count_x // 2)
            f, around_f = around(F1, x)
            for k in range(n1):
                V1[x, k] = (C1 * f[k] + C2 * around_f[k] + T1[k]) * m

    def sweep1(old, new, lo, hi):
        def body(x):
            m = plane_mask(my1, i * (NX // 2) + x - 5, count_x // 2)
            u, around_u = around(old, x)
            for k in range(n1):
                new[x, k] = (C0 * u[k] + D * (F1[x, k] + around_u[k])) * m

        each(lo, hi, body)

    sweep1(V1, X1, 2, 12)
    sweep1(X1, V1, 3, 11)

    far_x = jnp.where(far_i, 1.0, 0.0).astype(f32)

    def fill0(x):
        if 4 <= x < 12:
            v = src[x - 4]
        elif x < 4:
            v = jnp.where(odd_i, ra[x], rb[x] * far_x)
        else:
            v = jnp.where(odd_i, rb[x - 12] * far_x, ra[x - 12])
        a, b = rs1[x % 8], rs2[x % 8]
        h = 4 * (x // 8)
        lo = jnp.where(odd_j, a[h : h + 4], b[h : h + 4]) * low_j
        hi = jnp.where(odd_j, b[h : h + 4], a[h : h + 4]) * high_j
        for k in range(nz):
            s = slice(k * LANES, (k + 1) * LANES)
            F0[x, k, 0:4, :] = lo[:, s]
            F0[x, k, 4:20, :] = v[:, s]
            F0[x, k, 20:24, :] = hi[:, s]

    for x in range(16):
        fill0(x)
    my0 = row_mask(24, j * NY - 4, count_y)

    def start0(c):
        prolonged(T0, [V1[c + 3, k, 6:18, :] for k in range(n1)], 12)
        for p in (0, 1):
            x = 2 * c + p

            @pl.when(jnp.logical_and(x > 0, x < 15))
            def _():
                m = plane_mask(my0, i * NX + x - 4, count_x)
                f, around_f = around(F0, x)
                for k in range(nz):
                    V0[x, k] = (C1 * f[k] + C2 * around_f[k] + T0[k]) * m

    each(0, 8, start0)

    def sweep0(old, new, lo, hi):
        def body(x):
            m = plane_mask(my0, i * NX + x - 4, count_x)
            u, around_u = around(old, x)
            for k in range(nz):
                new[x, k] = (C0 * u[k] + D * (F0[x, k] + around_u[k])) * m

        each(lo, hi, body)

    sweep0(V0, X0, 2, 14)
    sweep0(X0, V0, 3, 13)

    def finish(x):
        u, around_u = around(V0, x + 4)
        for k in range(nz):
            s = slice(k * LANES, (k + 1) * LANES)
            press[x, :, s] = u[k][4:20]
            resid[x, :, s] = (F0[x + 4, k] - 6.0 * u[k] + around_u[k])[4:20]

    each(0, NX, finish)


def call(kernel, outs, scratch, *args):
    return pl.pallas_call(
        kernel,
        out_shape=[jax.ShapeDtypeStruct(s, f32) for s in outs],
        scratch_shapes=[pltpu.VMEM(s, f32) for s in scratch],
        compiler_params=pltpu.CompilerParams(vmem_limit_bytes=48 * 1024 * 1024),
    )(*args)


def swaps(leaves, subs):
    def table(partner):
        return [(i * subs + j, (lambda t: t[0] * subs + t[1])(partner(i, j))) for i in range(leaves) for j in range(subs)]

    def odd(n):
        return ((n + 1) ^ 1) - 1

    def inner(n, count):
        return 0 <= n < count

    a = table(lambda i, j: (i ^ 1, j))
    b = table(lambda i, j: (odd(i), j) if inner(odd(i), leaves) else (i, j ^ 1))
    s1 = table(lambda i, j: (i, j ^ 1))
    s2 = table(lambda i, j: (i, odd(j)) if inner(odd(j), subs) else (i ^ 1, j))
    c1 = table(lambda i, j: (i ^ 2, j))
    c2 = table(lambda i, j: (2 * odd(i // 2) + i % 2, j) if inner(odd(i // 2), leaves // 2) else (i, j ^ 1))
    return a, b, s1, s2, c1, c2


def shards(dims, volume_fraction, interface_mask):
    leaves, subs = dims
    depth = volume_fraction.shape[2]
    nz = depth // LANES
    pa, pb, ps1, ps2, pc1, pc2 = swaps(leaves, subs)
    move = lambda v, table: lax.ppermute(v, AXES, table)
    i, j = lax.axis_index("leaf"), lax.axis_index("sub")
    odd_i, odd_j = i % 2, j % 2

    vf = volume_fraction
    at_x, at_y = (1 - odd_i) * (NX - 1), (1 - odd_j) * (NY - 1)
    plane = lambda x: lax.dynamic_slice_in_dim(vf, x, 1, 0)
    rows = lambda y: lax.dynamic_slice_in_dim(vf, y, 1, 1).reshape(NX, depth)
    ha, hb = move(plane(at_x), pa), move(plane(NX - 1 - at_x), pb)
    hs1, hs2 = move(rows(at_y), ps1), move(rows(NY - 1 - at_y), ps2)

    n1 = nz // 2
    src, big_a, big_b, m1, m2, m2a, m2b, own2 = call(
        functools.partial(descent, dims),
        [
            (NX, NY, depth),
            (7, 16, depth),
            (7, 16, depth),
            (1, 16, depth),
            (1, 16, depth),
            (2, 8, depth // 4),
            (2, 8, depth // 4),
            (2, 8, depth // 4),
        ],
        [
            (6, 8, depth // 4),
            (NX + 2, nz, 16, LANES),
            (16, nz, 24, LANES),
            (16, nz, 24, LANES),
            (nz, 24, LANES),
            (14, n1, 16, LANES),
            (14, n1, 16, LANES),
            (n1, 16, LANES),
        ],
        vf,
        interface_mask,
        ha,
        hb,
        hs1,
        hs2,
    )
    r2a, r2b = move(m2a, pa), move(m2b, pb)
    ra, rb = move(big_a, pa), move(big_b, pb)
    rc1, rc2 = move(m1, pc1), move(m2, pc2)

    (out,) = call(functools.partial(sum2, dims), [(2 * subs, 2, 8, depth // 4)], [], own2, r2a, r2b)
    group = [list(range(k, k + 2 * subs)) for k in range(0, leaves * subs, 2 * subs)]
    got = lax.all_to_all(out, AXES, 0, 0, axis_index_groups=group)
    chips = leaves // 2
    (out,) = call(functools.partial(chip2, dims), [(chips, 4, 16, depth // 8)], [], got)
    f1x, s1, s2 = call(
        functools.partial(rows_out, dims),
        [(14, 16, depth // 2), (15, 8, depth), (15, 8, depth)],
        [],
        src,
        big_a,
        ra,
        rb,
        rc1,
        rc2,
    )
    rs1, rs2 = move(s1, ps1), move(s2, ps2)
    group = [[(2 * c + k) * subs + s for c in range(chips)] for k in (0, 1) for s in range(subs)]
    mine = lax.all_to_all(out, AXES, 0, 0, axis_index_groups=group).reshape(4 * chips, 16, depth // 8)
    other = move(mine, pa)
    x2 = 2 * leaves
    press, resid = call(
        functools.partial(ascent, dims),
        [(NX, NY, depth), (NX, NY, depth)],
        [
            (x2 + 10, nz // 4, 16, LANES),
            (x2 + 10, nz // 4, 16, LANES),
            (nz // 4, 16, LANES),
            (x2 // 2 + 4, nz // 8, 8, LANES),
            (x2 // 2 + 4, nz // 8, 8, LANES),
            (x2 // 2 + 4, nz // 8, 8, LANES),
            (10, nz // 4, 16, LANES),
            (10, nz // 4, 16, LANES),
            (n1, 24, LANES),
            (14, n1, 24, LANES),
            (14, n1, 24, LANES),
            (14, n1, 24, LANES),
            (nz, 24, LANES),
            (16, nz, 24, LANES),
            (16, nz, 24, LANES),
            (16, nz, 24, LANES),
        ],
        mine,
        other,
        src,
        ra,
        rb,
        f1x,
        rs1,
        rs2,
    )
    return press, resid


def solution(mesh):
    spec = P("leaf", "sub", None)
    dims = (mesh.shape["leaf"], mesh.shape["sub"])
    body = functools.partial(shards, dims)
    return jax.shard_map(body, mesh=mesh, in_specs=(spec, spec), out_specs=(spec, spec), check_vma=False)
```

```python
import functools

import jax
import jax.numpy as jnp
from jax import lax
from jax.experimental import pallas as pl
from jax.experimental.pallas import tpu as pltpu
from jax.sharding import PartitionSpec as P

D = 0.8 / 6.0
C1 = 2.0 * D - 6.0 * D * D
C2 = D * D
C0 = 1.0 - 6.0 * D
NX, NY = 8, 16
LANES = 128
AXES = ("leaf", "sub")
f32 = jnp.float32


def lanes(rows):
    return lax.broadcasted_iota(jnp.int32, (rows, LANES), 1)


def rows_of(rows):
    return lax.broadcasted_iota(jnp.int32, (rows, LANES), 0)


def along_z(cols):
    lane = lanes(cols[0].shape[0])
    first, last = lane == 0, lane == LANES - 1
    right = [pltpu.roll(c, 1, 1) for c in cols]
    left = [pltpu.roll(c, LANES - 1, 1) for c in cols]
    n = len(cols)
    before = [jnp.where(first, right[k - 1] if k else 0.0, right[k]) for k in range(n)]
    after = [jnp.where(last, left[k + 1] if k < n - 1 else 0.0, left[k]) for k in range(n)]
    return before, after


def around(ref, x, whole=False):
    n, rows = ref.shape[1], ref.shape[2]
    cols = [ref[x, k] for k in range(n)]
    before, after = along_z(cols)
    out = []
    for k, c in enumerate(cols):
        up, down = pltpu.roll(c, rows - 1, 0), pltpu.roll(c, 1, 0)
        if whole:
            row = rows_of(rows)
            up, down = jnp.where(row == rows - 1, 0.0, up), jnp.where(row == 0, 0.0, down)
        out.append((ref[x + 1, k] + ref[x - 1, k]) + (up + down) + (before[k] + after[k]))
    return cols, out


def pairs_z(even, odd):
    lane = lanes(even.shape[0])
    take = (lane * 2) % LANES
    got = [
        jnp.take_along_axis(c + pltpu.roll(c, LANES - 1, 1), take, axis=1, mode="promise_in_bounds") for c in (even, odd)
    ]
    return jnp.where(lane < LANES // 2, got[0], got[1])


def twice_z(col):
    lane = lanes(col.shape[0])
    return [jnp.take_along_axis(col, lane // 2 + h * (LANES // 2), axis=1, mode="promise_in_bounds") for h in (0, 1)]


def restricted(tmp, rows):
    sums = [tmp[k, pl.ds(0, rows, 2), :] + tmp[k, pl.ds(1, rows, 2), :] for k in range(tmp.shape[0])]
    return [0.5 * pairs_z(sums[2 * m], sums[2 * m + 1]) for m in range(tmp.shape[0] // 2)]


def prolonged(tmp, cols, rows, at=0):
    for m, c in enumerate(cols):
        for h, e in enumerate(twice_z(c)):
            tmp[2 * m + h, pl.ds(at, rows, 2), :] = e
            tmp[2 * m + h, pl.ds(at + 1, rows, 2), :] = e


def inside(pos, count):
    return jnp.logical_and(pos >= 0, pos < count)


def row_mask(rows, start, count):
    pos = rows_of(rows) + start
    return jnp.where(inside(pos, count), 1.0, 0.0).astype(f32)


def plane_mask(mask, x, count):
    return mask * jnp.where(inside(x, count), 1.0, 0.0).astype(f32)


def each(lo, hi, body, together=1):
    steps = (hi - lo) // together

    def step(s, carry):
        for t in range(together):
            body(lo + s * together + t)
        return carry

    lax.fori_loop(0, steps, step, 0)
    for x in range(lo + steps * together, hi):
        body(x)


def taps(cols):
    lane = lanes(cols[0].shape[0])
    before, after = along_z(cols)
    n = len(cols)
    three = [before[k] + cols[k] + after[k] for k in range(n)]
    right = [pltpu.roll(c, 2, 1) for c in three]
    left = [pltpu.roll(c, LANES - 2, 1) for c in three]
    out = []
    for k in range(n):
        lo = right[k - 1] if k else jnp.where(lane == 1, before[0], 0.0)
        hi = left[k + 1] if k < n - 1 else jnp.where(lane == LANES - 2, after[n - 1], 0.0)
        out.append(cols[k] + jnp.where(lane < 2, lo, right[k]) + jnp.where(lane >= LANES - 2, hi, left[k]))
    return out, before, after


def split(value):
    return [value[:, k * LANES : (k + 1) * LANES] for k in range(value.shape[1] // LANES)]


def place(leaves, subs):
    i, j = lax.axis_index("leaf"), lax.axis_index("sub")
    odd_i, odd_j = i % 2 == 1, j % 2 == 1
    far_i = jnp.where(odd_i, i < leaves - 1, i > 0)
    far_j = jnp.where(odd_j, j < subs - 1, j > 0)
    return i, j, odd_i, odd_j, far_i, far_j


def source(dims, vf, mask, ra, rb, rs1, rs2, src, out_a, out_b, H, G):
    leaves, subs = dims
    i, j, odd_i, odd_j, far_i, far_j = place(leaves, subs)
    nz = vf.shape[2] // LANES

    def level0(x):
        h, before, after = taps(split(vf[x]))
        m = mask[x].astype(f32)
        for k in range(nz):
            H[x + 1, k] = h[k]
            G[x, k] = (after[k] - before[k]) * (0.5 * m[:, k * LANES : (k + 1) * LANES])

    each(0, NX, level0, 2)
    far_x = jnp.where(far_i, 1.0, 0.0).astype(f32)
    far_y = jnp.where(far_j, 1.0, 0.0).astype(f32)
    ha, _, _ = taps(split(ra[0]))
    hb, _, _ = taps(split(rb[0]))
    hs1, _, _ = taps(split(rs1[...]))
    hs2, _, _ = taps(split(rs2[...]))
    for k in range(nz):
        b = hb[k] * far_x
        H[0, k] = jnp.where(odd_i, ha[k], b)
        H[NX + 1, k] = jnp.where(odd_i, b, ha[k])
    row = rows_of(16)
    low = [jnp.where(odd_j, hs1[k], hs2[k] * far_y) for k in range(nz)]
    high = [jnp.where(odd_j, hs2[k] * far_y, hs1[k]) for k in range(nz)]

    for x in range(NX):
        for k in range(nz):
            h = H[x + 1, k]
            up = jnp.where(row == 15, high[k][x : x + 1, :], pltpu.roll(h, 15, 0))
            down = jnp.where(row == 0, low[k][x : x + 1, :], pltpu.roll(h, 1, 0))
            ahead, behind = H[x + 2, k], H[x, k]
            sx, sy = 0.5 * (ahead - behind), 0.5 * (up - down)
            bend = ahead - 2.0 * h + behind + (up - 2.0 * h + down)
            inv = lax.rsqrt(1.0 + sx * sx + sy * sy)
            src[x, :, k * LANES : (k + 1) * LANES] = G[x, k] * (bend * (inv * inv * inv))
    at = jnp.where(odd_i, 0, 4)
    out_a[...] = src[pl.ds(at, 4)]
    out_b[...] = src[pl.ds(4 - at, 4)]


def descent(dims, src, f1_out, c1_out, c2_out, m2a, m2b, own2, F1c, F0, U0, T0, F1, U1, T1):
    leaves, subs = dims
    i, j, odd_i, odd_j, far_i, far_j = place(leaves, subs)
    nz = src.shape[2] // LANES
    zero = jnp.zeros((16, LANES), f32)
    zero24 = jnp.zeros((24, LANES), f32)
    for x in range(16):
        for k in range(nz):
            if 4 <= x < 12:
                F0[x, k, 0:4, :] = zero24[0:4]
                F0[x, k, 4:20, :] = src[x - 4, :, k * LANES : (k + 1) * LANES]
                F0[x, k, 20:24, :] = zero24[0:4]
            else:
                F0[x, k] = zero24

    count_x, count_y = leaves * NX, subs * NY
    my0 = row_mask(24, j * NY - 4, count_y)
    for x in (1, 2, 13, 14):
        for k in range(nz):
            U0[x, k] = zero24

    def smooth0(x):
        m = plane_mask(my0, i * NX + x - 4, count_x)
        f, around_f = around(F0, x)
        for k in range(nz):
            U0[x, k] = (C1 * f[k] + C2 * around_f[k]) * m

    each(3, 13, smooth0, 2)

    for x in range(0, 14):
        if x < 4 or x >= 10:
            for k in range(nz // 2):
                F1[x, k] = zero

    def restrict0(c):
        total = [zero24] * nz
        for p in (0, 1):
            x = 2 * c + p
            m = plane_mask(my0, i * NX + x - 4, count_x)
            u, around_u = around(U0, x)
            total = [total[k] + (F0[x, k] - 6.0 * u[k] + around_u[k]) * m for k in range(nz)]
        for k in range(nz):
            T0[c, k] = total[k]
        for k, v in enumerate(restricted(T0.at[c], 12)):
            F1[c + 3, k, 0:2, :] = zero[0:2]
            F1[c + 3, k, 2:14, :] = v
            F1[c + 3, k, 14:16, :] = zero[0:2]

    each(1, 7, restrict0)

    n1 = nz // 2
    my1 = row_mask(16, j * (NY // 2) - 4, count_y // 2)
    for x in (0, 1, 2, 11, 12, 13):
        for k in range(n1):
            U1[x, k] = zero

    def smooth1(x):
        m = plane_mask(my1, i * (NX // 2) + x - 5, count_x // 2)
        f, around_f = around(F1, x)
        for k in range(n1):
            U1[x, k] = (C1 * f[k] + C2 * around_f[k]) * m

    each(3, 11, smooth1, 4)

    def restrict1(c):
        total = [zero] * n1
        for p in (0, 1):
            x = 2 * c + 1 + p
            m = plane_mask(my1, i * (NX // 2) + x - 5, count_x // 2)
            u, around_u = around(U1, x)
            total = [total[k] + (F1[x, k] - 6.0 * u[k] + around_u[k]) * m for k in range(n1)]
        for k in range(n1):
            T1[c, k] = total[k]
        for k, v in enumerate(restricted(T1.at[c], 8)):
            F1c[c, :, k * LANES : (k + 1) * LANES] = v

    each(0, 6, restrict1, 3)

    at = jnp.where(odd_i, 0, 4)
    m2a[...] = F1c[pl.ds(at, 2)]
    m2b[...] = F1c[pl.ds(4 - at, 2)]
    own2[...] = F1c[2:4]
    for p in range(3):
        for k in range(n1):
            for h in (0, 1):
                f1_out[p, :, (h * n1 + k) * LANES : (h * n1 + k + 1) * LANES] = F1[4 + p + 3 * h, k]
    odd_c = (i // 2) % 2 == 1
    first = jnp.where(odd_c, 4, 8)
    for k in range(n1):
        for h in (0, 1):
            s = slice((h * n1 + k) * LANES, (h * n1 + k + 1) * LANES)
            c1_out[0, :, s] = F1[first + h, k]
            c2_out[0, :, s] = F1[12 - first + h, k]


def sum2(dims, own2, ra, rb, out):
    far = place(*dims)[4]
    v = own2[...] + ra[...] + jnp.where(far, rb[...], 0.0)
    for k in range(out.shape[0]):
        out[k] = v


def chip2(dims, got, f2, edge, out, F2, U2, T2):
    leaves, subs = dims
    i = lax.axis_index("leaf")
    odd_i, c = i % 2 == 1, i // 2
    n2 = f2.shape[2] // LANES
    row = rows_of(8)
    zero = jnp.zeros((16, LANES), f32)
    for x in (0, 1, 2, 7, 8, 9):
        for k in range(n2):
            F2[x, k] = zero
    for x in (0, 1, 8, 9):
        for k in range(n2):
            U2[x, k] = zero
    for x in range(4):
        for k in range(n2):
            s = slice(k * LANES, (k + 1) * LANES)
            t = [got[4 * (x // 2) + j, x % 2, :, s] for j in range(4)]
            one, two = pltpu.roll(t[1], 2, 0), pltpu.roll(t[2], 6, 0)
            lo = jnp.where(row < 6, pltpu.roll(t[0], 6, 0), two) + jnp.where(row >= 2, one, 0.0)
            hi = jnp.where(row >= 2, pltpu.roll(t[3], 2, 0), one) + jnp.where(row < 6, two, 0.0)
            f2[x, 0:8, s] = lo
            f2[x, 8:16, s] = hi
            F2[x + 3, k, 0:8, :] = lo
            F2[x + 3, k, 8:16, :] = hi
    edge[0] = f2[jnp.where(odd_i, 3, 0)]
    m2 = jnp.ones((16, LANES), f32)
    for x in range(2, 8):
        m = plane_mask(m2, 4 * c + x - 3, 2 * leaves)
        f, around_f = around(F2, x, True)
        for k in range(n2):
            U2[x, k] = (C1 * f[k] + C2 * around_f[k]) * m
    for q in range(4):
        total = [zero] * n2
        for x in (2 * q + 1, 2 * q + 2):
            m = plane_mask(m2, 4 * c + x - 3, 2 * leaves)
            u, around_u = around(U2, x, True)
            total = [total[k] + (F2[x, k] - 6.0 * u[k] + around_u[k]) * m for k in range(n2)]
        for k in range(n2):
            T2[q, k] = total[k]
    for q in range(4):
        for k, v in enumerate(restricted(T2.at[q], 8)):
            for t in range(out.shape[0]):
                out[t, q, :, k * LANES : (k + 1) * LANES] = v


def rows_out(dims, src, f1, ra, rb, r1a, r1b, rc1, rc2, f1x, s1, s2):
    leaves, subs = dims
    i, j, odd_i, odd_j, far_i, far_j = place(leaves, subs)
    odd_c = (i // 2) % 2 == 1
    chips = leaves // 2
    c = i // 2
    far_c = jnp.where(odd_c, c < chips - 1, c > 0)
    n = src.shape[2] // 2

    def halves(ref, p):
        return ref[p % 3, :, (p // 3) * n : (p // 3 + 1) * n]

    a = [halves(r1a, p) for p in range(6)]
    b = [jnp.where(far_i, halves(r1b, p), 0.0) for p in range(6)]
    before = [jnp.where(odd_i, a[p], b[p]) for p in range(6)]
    after = [jnp.where(odd_i, b[p], a[p]) for p in range(6)]
    d1 = [rc1[0, :, h * n : (h + 1) * n] for h in (0, 1)]
    d2 = [jnp.where(far_c, rc2[0, :, h * n : (h + 1) * n], 0.0) for h in (0, 1)]
    before2 = [jnp.where(odd_c, d1[h], d2[h]) for h in (0, 1)]
    after2 = [jnp.where(odd_c, d2[h], d1[h]) for h in (0, 1)]
    own = [halves(f1, p) for p in range(6)]
    planes = {}

    def add(x, v):
        planes[x] = planes[x] + v if x in planes else v

    for p in range(6):
        add(p - 1, own[p])
        add(p - 5, before[p])
        add(p + 3, after[p])
    for h in (0, 1):
        add(-5 + h, before2[h])
        add(7 + h, after2[h])
    for x in range(14):
        f1x[x] = planes[x - 5]

    def fine(x):
        if 4 <= x < 12:
            return src[x - 4]
        if x < 4:
            return jnp.where(odd_i, ra[x], jnp.where(far_i, rb[x], 0.0))
        return jnp.where(odd_i, jnp.where(far_i, rb[x - 12], 0.0), ra[x - 12])

    for x in range(8):
        u, v = fine(x), fine(x + 8)
        for out, up in ((s1, odd_j == False), (s2, odd_j)):
            out[x, 0:4, :] = jnp.where(up, u[12:16], u[0:4])
            out[x, 4:8, :] = jnp.where(up, v[12:16], v[0:4])
    for x in range(14):
        v = planes[x - 5]
        s = slice((x // 7) * n, (x // 7 + 1) * n)
        last, first = v[5:13], v[3:11]
        s1[8 + x % 7, :, s] = jnp.where(odd_j, first, last)
        s2[8 + x % 7, :, s] = jnp.where(odd_j, last, first)


def coarsest(dims, got, out, G3, U3, V3):
    leaves = dims[0]
    chips, n3 = got.shape[0], got.shape[3] // LANES
    zero = jnp.zeros((8, LANES), f32)
    for k in range(n3):
        s = slice(k * LANES, (k + 1) * LANES)
        for x in (0, 1, leaves + 2, leaves + 3):
            U3[x, k] = zero
            V3[x, k] = zero
        for c in range(chips):
            a, b = got[c, 1, :, s], got[c, 2, :, s]
            if c > 0:
                a = a + got[c - 1, 3, :, s]
            if c < chips - 1:
                b = b + got[c + 1, 0, :, s]
            G3[2 * c + 2, k], G3[2 * c + 3, k] = a, b
            U3[2 * c + 2, k], U3[2 * c + 3, k] = D * a, D * b

    def sweep3(old, new):
        def body(x):
            u, around_u = around(old, x, True)
            for k in range(n3):
                new[x, k] = C0 * u[k] + D * (G3[x, k] + around_u[k])

        each(2, leaves + 2, body, 16)

    for _ in range(3):
        sweep3(U3, V3)
        sweep3(V3, U3)
    sweep3(U3, V3)
    i = lax.axis_index("leaf")
    for x in range(5):
        for k in range(n3):
            out[x, :, k * LANES : (k + 1) * LANES] = V3[i + x, k]


def ascent(dims, u3, f2, r2c1, r2c2, r2e, src, ra, rb, f1x, rs1, rs2, press, resid, F2, T2, W2, X2, T1, F1, V1, X1, T0, F0, V0, X0):
    leaves, subs = dims
    i, j, odd_i, odd_j, far_i, far_j = place(leaves, subs)
    count_x, count_y = leaves * NX, subs * NY
    nz = src.shape[2] // LANES
    n1, n2, n3 = nz // 2, nz // 4, nz // 8
    zero = jnp.zeros((24, LANES), f32)

    c, chips = i // 2, leaves // 2
    odd_c = c % 2 == 1
    far_c = jnp.where(jnp.where(odd_c, c < chips - 1, c > 0), 1.0, 0.0).astype(f32)
    far_e = jnp.where(jnp.where(odd_i, c < chips - 2, c > 1), 1.0, 0.0).astype(f32)
    base = jnp.where(odd_i, 2, 0)
    for k in range(n2):
        s = slice(k * LANES, (k + 1) * LANES)
        e = r2e[0, :, s] * far_e
        F2[0, k] = e
        F2[13, k] = e
        for x in range(4):
            a, b = r2c1[x, :, s], r2c2[x, :, s] * far_c
            F2[x + 1, k] = jnp.where(odd_c, a, b)
            F2[x + 5, k] = f2[x, :, s]
            F2[x + 9, k] = jnp.where(odd_c, b, a)
    m2 = jnp.ones((16, LANES), f32)
    for x in range(5):
        prolonged(T2.at[x], [u3[x, :, k * LANES : (k + 1) * LANES] for k in range(n3)], 8)
    for w in range(10):
        m = plane_mask(m2, 2 * i + w - 4, 2 * leaves)
        f, around_f = around(F2, base + w + 1, True)
        for k in range(n2):
            W2[w, k] = (C1 * f[k] + C2 * around_f[k] + T2[w // 2, k]) * m

    def sweep2(old, new, lo, hi):
        for w in range(lo, hi):
            m = plane_mask(m2, 2 * i + w - 4, 2 * leaves)
            u, around_u = around(old, w, True)
            for k in range(n2):
                new[w, k] = (C0 * u[k] + D * (F2[base + w + 1, k] + around_u[k])) * m

    sweep2(W2, X2, 1, 9)
    sweep2(X2, W2, 2, 8)

    for c in range(6):
        for k in range(n1):
            T1[c, k] = zero
    low_j = jnp.where(j > 0, 1.0, 0.0).astype(f32)
    high_j = jnp.where(j < subs - 1, 1.0, 0.0).astype(f32)

    def fill1(x):
        part, at = x // 7, 8 + x % 7
        for k in range(n1):
            s = slice(k * LANES, (k + 1) * LANES)
            F1[x, k] = zero
            F1[x, k, 4:20, :] = f1x[x, :, s]
            s = slice((part * n1 + k) * LANES, (part * n1 + k + 1) * LANES)
            lo = jnp.where(odd_j, rs1[at, :, s], rs2[at, :, s]) * low_j
            hi = jnp.where(odd_j, rs2[at, :, s], rs1[at, :, s]) * high_j
            F1[x, k, 1:9, :] = F1[x, k, 1:9, :] + lo
            F1[x, k, 15:23, :] = F1[x, k, 15:23, :] + hi

    for x in range(14):
        fill1(x)
    my1 = row_mask(24, j * (NY // 2) - 8, count_y // 2)

    for c in range(6):
        cols = [pltpu.roll(W2[c + 2, k], (18 - 4 * j) % 16, 0)[0:8] for k in range(n2)]
        prolonged(T1.at[c], cols, 8, 4)
    for c in range(6):
        for p in (0, 1):
            x = 2 * c + p + 1
            m = plane_mask(my1, i * (NX // 2) + x - 5, count_x // 2)
            f, around_f = around(F1, x)
            for k in range(n1):
                V1[x, k] = (C1 * f[k] + C2 * around_f[k] + T1[c, k]) * m

    def sweep1(old, new, lo, hi):
        def body(x):
            m = plane_mask(my1, i * (NX // 2) + x - 5, count_x // 2)
            u, around_u = around(old, x)
            for k in range(n1):
                new[x, k] = (C0 * u[k] + D * (F1[x, k] + around_u[k])) * m

        each(lo, hi, body, 2)

    sweep1(V1, X1, 2, 12)
    sweep1(X1, V1, 3, 11)

    far_x = jnp.where(far_i, 1.0, 0.0).astype(f32)

    def fill0(x):
        if 4 <= x < 12:
            v = src[x - 4]
        elif x < 4:
            v = jnp.where(odd_i, ra[x], rb[x] * far_x)
        else:
            v = jnp.where(odd_i, rb[x - 12] * far_x, ra[x - 12])
        a, b = rs1[x % 8], rs2[x % 8]
        h = 4 * (x // 8)
        lo = jnp.where(odd_j, a[h : h + 4], b[h : h + 4]) * low_j
        hi = jnp.where(odd_j, b[h : h + 4], a[h : h + 4]) * high_j
        for k in range(nz):
            s = slice(k * LANES, (k + 1) * LANES)
            F0[x, k, 0:4, :] = lo[:, s]
            F0[x, k, 4:20, :] = v[:, s]
            F0[x, k, 20:24, :] = hi[:, s]

    for x in range(16):
        fill0(x)
    my0 = row_mask(24, j * NY - 4, count_y)

    def start0(c):
        prolonged(T0.at[c], [V1[c + 3, k, 6:18, :] for k in range(n1)], 12)

    each(0, 8, start0, 2)

    def smooth0(x):
        m = plane_mask(my0, i * NX + x - 4, count_x)
        f, around_f = around(F0, x)
        for k in range(nz):
            V0[x, k] = (C1 * f[k] + C2 * around_f[k] + T0[x // 2, k]) * m

    each(1, 15, smooth0, 2)

    def sweep0(old, new, lo, hi):
        def body(x):
            m = plane_mask(my0, i * NX + x - 4, count_x)
            u, around_u = around(old, x)
            for k in range(nz):
                new[x, k] = (C0 * u[k] + D * (F0[x, k] + around_u[k])) * m

        each(lo, hi, body, 2)

    sweep0(V0, X0, 2, 14)
    sweep0(X0, V0, 3, 13)

    def finish(x):
        u, around_u = around(V0, x + 4)
        for k in range(nz):
            s = slice(k * LANES, (k + 1) * LANES)
            press[x, :, s] = u[k][4:20]
            resid[x, :, s] = (F0[x + 4, k] - 6.0 * u[k] + around_u[k])[4:20]

    each(0, NX, finish, 2)


def call(kernel, outs, scratch, *args):
    return pl.pallas_call(
        kernel,
        out_shape=[jax.ShapeDtypeStruct(s, f32) for s in outs],
        scratch_shapes=[pltpu.VMEM(s, f32) for s in scratch],
        compiler_params=pltpu.CompilerParams(vmem_limit_bytes=48 * 1024 * 1024),
    )(*args)


def swaps(leaves, subs):
    def table(partner):
        return [(i * subs + j, (lambda t: t[0] * subs + t[1])(partner(i, j))) for i in range(leaves) for j in range(subs)]

    def odd(n):
        return ((n + 1) ^ 1) - 1

    def inner(n, count):
        return 0 <= n < count

    a = table(lambda i, j: (i ^ 1, j))
    b = table(lambda i, j: (odd(i), j) if inner(odd(i), leaves) else (i, j ^ 1))
    s1 = table(lambda i, j: (i, j ^ 1))
    s2 = table(lambda i, j: (i, odd(j)) if inner(odd(j), subs) else (i ^ 1, j))
    c1 = table(lambda i, j: (i ^ 2, j))
    c2 = table(lambda i, j: (2 * odd(i // 2) + i % 2, j) if inner(odd(i // 2), leaves // 2) else (i, j ^ 1))
    def two_on(i):
        t = 2 * (i // 2 + (2 if i % 2 else -2)) + 1 - i % 2
        return t if inner(t, leaves) else None

    e = table(lambda i, j: (two_on(i), j) if two_on(i) is not None else (i, j ^ 1))
    return a, b, s1, s2, c1, c2, e


def shards(dims, volume_fraction, interface_mask):
    leaves, subs = dims
    depth = volume_fraction.shape[2]
    nz = depth // LANES
    pa, pb, ps1, ps2, pc1, pc2, pe = swaps(leaves, subs)
    move = lambda v, table: lax.ppermute(v, AXES, table)
    i, j = lax.axis_index("leaf"), lax.axis_index("sub")
    odd_i, odd_j = i % 2, j % 2

    vf = volume_fraction
    at_x, at_y = (1 - odd_i) * (NX - 1), (1 - odd_j) * (NY - 1)
    plane = lambda x: lax.dynamic_slice_in_dim(vf, x, 1, 0)
    rows = lambda y: lax.dynamic_slice_in_dim(vf, y, 1, 1).reshape(NX, depth)
    ha, hb = move(plane(at_x), pa), move(plane(NX - 1 - at_x), pb)
    hs1, hs2 = move(rows(at_y), ps1), move(rows(NY - 1 - at_y), ps2)

    n1, n2, n3 = nz // 2, nz // 4, nz // 8
    src, out_a, out_b = call(
        functools.partial(source, dims),
        [(NX, NY, depth), (4, NY, depth), (4, NY, depth)],
        [(NX + 2, nz, 16, LANES), (NX, nz, 16, LANES)],
        vf,
        interface_mask,
        ha,
        hb,
        hs1,
        hs2,
    )
    ra, rb = move(out_a, pa), move(out_b, pb)
    f1, m1, m2, m2a, m2b, own2 = call(
        functools.partial(descent, dims),
        [(3, 16, depth), (1, 16, depth), (1, 16, depth)] + [(2, 8, depth // 4)] * 3,
        [
            (6, 8, depth // 4),
            (16, nz, 24, LANES),
            (16, nz, 24, LANES),
            (8, nz, 24, LANES),
            (14, n1, 16, LANES),
            (14, n1, 16, LANES),
            (6, n1, 16, LANES),
        ],
        src,
    )
    r2a, r2b = move(m2a, pa), move(m2b, pb)
    (out,) = call(functools.partial(sum2, dims), [(2 * subs, 2, 8, depth // 4)], [], own2, r2a, r2b)
    out, g1, m1, m2 = lax.optimization_barrier((out, f1, m1, m2))
    r1a, r1b = move(g1, pa), move(g1, pb)
    rc1, rc2 = move(m1, pc1), move(m2, pc2)
    group = [list(range(k, k + 2 * subs)) for k in range(0, leaves * subs, 2 * subs)]
    got = lax.all_to_all(out, AXES, 0, 0, axis_index_groups=group)
    got, r1a, r1b, rc1, rc2 = lax.optimization_barrier((got, r1a, r1b, rc1, rc2))
    f1x, s1, s2 = call(
        functools.partial(rows_out, dims),
        [(14, 16, depth // 2), (15, 8, depth), (15, 8, depth)],
        [],
        src,
        f1,
        ra,
        rb,
        r1a,
        r1b,
        rc1,
        rc2,
    )
    chips = leaves // 2
    f2, edge, out = call(
        functools.partial(chip2, dims),
        [(4, 16, depth // 4), (1, 16, depth // 4), (chips, 4, 8, depth // 8)],
        [(10, n2, 16, LANES), (10, n2, 16, LANES), (4, n2, 16, LANES)],
        got,
    )
    out, s1, s2, g2, edge = lax.optimization_barrier((out, s1, s2, f2, edge))
    rs1, rs2 = move(s1, ps1), move(s2, ps2)
    r2c1, r2c2, r2e = move(g2, pc1), move(g2, pc2), move(edge, pe)
    group = [[(2 * c + k) * subs + s for c in range(chips)] for k in (0, 1) for s in range(subs)]
    got = lax.all_to_all(out, AXES, 0, 0, axis_index_groups=group)
    (u3,) = call(
        functools.partial(coarsest, dims), [(5, 8, depth // 8)], [(leaves + 4, n3, 8, LANES)] * 3, got
    )
    return call(
        functools.partial(ascent, dims),
        [(NX, NY, depth), (NX, NY, depth)],
        [
            (14, n2, 16, LANES),
            (5, n2, 16, LANES),
            (10, n2, 16, LANES),
            (10, n2, 16, LANES),
            (6, n1, 24, LANES),
            (14, n1, 24, LANES),
            (14, n1, 24, LANES),
            (14, n1, 24, LANES),
            (8, nz, 24, LANES),
            (16, nz, 24, LANES),
            (16, nz, 24, LANES),
            (16, nz, 24, LANES),
        ],
        u3,
        f2,
        r2c1,
        r2c2,
        r2e,
        src,
        ra,
        rb,
        f1x,
        rs1,
        rs2,
    )


def solution(mesh):
    spec = P("leaf", "sub", None)
    dims = (mesh.shape["leaf"], mesh.shape["sub"])
    body = functools.partial(shards, dims)
    return jax.shard_map(body, mesh=mesh, in_specs=(spec, spec), out_specs=(spec, spec), check_vma=False)
```

```python
import functools

import jax
import jax.numpy as jnp
from jax import lax
from jax.experimental import pallas as pl
from jax.experimental.pallas import tpu as pltpu
from jax.sharding import PartitionSpec as P

D = 0.8 / 6.0
C1 = 2.0 * D - 6.0 * D * D
C2 = D * D
C0 = 1.0 - 6.0 * D
NX, NY = 8, 16
LANES = 128
AXES = ("leaf", "sub")
f32 = jnp.float32


def lanes(rows):
    return lax.broadcasted_iota(jnp.int32, (rows, LANES), 1)


def rows_of(rows):
    return lax.broadcasted_iota(jnp.int32, (rows, LANES), 0)


def along_z(cols):
    lane = lanes(cols[0].shape[0])
    first, last = lane == 0, lane == LANES - 1
    right = [pltpu.roll(c, 1, 1) for c in cols]
    left = [pltpu.roll(c, LANES - 1, 1) for c in cols]
    n = len(cols)
    before = [jnp.where(first, right[k - 1] if k else 0.0, right[k]) for k in range(n)]
    after = [jnp.where(last, left[k + 1] if k < n - 1 else 0.0, left[k]) for k in range(n)]
    return before, after


def around(ref, x, whole=False):
    n, rows = ref.shape[1], ref.shape[2]
    cols = [ref[x, k] for k in range(n)]
    before, after = along_z(cols)
    out = []
    for k, c in enumerate(cols):
        up, down = pltpu.roll(c, rows - 1, 0), pltpu.roll(c, 1, 0)
        if whole:
            row = rows_of(rows)
            up, down = jnp.where(row == rows - 1, 0.0, up), jnp.where(row == 0, 0.0, down)
        out.append((ref[x + 1, k] + ref[x - 1, k]) + (up + down) + (before[k] + after[k]))
    return cols, out


def pairs_z(even, odd):
    lane = lanes(even.shape[0])
    take = (lane * 2) % LANES
    got = [
        jnp.take_along_axis(c + pltpu.roll(c, LANES - 1, 1), take, axis=1, mode="promise_in_bounds") for c in (even, odd)
    ]
    return jnp.where(lane < LANES // 2, got[0], got[1])


def twice_z(col):
    lane = lanes(col.shape[0])
    return [jnp.take_along_axis(col, lane // 2 + h * (LANES // 2), axis=1, mode="promise_in_bounds") for h in (0, 1)]


def restricted(tmp, rows):
    sums = [tmp[k, pl.ds(0, rows, 2), :] + tmp[k, pl.ds(1, rows, 2), :] for k in range(tmp.shape[0])]
    return [0.5 * pairs_z(sums[2 * m], sums[2 * m + 1]) for m in range(tmp.shape[0] // 2)]


def prolonged(tmp, cols, rows, at=0):
    for m, c in enumerate(cols):
        for h, e in enumerate(twice_z(c)):
            tmp[2 * m + h, pl.ds(at, rows, 2), :] = e
            tmp[2 * m + h, pl.ds(at + 1, rows, 2), :] = e


def inside(pos, count):
    return jnp.logical_and(pos >= 0, pos < count)


def row_mask(rows, start, count):
    pos = rows_of(rows) + start
    return jnp.where(inside(pos, count), 1.0, 0.0).astype(f32)


def plane_mask(mask, x, count):
    return mask * jnp.where(inside(x, count), 1.0, 0.0).astype(f32)


def each(lo, hi, body, together=1):
    steps = (hi - lo) // together

    def step(s, carry):
        for t in range(together):
            body(lo + s * together + t)
        return carry

    lax.fori_loop(0, steps, step, 0)
    for x in range(lo + steps * together, hi):
        body(x)


def taps(cols):
    lane = lanes(cols[0].shape[0])
    before, after = along_z(cols)
    n = len(cols)
    three = [before[k] + cols[k] + after[k] for k in range(n)]
    right = [pltpu.roll(c, 2, 1) for c in three]
    left = [pltpu.roll(c, LANES - 2, 1) for c in three]
    out = []
    for k in range(n):
        lo = right[k - 1] if k else jnp.where(lane == 1, before[0], 0.0)
        hi = left[k + 1] if k < n - 1 else jnp.where(lane == LANES - 2, after[n - 1], 0.0)
        out.append(cols[k] + jnp.where(lane < 2, lo, right[k]) + jnp.where(lane >= LANES - 2, hi, left[k]))
    return out, before, after


def split(value):
    return [value[:, k * LANES : (k + 1) * LANES] for k in range(value.shape[1] // LANES)]


def place(leaves, subs):
    i, j = lax.axis_index("leaf"), lax.axis_index("sub")
    odd_i, odd_j = i % 2 == 1, j % 2 == 1
    far_i = jnp.where(odd_i, i < leaves - 1, i > 0)
    far_j = jnp.where(odd_j, j < subs - 1, j > 0)
    return i, j, odd_i, odd_j, far_i, far_j


def edges(dims, vf, to_a, to_b, to_1, to_2):
    _, _, odd_i, odd_j, _, _ = place(*dims)
    to_a[0] = vf[jnp.where(odd_i, 0, NX - 1)]
    to_b[0] = vf[jnp.where(odd_i, NX - 1, 0)]
    for x in range(NX):
        first, last = vf[x, 0:1, :], vf[x, NY - 1 : NY, :]
        to_1[x : x + 1, :] = jnp.where(odd_j, first, last)
        to_2[x : x + 1, :] = jnp.where(odd_j, last, first)


def columns(vf, mask, H, G):
    nz = vf.shape[2] // LANES

    def level0(x):
        h, before, after = taps(split(vf[x]))
        m = mask[x].astype(f32)
        for k in range(nz):
            H[x, k] = h[k]
            G[x, k] = (after[k] - before[k]) * (0.5 * m[:, k * LANES : (k + 1) * LANES])

    each(0, NX, level0, 2)


def source(dims, H, G, ra, rb, rs1, rs2, src):
    _, _, odd_i, odd_j, far_i, far_j = place(*dims)
    nz = H.shape[1]
    far_x = jnp.where(far_i, 1.0, 0.0).astype(f32)
    far_y = jnp.where(far_j, 1.0, 0.0).astype(f32)
    ha, _, _ = taps(split(ra[0]))
    hb, _, _ = taps(split(rb[0]))
    hs1, _, _ = taps(split(rs1[...]))
    hs2, _, _ = taps(split(rs2[...]))
    row = rows_of(NY)
    for k in range(nz):
        b = hb[k] * far_x
        below, above = jnp.where(odd_i, ha[k], b), jnp.where(odd_i, b, ha[k])
        low = jnp.where(odd_j, hs1[k], hs2[k] * far_y)
        high = jnp.where(odd_j, hs2[k] * far_y, hs1[k])
        for x in range(NX):
            h = H[x, k]
            up = jnp.where(row == NY - 1, high[x : x + 1, :], pltpu.roll(h, NY - 1, 0))
            down = jnp.where(row == 0, low[x : x + 1, :], pltpu.roll(h, 1, 0))
            ahead = H[x + 1, k] if x < NX - 1 else above
            behind = H[x - 1, k] if x > 0 else below
            sx, sy = 0.5 * (ahead - behind), 0.5 * (up - down)
            bend = ahead - 2.0 * h + behind + (up - 2.0 * h + down)
            inv = lax.rsqrt(1.0 + sx * sx + sy * sy)
            src[x, :, k * LANES : (k + 1) * LANES] = G[x, k] * (bend * (inv * inv * inv))


def descent(dims, src, big, m2a, m2b, own2, F1c, F0, U0, T0, F1, U1, T1):
    leaves, subs = dims
    i, j, odd_i, odd_j, far_i, far_j = place(leaves, subs)
    nz = src.shape[2] // LANES
    zero = jnp.zeros((16, LANES), f32)
    zero24 = jnp.zeros((24, LANES), f32)
    for x in range(16):
        for k in range(nz):
            if 4 <= x < 12:
                F0[x, k, 0:4, :] = zero24[0:4]
                F0[x, k, 4:20, :] = src[x - 4, :, k * LANES : (k + 1) * LANES]
                F0[x, k, 20:24, :] = zero24[0:4]
            else:
                F0[x, k] = zero24

    count_x, count_y = leaves * NX, subs * NY
    my0 = row_mask(24, j * NY - 4, count_y)
    for x in (1, 2, 13, 14):
        for k in range(nz):
            U0[x, k] = zero24

    def smooth0(x):
        m = plane_mask(my0, i * NX + x - 4, count_x)
        f, around_f = around(F0, x)
        for k in range(nz):
            U0[x, k] = (C1 * f[k] + C2 * around_f[k]) * m

    each(3, 13, smooth0, 5)

    for x in range(0, 14):
        if x < 4 or x >= 10:
            for k in range(nz // 2):
                F1[x, k] = zero

    def restrict0(c):
        total = [zero24] * nz
        for p in (0, 1):
            x = 2 * c + p
            m = plane_mask(my0, i * NX + x - 4, count_x)
            u, around_u = around(U0, x)
            total = [total[k] + (F0[x, k] - 6.0 * u[k] + around_u[k]) * m for k in range(nz)]
        for k in range(nz):
            T0[c, k] = total[k]
        for k, v in enumerate(restricted(T0.at[c], 12)):
            F1[c + 3, k, 0:2, :] = zero[0:2]
            F1[c + 3, k, 2:14, :] = v
            F1[c + 3, k, 14:16, :] = zero[0:2]

    each(1, 7, restrict0, 2)

    n1 = nz // 2
    my1 = row_mask(16, j * (NY // 2) - 4, count_y // 2)
    for x in (0, 1, 2, 11, 12, 13):
        for k in range(n1):
            U1[x, k] = zero

    def smooth1(x):
        m = plane_mask(my1, i * (NX // 2) + x - 5, count_x // 2)
        f, around_f = around(F1, x)
        for k in range(n1):
            U1[x, k] = (C1 * f[k] + C2 * around_f[k]) * m

    each(3, 11, smooth1, 4)

    def restrict1(c):
        total = [zero] * n1
        for p in (0, 1):
            x = 2 * c + 1 + p
            m = plane_mask(my1, i * (NX // 2) + x - 5, count_x // 2)
            u, around_u = around(U1, x)
            total = [total[k] + (F1[x, k] - 6.0 * u[k] + around_u[k]) * m for k in range(n1)]
        for k in range(n1):
            T1[c, k] = total[k]
        for k, v in enumerate(restricted(T1.at[c], 8)):
            F1c[c, :, k * LANES : (k + 1) * LANES] = v

    each(0, 6, restrict1, 3)

    at = jnp.where(odd_i, 0, 4)
    m2a[...] = F1c[pl.ds(at, 2)]
    m2b[...] = F1c[pl.ds(4 - at, 2)]
    own2[...] = F1c[2:4]
    big[0:4] = src[pl.ds(at, 4)]
    for p in range(3):
        for k in range(n1):
            for h in (0, 1):
                big[4 + p, :, (h * n1 + k) * LANES : (h * n1 + k + 1) * LANES] = F1[4 + p + 3 * h, k]


def half_planes(ref, p):
    n = ref.shape[2] // 2
    return ref[4 + p % 3, :, (p // 3) * n : (p // 3 + 1) * n]


def middle(dims, own2, r2a, r2b, src, big, ra, out, to_b):
    _, _, odd_i, _, far_i, _ = place(*dims)
    n = src.shape[2] // 2
    v = own2[...] + r2a[...] + jnp.where(far_i, r2b[...], 0.0)
    for k in range(out.shape[0]):
        out[k] = v
    to_b[0:4] = src[pl.ds(jnp.where(odd_i, 4, 0), 4)]
    more = {
        0: jnp.where(odd_i, half_planes(ra, 4), 0.0),
        1: jnp.where(odd_i, half_planes(ra, 5), 0.0),
        4: jnp.where(odd_i, 0.0, half_planes(ra, 0)),
        5: jnp.where(odd_i, 0.0, half_planes(ra, 1)),
    }
    for p in range(6):
        v = half_planes(big, p)
        to_b[4 + p % 3, :, (p // 3) * n : (p // 3 + 1) * n] = v + more[p] if p in more else v


def chip2(dims, got, f2, edge, out, F2, U2, T2):
    leaves, subs = dims
    i = lax.axis_index("leaf")
    odd_i, c = i % 2 == 1, i // 2
    n2 = f2.shape[2] // LANES
    row = rows_of(8)
    zero = jnp.zeros((16, LANES), f32)
    for x in (0, 1, 2, 7, 8, 9):
        for k in range(n2):
            F2[x, k] = zero
    for x in (0, 1, 8, 9):
        for k in range(n2):
            U2[x, k] = zero
    for x in range(4):
        for k in range(n2):
            s = slice(k * LANES, (k + 1) * LANES)
            t = [got[4 * (x // 2) + j, x % 2, :, s] for j in range(4)]
            one, two = pltpu.roll(t[1], 2, 0), pltpu.roll(t[2], 6, 0)
            lo = jnp.where(row < 6, pltpu.roll(t[0], 6, 0), two) + jnp.where(row >= 2, one, 0.0)
            hi = jnp.where(row >= 2, pltpu.roll(t[3], 2, 0), one) + jnp.where(row < 6, two, 0.0)
            f2[x, 0:8, s] = lo
            f2[x, 8:16, s] = hi
            F2[x + 3, k, 0:8, :] = lo
            F2[x + 3, k, 8:16, :] = hi
    edge[0] = f2[jnp.where(odd_i, 3, 0)]
    m2 = jnp.ones((16, LANES), f32)
    for x in range(2, 8):
        m = plane_mask(m2, 4 * c + x - 3, 2 * leaves)
        f, around_f = around(F2, x, True)
        for k in range(n2):
            U2[x, k] = (C1 * f[k] + C2 * around_f[k]) * m
    for q in range(4):
        total = [zero] * n2
        for x in (2 * q + 1, 2 * q + 2):
            m = plane_mask(m2, 4 * c + x - 3, 2 * leaves)
            u, around_u = around(U2, x, True)
            total = [total[k] + (F2[x, k] - 6.0 * u[k] + around_u[k]) * m for k in range(n2)]
        for k in range(n2):
            T2[q, k] = total[k]
    for q in range(4):
        for k, v in enumerate(restricted(T2.at[q], 8)):
            for t in range(out.shape[0]):
                out[t, q, :, k * LANES : (k + 1) * LANES] = v


def rows_out(dims, src, big, ra, rb, far, f1x, s1, s2):
    _, _, odd_i, odd_j, far_i, _ = place(*dims)
    i = lax.axis_index("leaf")
    n = src.shape[2] // 2
    a = [half_planes(ra, p) for p in range(6)]
    b = [jnp.where(far_i, half_planes(rb, p), 0.0) for p in range(6)]
    before = [jnp.where(odd_i, a[p], b[p]) for p in range(6)]
    after = [jnp.where(odd_i, b[p], a[p]) for p in range(6)]
    far_two = jnp.where(odd_i, i > 1, i < dims[0] - 2)
    d = [jnp.where(far_two, far[p % 3, :, (p // 3) * n : (p // 3 + 1) * n], 0.0) for p in (0, 1, 4, 5)]
    before2 = [jnp.where(odd_i, d[2 + h], 0.0) for h in (0, 1)]
    after2 = [jnp.where(odd_i, 0.0, d[h]) for h in (0, 1)]
    own = [half_planes(big, p) for p in range(6)]
    planes = {}

    def add(x, v):
        planes[x] = planes[x] + v if x in planes else v

    for p in range(6):
        add(p - 1, own[p])
        add(p - 5, before[p])
        add(p + 3, after[p])
    for h in (0, 1):
        add(-5 + h, before2[h])
        add(7 + h, after2[h])
    for x in range(14):
        f1x[x] = planes[x - 5]

    def fine(x):
        if 4 <= x < 12:
            return src[x - 4]
        if x < 4:
            return jnp.where(odd_i, ra[x], jnp.where(far_i, rb[x], 0.0))
        return jnp.where(odd_i, jnp.where(far_i, rb[x - 12], 0.0), ra[x - 12])

    for x in range(8):
        u, v = fine(x), fine(x + 8)
        for out, up in ((s1, odd_j == False), (s2, odd_j)):
            out[x, 0:4, :] = jnp.where(up, u[12:16], u[0:4])
            out[x, 4:8, :] = jnp.where(up, v[12:16], v[0:4])
    for x in range(14):
        v = planes[x - 5]
        s = slice((x // 7) * n, (x // 7 + 1) * n)
        last, first = v[5:13], v[3:11]
        s1[8 + x % 7, :, s] = jnp.where(odd_j, first, last)
        s2[8 + x % 7, :, s] = jnp.where(odd_j, last, first)


def coarsest(dims, got, out, G3, U3, V3):
    leaves = dims[0]
    chips, n3 = got.shape[0], got.shape[3] // LANES
    zero = jnp.zeros((8, LANES), f32)
    for k in range(n3):
        s = slice(k * LANES, (k + 1) * LANES)
        for x in (0, 1, leaves + 2, leaves + 3):
            U3[x, k] = zero
            V3[x, k] = zero
        for c in range(chips):
            a, b = got[c, 1, :, s], got[c, 2, :, s]
            if c > 0:
                a = a + got[c - 1, 3, :, s]
            if c < chips - 1:
                b = b + got[c + 1, 0, :, s]
            G3[2 * c + 2, k], G3[2 * c + 3, k] = a, b
            U3[2 * c + 2, k], U3[2 * c + 3, k] = D * a, D * b

    def sweep3(old, new):
        def body(x):
            u, around_u = around(old, x, True)
            for k in range(n3):
                new[x, k] = C0 * u[k] + D * (G3[x, k] + around_u[k])

        each(2, leaves + 2, body, 16)

    for _ in range(3):
        sweep3(U3, V3)
        sweep3(V3, U3)
    sweep3(U3, V3)
    i = lax.axis_index("leaf")
    for x in range(5):
        for k in range(n3):
            out[x, :, k * LANES : (k + 1) * LANES] = V3[i + x, k]


def ready(dims, src, ra, rb, f1x, rs1, rs2, F0, P0, F1, P1):
    leaves, subs = dims
    i, j, odd_i, odd_j, far_i, far_j = place(leaves, subs)
    count_x, count_y = leaves * NX, subs * NY
    nz = src.shape[2] // LANES
    n1 = nz // 2
    zero = jnp.zeros((24, LANES), f32)
    far_x = jnp.where(far_i, 1.0, 0.0).astype(f32)

    low_j = jnp.where(j > 0, 1.0, 0.0).astype(f32)
    high_j = jnp.where(j < subs - 1, 1.0, 0.0).astype(f32)

    def fill1(x):
        part, at = x // 7, 8 + x % 7
        for k in range(n1):
            s = slice(k * LANES, (k + 1) * LANES)
            F1[x, k] = zero
            F1[x, k, 4:20, :] = f1x[x, :, s]
            s = slice((part * n1 + k) * LANES, (part * n1 + k + 1) * LANES)
            lo = jnp.where(odd_j, rs1[at, :, s], rs2[at, :, s]) * low_j
            hi = jnp.where(odd_j, rs2[at, :, s], rs1[at, :, s]) * high_j
            F1[x, k, 1:9, :] = F1[x, k, 1:9, :] + lo
            F1[x, k, 15:23, :] = F1[x, k, 15:23, :] + hi

    for x in range(14):
        fill1(x)
    my1 = row_mask(24, j * (NY // 2) - 8, count_y // 2)

    def smooth1(x):
        m = plane_mask(my1, i * (NX // 2) + x - 5, count_x // 2)
        f, around_f = around(F1, x)
        for k in range(n1):
            P1[x, k] = (C1 * f[k] + C2 * around_f[k]) * m

    each(1, 13, smooth1, 4)

    def fill0(x):
        if 4 <= x < 12:
            v = src[x - 4]
        elif x < 4:
            v = jnp.where(odd_i, ra[x], rb[x] * far_x)
        else:
            v = jnp.where(odd_i, rb[x - 12] * far_x, ra[x - 12])
        a, b = rs1[x % 8], rs2[x % 8]
        h = 4 * (x // 8)
        lo = jnp.where(odd_j, a[h : h + 4], b[h : h + 4]) * low_j
        hi = jnp.where(odd_j, b[h : h + 4], a[h : h + 4]) * high_j
        for k in range(nz):
            s = slice(k * LANES, (k + 1) * LANES)
            F0[x, k, 0:4, :] = lo[:, s]
            F0[x, k, 4:20, :] = v[:, s]
            F0[x, k, 20:24, :] = hi[:, s]

    for x in range(16):
        fill0(x)
    my0 = row_mask(24, j * NY - 4, count_y)

    def smooth0(x):
        m = plane_mask(my0, i * NX + x - 4, count_x)
        f, around_f = around(F0, x)
        for k in range(nz):
            P0[x, k] = (C1 * f[k] + C2 * around_f[k]) * m

    each(1, 15, smooth0, 4)


def ascent(dims, u3, f2, r2c1, r2c2, r2e, F0, P0, F1, P1, press, resid, F2, T2, W2, X2, T1, V1, X1, T0, V0, X0):
    leaves, subs = dims
    i, j, odd_i, odd_j, far_i, far_j = place(leaves, subs)
    count_x, count_y = leaves * NX, subs * NY
    nz = F0.shape[1]
    n1, n2, n3 = nz // 2, nz // 4, nz // 8
    zero = jnp.zeros((24, LANES), f32)

    c, chips = i // 2, leaves // 2
    odd_c = c % 2 == 1
    far_c = jnp.where(jnp.where(odd_c, c < chips - 1, c > 0), 1.0, 0.0).astype(f32)
    far_e = jnp.where(jnp.where(odd_i, c < chips - 2, c > 1), 1.0, 0.0).astype(f32)
    base = jnp.where(odd_i, 2, 0)
    for k in range(n2):
        s = slice(k * LANES, (k + 1) * LANES)
        e = r2e[0, :, s] * far_e
        F2[0, k] = e
        F2[13, k] = e
        for x in range(4):
            a, b = r2c1[x, :, s], r2c2[x, :, s] * far_c
            F2[x + 1, k] = jnp.where(odd_c, a, b)
            F2[x + 5, k] = f2[x, :, s]
            F2[x + 9, k] = jnp.where(odd_c, b, a)
    m2 = jnp.ones((16, LANES), f32)
    for x in range(5):
        prolonged(T2.at[x], [u3[x, :, k * LANES : (k + 1) * LANES] for k in range(n3)], 8)
    for w in range(10):
        m = plane_mask(m2, 2 * i + w - 4, 2 * leaves)
        f, around_f = around(F2, base + w + 1, True)
        for k in range(n2):
            W2[w, k] = (C1 * f[k] + C2 * around_f[k] + T2[w // 2, k]) * m

    def sweep2(old, new, lo, hi):
        for w in range(lo, hi):
            m = plane_mask(m2, 2 * i + w - 4, 2 * leaves)
            u, around_u = around(old, w, True)
            for k in range(n2):
                new[w, k] = (C0 * u[k] + D * (F2[base + w + 1, k] + around_u[k])) * m

    sweep2(W2, X2, 1, 9)
    sweep2(X2, W2, 2, 8)

    for c in range(6):
        for k in range(n1):
            T1[c, k] = zero
    my1 = row_mask(24, j * (NY // 2) - 8, count_y // 2)

    for c in range(6):
        cols = [pltpu.roll(W2[c + 2, k], (18 - 4 * j) % 16, 0)[0:8] for k in range(n2)]
        prolonged(T1.at[c], cols, 8, 4)
    for c in range(6):
        for p in (0, 1):
            x = 2 * c + p + 1
            m = plane_mask(my1, i * (NX // 2) + x - 5, count_x // 2)
            for k in range(n1):
                V1[x, k] = P1[x, k] + T1[c, k] * m

    def sweep1(old, new, lo, hi):
        def body(x):
            m = plane_mask(my1, i * (NX // 2) + x - 5, count_x // 2)
            u, around_u = around(old, x)
            for k in range(n1):
                new[x, k] = (C0 * u[k] + D * (F1[x, k] + around_u[k])) * m

        each(lo, hi, body, 4)

    sweep1(V1, X1, 2, 12)
    sweep1(X1, V1, 3, 11)


    my0 = row_mask(24, j * NY - 4, count_y)

    def start0(c):
        prolonged(T0.at[c], [V1[c + 3, k, 6:18, :] for k in range(n1)], 12)

    each(0, 8, start0, 2)

    def smooth0(x):
        m = plane_mask(my0, i * NX + x - 4, count_x)
        for k in range(nz):
            V0[x, k] = P0[x, k] + T0[x // 2, k] * m

    each(1, 15, smooth0, 4)

    def sweep0(old, new, lo, hi):
        def body(x):
            m = plane_mask(my0, i * NX + x - 4, count_x)
            u, around_u = around(old, x)
            for k in range(nz):
                new[x, k] = (C0 * u[k] + D * (F0[x, k] + around_u[k])) * m

        each(lo, hi, body, 4)

    sweep0(V0, X0, 2, 14)
    sweep0(X0, V0, 3, 13)

    def finish(x):
        u, around_u = around(V0, x + 4)
        for k in range(nz):
            s = slice(k * LANES, (k + 1) * LANES)
            press[x, :, s] = u[k][4:20]
            resid[x, :, s] = (F0[x + 4, k] - 6.0 * u[k] + around_u[k])[4:20]

    each(0, NX, finish, 4)


def call(kernel, outs, scratch, *args, us=1.0):
    return pl.pallas_call(
        kernel,
        out_shape=[jax.ShapeDtypeStruct(s, f32) for s in outs],
        scratch_shapes=[pltpu.VMEM(s, f32) for s in scratch],
        compiler_params=pltpu.CompilerParams(vmem_limit_bytes=20 * 1024 * 1024),
        cost_estimate=pl.CostEstimate(flops=0, transcendentals=0, bytes_accessed=int(us * 3.6e6)),
    )(*args)


def swaps(leaves, subs):
    def table(partner):
        return [(i * subs + j, (lambda t: t[0] * subs + t[1])(partner(i, j))) for i in range(leaves) for j in range(subs)]

    def odd(n):
        return ((n + 1) ^ 1) - 1

    def inner(n, count):
        return 0 <= n < count

    a = table(lambda i, j: (i ^ 1, j))
    b = table(lambda i, j: (odd(i), j) if inner(odd(i), leaves) else (i, j ^ 1))
    s1 = table(lambda i, j: (i, j ^ 1))
    s2 = table(lambda i, j: (i, odd(j)) if inner(odd(j), subs) else (i ^ 1, j))
    c1 = table(lambda i, j: (i ^ 2, j))
    c2 = table(lambda i, j: (2 * odd(i // 2) + i % 2, j) if inner(odd(i // 2), leaves // 2) else (i ^ 1, j))

    def two_on(i):
        t = 2 * (i // 2 + (2 if i % 2 else -2)) + 1 - i % 2
        return t if inner(t, leaves) else None

    e = table(lambda i, j: (two_on(i), j) if two_on(i) is not None else (i ^ 2, j))
    return a, b, s1, s2, c1, c2, e


def shards(dims, volume_fraction, interface_mask):
    leaves, subs = dims
    depth = volume_fraction.shape[2]
    nz = depth // LANES
    pa, pb, ps1, ps2, pc1, pc2, pe = swaps(leaves, subs)
    move = lambda v, table: lax.ppermute(v, AXES, table)
    n1, n2, n3 = nz // 2, nz // 4, nz // 8

    plane, rows = (1, NY, depth), (NX, depth)
    to_a, to_b, to_1, to_2 = call(functools.partial(edges, dims), [plane, plane, rows, rows], [], volume_fraction)
    halos = move(to_a, pa), move(to_b, pb), move(to_1, ps1), move(to_2, ps2)
    shape = (NX, nz, NY, LANES)
    heights, slope = call(columns, [shape, shape], [], volume_fraction, interface_mask)
    (src,) = call(functools.partial(source, dims), [(NX, NY, depth)], [], heights, slope, *halos)
    big, m2a, m2b, own2 = call(
        functools.partial(descent, dims),
        [(7, NY, depth)] + [(2, 8, depth // 4)] * 3,
        [
            (6, 8, depth // 4),
            (16, nz, 24, LANES),
            (16, nz, 24, LANES),
            (8, nz, 24, LANES),
            (14, n1, 16, LANES),
            (14, n1, 16, LANES),
            (6, n1, 16, LANES),
        ],
        src,
    )
    r2a, r2b, ra = move(m2a, pa), move(m2b, pb), move(big, pa)
    out, to_b = call(
        functools.partial(middle, dims), [(2 * subs, 2, 8, depth // 4), (7, NY, depth)], [], own2, r2a, r2b, src, big, ra
    )
    rb = move(to_b, pb)
    group = [list(range(k, k + 2 * subs)) for k in range(0, leaves * subs, 2 * subs)]
    got = lax.all_to_all(out, AXES, 0, 0, axis_index_groups=group)
    got, rb = lax.optimization_barrier((got, rb))
    far = move(rb[4:7], pa)
    chips = leaves // 2
    f2, edge, out = call(
        functools.partial(chip2, dims),
        [(4, 16, depth // 4), (1, 16, depth // 4), (chips, 4, 8, depth // 8)],
        [(10, n2, 16, LANES), (10, n2, 16, LANES), (4, n2, 16, LANES)],
        got,
    )
    f1x, s1, s2 = call(
        functools.partial(rows_out, dims),
        [(14, 16, depth // 2), (15, 8, depth), (15, 8, depth)],
        [],
        src,
        big,
        ra,
        rb,
        far,
    )
    out, s1, s2 = lax.optimization_barrier((out, s1, s2))
    rs1, rs2 = move(s1, ps1), move(s2, ps2)
    group = [[(2 * c + k) * subs + s for c in range(chips)] for k in (0, 1) for s in range(subs)]
    got = lax.all_to_all(out, AXES, 0, 0, axis_index_groups=group)
    r2c1, r2c2, r2e = move(f2, pc1), move(f2, pc2), move(edge, pe)
    (u3,) = call(
        functools.partial(coarsest, dims), [(5, 8, depth // 8)], [(leaves + 4, n3, 8, LANES)] * 3, got
    )
    shape0, shape1 = (16, nz, 24, LANES), (14, n1, 24, LANES)
    F0, P0, F1, P1 = call(functools.partial(ready, dims), [shape0, shape0, shape1, shape1], [], src, ra, rb, f1x, rs1, rs2)
    return call(
        functools.partial(ascent, dims),
        [(NX, NY, depth), (NX, NY, depth)],
        [
            (14, n2, 16, LANES),
            (5, n2, 16, LANES),
            (10, n2, 16, LANES),
            (10, n2, 16, LANES),
            (6, n1, 24, LANES),
            shape1,
            shape1,
            (8, nz, 24, LANES),
            shape0,
            shape0,
        ],
        u3,
        f2,
        r2c1,
        r2c2,
        r2e,
        F0,
        P0,
        F1,
        P1,
    )


def solution(mesh):
    spec = P("leaf", "sub", None)
    dims = (mesh.shape["leaf"], mesh.shape["sub"])
    body = functools.partial(shards, dims)
    return jax.shard_map(body, mesh=mesh, in_specs=(spec, spec), out_specs=(spec, spec), check_vma=False)
```

```python
import functools

import jax
import jax.numpy as jnp
from jax import lax
from jax.experimental import pallas as pl
from jax.experimental.pallas import tpu as pltpu
from jax.sharding import PartitionSpec as P

D = 0.8 / 6.0
C1 = 2.0 * D - 6.0 * D * D
C2 = D * D
C0 = 1.0 - 6.0 * D
NX, NY = 8, 16
LANES = 128
AXES = ("leaf", "sub")
f32 = jnp.float32


def lanes(rows):
    return lax.broadcasted_iota(jnp.int32, (rows, LANES), 1)


def rows_of(rows):
    return lax.broadcasted_iota(jnp.int32, (rows, LANES), 0)


def lane_before(col):
    lane = lanes(col.shape[0])
    wrapped = jnp.where(lane == 0, 0.0, pltpu.roll(col, 9, 1))
    return jnp.where(lane < 8, wrapped, pltpu.roll(col, 8, 1))


def lane_after(col):
    lane = lanes(col.shape[0])
    wrapped = jnp.where(lane == LANES - 1, 0.0, pltpu.roll(col, LANES - 9, 1))
    return jnp.where(lane >= LANES - 8, wrapped, pltpu.roll(col, LANES - 8, 1))


def along_z(cols):
    return [lane_before(cols[-1])] + cols[:-1], cols[1:] + [lane_after(cols[0])]


def regroup(cols):
    cols = list(cols)
    lane = lanes(cols[0].shape[0])
    for s in (1, 2, 4):
        low, beside = (lane & s) == 0, lane ^ s
        for a in range(8):
            b = a | s
            if a != b:
                moved = jnp.where(low, cols[b], cols[a])
                moved = jnp.take_along_axis(moved, beside, axis=1, mode="promise_in_bounds")
                cols[a], cols[b] = jnp.where(low, cols[a], moved), jnp.where(low, moved, cols[b])
    return cols


def around(ref, x, whole=False):
    n, rows = ref.shape[1], ref.shape[2]
    cols = [ref[x, k] for k in range(n)]
    before, after = along_z(cols)
    out = []
    for k, c in enumerate(cols):
        up, down = pltpu.roll(c, rows - 1, 0), pltpu.roll(c, 1, 0)
        if whole:
            row = rows_of(rows)
            up, down = jnp.where(row == rows - 1, 0.0, up), jnp.where(row == 0, 0.0, down)
        out.append((ref[x + 1, k] + ref[x - 1, k]) + (up + down) + (before[k] + after[k]))
    return cols, out


def restricted(tmp, rows):
    sums = [tmp[k, pl.ds(0, rows, 2), :] + tmp[k, pl.ds(1, rows, 2), :] for k in range(tmp.shape[0])]
    return [0.5 * (sums[2 * m] + sums[2 * m + 1]) for m in range(tmp.shape[0] // 2)]


def prolonged(tmp, cols, rows, at=0):
    for m, c in enumerate(cols):
        tmp[m, pl.ds(at, rows, 2), :] = c
        tmp[m, pl.ds(at + 1, rows, 2), :] = c


def inside(pos, count):
    return jnp.logical_and(pos >= 0, pos < count)


def row_mask(rows, start, count):
    pos = rows_of(rows) + start
    return jnp.where(inside(pos, count), 1.0, 0.0).astype(f32)


def plane_mask(mask, x, count):
    return mask * jnp.where(inside(x, count), 1.0, 0.0).astype(f32)


def each(lo, hi, body, together=1):
    steps = (hi - lo) // together

    def step(s, carry):
        for t in range(together):
            body(lo + s * together + t)
        return carry

    lax.fori_loop(0, steps, step, 0)
    for x in range(lo + steps * together, hi):
        body(x)


def taps(cols):
    n = len(cols)
    more = [lane_before(c) for c in cols[-3:]] + cols + [lane_after(c) for c in cols[:3]]
    out = [((more[k] + more[k + 1]) + (more[k + 2] + more[k + 3])) + ((more[k + 4] + more[k + 5]) + more[k + 6]) for k in range(n)]
    return out, more[2 : n + 2], more[4 : n + 4]


def split(value):
    return regroup(value[:, k * LANES : (k + 1) * LANES] for k in range(value.shape[1] // LANES))


def place(leaves, subs):
    i, j = lax.axis_index("leaf"), lax.axis_index("sub")
    odd_i, odd_j = i % 2 == 1, j % 2 == 1
    far_i = jnp.where(odd_i, i < leaves - 1, i > 0)
    far_j = jnp.where(odd_j, j < subs - 1, j > 0)
    return i, j, odd_i, odd_j, far_i, far_j


def edges(dims, vf, to_a, to_b, to_1, to_2):
    _, _, odd_i, odd_j, _, _ = place(*dims)
    to_a[0] = vf[jnp.where(odd_i, 0, NX - 1)]
    to_b[0] = vf[jnp.where(odd_i, NX - 1, 0)]
    for x in range(NX):
        first, last = vf[x, 0:1, :], vf[x, NY - 1 : NY, :]
        to_1[x : x + 1, :] = jnp.where(odd_j, first, last)
        to_2[x : x + 1, :] = jnp.where(odd_j, last, first)


def columns(vf, mask_in, H, G, mask, sem):
    nz = vf.shape[2] // LANES
    copy = pltpu.make_async_copy(mask_in, mask, sem)
    copy.start()

    def level0(x):
        h, before, after = taps(split(vf[x]))
        for k in range(nz):
            H[x, k] = h[k]
            G[x, k] = 0.5 * (after[k] - before[k])

    def masked(x):
        m = split(mask[x].astype(f32))
        for k in range(nz):
            G[x, k] = G[x, k] * m[k]

    each(0, NX, level0, 4)
    copy.wait()
    each(0, NX, masked, 8)


def source(dims, H, G, ra, rb, rs1, rs2, src):
    _, _, odd_i, odd_j, far_i, far_j = place(*dims)
    nz = H.shape[1]
    far_x = jnp.where(far_i, 1.0, 0.0).astype(f32)
    far_y = jnp.where(far_j, 1.0, 0.0).astype(f32)
    ha, _, _ = taps(split(ra[0]))
    hb, _, _ = taps(split(rb[0]))
    hs1, _, _ = taps(split(rs1[...]))
    hs2, _, _ = taps(split(rs2[...]))
    row = rows_of(NY)
    for k in range(nz):
        b = hb[k] * far_x
        below, above = jnp.where(odd_i, ha[k], b), jnp.where(odd_i, b, ha[k])
        low = jnp.where(odd_j, hs1[k], hs2[k] * far_y)
        high = jnp.where(odd_j, hs2[k] * far_y, hs1[k])
        for x in range(NX):
            h = H[x, k]
            up = jnp.where(row == NY - 1, high[x : x + 1, :], pltpu.roll(h, NY - 1, 0))
            down = jnp.where(row == 0, low[x : x + 1, :], pltpu.roll(h, 1, 0))
            ahead = H[x + 1, k] if x < NX - 1 else above
            behind = H[x - 1, k] if x > 0 else below
            sx, sy = 0.5 * (ahead - behind), 0.5 * (up - down)
            bend = ahead - 2.0 * h + behind + (up - 2.0 * h + down)
            inv = lax.rsqrt(1.0 + sx * sx + sy * sy)
            src[x, :, k * LANES : (k + 1) * LANES] = G[x, k] * (bend * (inv * inv * inv))


def descent(dims, src, big, m2a, m2b, own2, F1c, F0, U0, T0, F1, U1, T1):
    leaves, subs = dims
    i, j, odd_i, odd_j, far_i, far_j = place(leaves, subs)
    nz = src.shape[2] // LANES
    zero = jnp.zeros((16, LANES), f32)
    zero24 = jnp.zeros((24, LANES), f32)
    for x in range(16):
        for k in range(nz):
            if 4 <= x < 12:
                F0[x, k, 0:4, :] = zero24[0:4]
                F0[x, k, 4:20, :] = src[x - 4, :, k * LANES : (k + 1) * LANES]
                F0[x, k, 20:24, :] = zero24[0:4]
            else:
                F0[x, k] = zero24

    count_x, count_y = leaves * NX, subs * NY
    my0 = row_mask(24, j * NY - 4, count_y)
    for x in (1, 2, 13, 14):
        for k in range(nz):
            U0[x, k] = zero24

    def smooth0(x):
        m = plane_mask(my0, i * NX + x - 4, count_x)
        f, around_f = around(F0, x)
        for k in range(nz):
            U0[x, k] = (C1 * f[k] + C2 * around_f[k]) * m

    each(3, 13, smooth0, 5)

    for x in range(0, 14):
        if x < 4 or x >= 10:
            for k in range(nz // 2):
                F1[x, k] = zero

    def restrict0(c):
        total = [zero24] * nz
        for p in (0, 1):
            x = 2 * c + p
            m = plane_mask(my0, i * NX + x - 4, count_x)
            u, around_u = around(U0, x)
            total = [total[k] + (F0[x, k] - 6.0 * u[k] + around_u[k]) * m for k in range(nz)]
        for k in range(nz):
            T0[c, k] = total[k]
        for k, v in enumerate(restricted(T0.at[c], 12)):
            F1[c + 3, k, 0:2, :] = zero[0:2]
            F1[c + 3, k, 2:14, :] = v
            F1[c + 3, k, 14:16, :] = zero[0:2]

    each(1, 7, restrict0, 2)

    n1 = nz // 2
    my1 = row_mask(16, j * (NY // 2) - 4, count_y // 2)
    for x in (0, 1, 2, 11, 12, 13):
        for k in range(n1):
            U1[x, k] = zero

    def smooth1(x):
        m = plane_mask(my1, i * (NX // 2) + x - 5, count_x // 2)
        f, around_f = around(F1, x)
        for k in range(n1):
            U1[x, k] = (C1 * f[k] + C2 * around_f[k]) * m

    each(3, 11, smooth1, 4)

    def restrict1(c):
        total = [zero] * n1
        for p in (0, 1):
            x = 2 * c + 1 + p
            m = plane_mask(my1, i * (NX // 2) + x - 5, count_x // 2)
            u, around_u = around(U1, x)
            total = [total[k] + (F1[x, k] - 6.0 * u[k] + around_u[k]) * m for k in range(n1)]
        for k in range(n1):
            T1[c, k] = total[k]
        for k, v in enumerate(restricted(T1.at[c], 8)):
            F1c[c, :, k * LANES : (k + 1) * LANES] = v

    each(0, 6, restrict1, 3)

    at = jnp.where(odd_i, 0, 4)
    m2a[...] = F1c[pl.ds(at, 2)]
    m2b[...] = F1c[pl.ds(4 - at, 2)]
    own2[...] = F1c[2:4]
    big[0:4] = src[pl.ds(at, 4)]
    for p in range(3):
        for k in range(n1):
            for h in (0, 1):
                big[4 + p, :, (h * n1 + k) * LANES : (h * n1 + k + 1) * LANES] = F1[4 + p + 3 * h, k]


def half_planes(ref, p):
    n = ref.shape[2] // 2
    return ref[4 + p % 3, :, (p // 3) * n : (p // 3 + 1) * n]


def middle(dims, own2, r2a, r2b, src, big, ra, out, to_b):
    _, _, odd_i, _, far_i, _ = place(*dims)
    n = src.shape[2] // 2
    v = own2[...] + r2a[...] + jnp.where(far_i, r2b[...], 0.0)
    for k in range(out.shape[0]):
        out[k] = v
    to_b[0:4] = src[pl.ds(jnp.where(odd_i, 4, 0), 4)]
    more = {
        0: jnp.where(odd_i, half_planes(ra, 4), 0.0),
        1: jnp.where(odd_i, half_planes(ra, 5), 0.0),
        4: jnp.where(odd_i, 0.0, half_planes(ra, 0)),
        5: jnp.where(odd_i, 0.0, half_planes(ra, 1)),
    }
    for p in range(6):
        v = half_planes(big, p)
        to_b[4 + p % 3, :, (p // 3) * n : (p // 3 + 1) * n] = v + more[p] if p in more else v


def chip2(dims, got, f2, edge, out, F2, U2, T2):
    leaves, subs = dims
    i = lax.axis_index("leaf")
    odd_i, c = i % 2 == 1, i // 2
    n2 = f2.shape[2] // LANES
    row = rows_of(8)
    zero = jnp.zeros((16, LANES), f32)
    for x in (0, 1, 2, 7, 8, 9):
        for k in range(n2):
            F2[x, k] = zero
    for x in (0, 1, 8, 9):
        for k in range(n2):
            U2[x, k] = zero
    for x in range(4):
        for k in range(n2):
            s = slice(k * LANES, (k + 1) * LANES)
            t = [got[4 * (x // 2) + j, x % 2, :, s] for j in range(4)]
            one, two = pltpu.roll(t[1], 2, 0), pltpu.roll(t[2], 6, 0)
            lo = jnp.where(row < 6, pltpu.roll(t[0], 6, 0), two) + jnp.where(row >= 2, one, 0.0)
            hi = jnp.where(row >= 2, pltpu.roll(t[3], 2, 0), one) + jnp.where(row < 6, two, 0.0)
            f2[x, 0:8, s] = lo
            f2[x, 8:16, s] = hi
            F2[x + 3, k, 0:8, :] = lo
            F2[x + 3, k, 8:16, :] = hi
    edge[0] = f2[jnp.where(odd_i, 3, 0)]
    m2 = jnp.ones((16, LANES), f32)
    for x in range(2, 8):
        m = plane_mask(m2, 4 * c + x - 3, 2 * leaves)
        f, around_f = around(F2, x, True)
        for k in range(n2):
            U2[x, k] = (C1 * f[k] + C2 * around_f[k]) * m
    for q in range(4):
        total = [zero] * n2
        for x in (2 * q + 1, 2 * q + 2):
            m = plane_mask(m2, 4 * c + x - 3, 2 * leaves)
            u, around_u = around(U2, x, True)
            total = [total[k] + (F2[x, k] - 6.0 * u[k] + around_u[k]) * m for k in range(n2)]
        for k in range(n2):
            T2[q, k] = total[k]
    for q in range(4):
        for k, v in enumerate(restricted(T2.at[q], 8)):
            for t in range(out.shape[0]):
                out[t, q, :, k * LANES : (k + 1) * LANES] = in_order(v)


def rows_out(dims, src, big, ra, rb, far, f1x, s1, s2):
    _, _, odd_i, odd_j, far_i, _ = place(*dims)
    i = lax.axis_index("leaf")
    n = src.shape[2] // 2
    a = [half_planes(ra, p) for p in range(6)]
    b = [jnp.where(far_i, half_planes(rb, p), 0.0) for p in range(6)]
    before = [jnp.where(odd_i, a[p], b[p]) for p in range(6)]
    after = [jnp.where(odd_i, b[p], a[p]) for p in range(6)]
    far_two = jnp.where(odd_i, i > 1, i < dims[0] - 2)
    d = [jnp.where(far_two, far[p % 3, :, (p // 3) * n : (p // 3 + 1) * n], 0.0) for p in (0, 1, 4, 5)]
    before2 = [jnp.where(odd_i, d[2 + h], 0.0) for h in (0, 1)]
    after2 = [jnp.where(odd_i, 0.0, d[h]) for h in (0, 1)]
    own = [half_planes(big, p) for p in range(6)]
    planes = {}

    def add(x, v):
        planes[x] = planes[x] + v if x in planes else v

    for p in range(6):
        add(p - 1, own[p])
        add(p - 5, before[p])
        add(p + 3, after[p])
    for h in (0, 1):
        add(-5 + h, before2[h])
        add(7 + h, after2[h])
    for x in range(14):
        f1x[x] = planes[x - 5]

    def fine(x):
        if 4 <= x < 12:
            return src[x - 4]
        if x < 4:
            return jnp.where(odd_i, ra[x], jnp.where(far_i, rb[x], 0.0))
        return jnp.where(odd_i, jnp.where(far_i, rb[x - 12], 0.0), ra[x - 12])

    for x in range(8):
        u, v = fine(x), fine(x + 8)
        for out, up in ((s1, odd_j == False), (s2, odd_j)):
            out[x, 0:4, :] = jnp.where(up, u[12:16], u[0:4])
            out[x, 4:8, :] = jnp.where(up, v[12:16], v[0:4])
    for x in range(14):
        v = planes[x - 5]
        s = slice((x // 7) * n, (x // 7 + 1) * n)
        last, first = v[5:13], v[3:11]
        s1[8 + x % 7, :, s] = jnp.where(odd_j, first, last)
        s2[8 + x % 7, :, s] = jnp.where(odd_j, last, first)


def in_order(col):
    lane = lanes(col.shape[0])
    return jnp.take_along_axis(col, 8 * (lane % 16) + lane // 16, axis=1, mode="promise_in_bounds")


def as_kept(col):
    lane = lanes(col.shape[0])
    return jnp.take_along_axis(col, 16 * (lane % 8) + lane // 8, axis=1, mode="promise_in_bounds")


def coarsest(dims, got, out, G3):
    leaves = dims[0]
    chips = got.shape[0]
    i = lax.axis_index("leaf")
    zero = jnp.zeros((8, LANES), f32)
    for x in range(9):
        G3[x] = zero
        G3[leaves + 9 + x] = zero
    for c in range(chips):
        a, b = got[c, 1], got[c, 2]
        if c > 0:
            a = a + got[c - 1, 3]
        if c < chips - 1:
            b = b + got[c + 1, 0]
        G3[2 * c + 9], G3[2 * c + 10] = a, b
    lane, row = lanes(8), rows_of(8)
    ends = [lane == 0, lane == LANES - 1, row == 0, row == 7]
    f = [D * G3[i + w] for w in range(19)]
    keep = [jnp.where(inside(i + w - 9, leaves), 1.0, 0.0).astype(f32) for w in range(19)]
    u = list(f)
    for s in range(1, 8):
        new = list(u)
        for w in range(s, 19 - s):
            c = u[w]
            z = jnp.where(ends[0], 0.0, pltpu.roll(c, 1, 1)) + jnp.where(ends[1], 0.0, pltpu.roll(c, LANES - 1, 1))
            y = jnp.where(ends[2], 0.0, pltpu.roll(c, 1, 0)) + jnp.where(ends[3], 0.0, pltpu.roll(c, 7, 0))
            new[w] = (C0 * c + (f[w] + D * ((u[w + 1] + u[w - 1]) + (y + z)))) * keep[w]
        u = new
    for x in range(5):
        out[x] = as_kept(u[7 + x])


def ready(dims, src, ra, rb, f1x, rs1, rs2, F0, P0, F1, P1):
    leaves, subs = dims
    i, j, odd_i, odd_j, far_i, far_j = place(leaves, subs)
    count_x, count_y = leaves * NX, subs * NY
    nz = src.shape[2] // LANES
    n1 = nz // 2
    zero = jnp.zeros((24, LANES), f32)
    far_x = jnp.where(far_i, 1.0, 0.0).astype(f32)

    low_j = jnp.where(j > 0, 1.0, 0.0).astype(f32)
    high_j = jnp.where(j < subs - 1, 1.0, 0.0).astype(f32)

    def fill1(x):
        part, at = x // 7, 8 + x % 7
        for k in range(n1):
            s = slice(k * LANES, (k + 1) * LANES)
            F1[x, k] = zero
            F1[x, k, 4:20, :] = f1x[x, :, s]
            s = slice((part * n1 + k) * LANES, (part * n1 + k + 1) * LANES)
            lo = jnp.where(odd_j, rs1[at, :, s], rs2[at, :, s]) * low_j
            hi = jnp.where(odd_j, rs2[at, :, s], rs1[at, :, s]) * high_j
            F1[x, k, 1:9, :] = F1[x, k, 1:9, :] + lo
            F1[x, k, 15:23, :] = F1[x, k, 15:23, :] + hi

    for x in range(14):
        fill1(x)
    my1 = row_mask(24, j * (NY // 2) - 8, count_y // 2)

    def smooth1(x):
        m = plane_mask(my1, i * (NX // 2) + x - 5, count_x // 2)
        f, around_f = around(F1, x)
        for k in range(n1):
            P1[x, k] = (C1 * f[k] + C2 * around_f[k]) * m

    each(1, 13, smooth1, 4)

    def fill0(x):
        if 4 <= x < 12:
            v = src[x - 4]
        elif x < 4:
            v = jnp.where(odd_i, ra[x], rb[x] * far_x)
        else:
            v = jnp.where(odd_i, rb[x - 12] * far_x, ra[x - 12])
        a, b = rs1[x % 8], rs2[x % 8]
        h = 4 * (x // 8)
        lo = jnp.where(odd_j, a[h : h + 4], b[h : h + 4]) * low_j
        hi = jnp.where(odd_j, b[h : h + 4], a[h : h + 4]) * high_j
        for k in range(nz):
            s = slice(k * LANES, (k + 1) * LANES)
            F0[x, k, 0:4, :] = lo[:, s]
            F0[x, k, 4:20, :] = v[:, s]
            F0[x, k, 20:24, :] = hi[:, s]

    for x in range(16):
        fill0(x)
    my0 = row_mask(24, j * NY - 4, count_y)

    def smooth0(x):
        m = plane_mask(my0, i * NX + x - 4, count_x)
        f, around_f = around(F0, x)
        for k in range(nz):
            P0[x, k] = (C1 * f[k] + C2 * around_f[k]) * m

    each(1, 15, smooth0, 4)


def ascent(dims, u3, f2, r2c1, r2c2, r2e, F0, P0, F1, P1, press_out, resid_out, F2, T2, W2, X2, T1, V1, X1, T0, V0, X0, press, resid, done):
    leaves, subs = dims
    i, j, odd_i, odd_j, far_i, far_j = place(leaves, subs)
    count_x, count_y = leaves * NX, subs * NY
    nz = F0.shape[1]
    n1, n2, n3 = nz // 2, nz // 4, nz // 8
    zero = jnp.zeros((24, LANES), f32)

    c, chips = i // 2, leaves // 2
    odd_c = c % 2 == 1
    far_c = jnp.where(jnp.where(odd_c, c < chips - 1, c > 0), 1.0, 0.0).astype(f32)
    far_e = jnp.where(jnp.where(odd_i, c < chips - 2, c > 1), 1.0, 0.0).astype(f32)
    base = jnp.where(odd_i, 2, 0)
    for k in range(n2):
        s = slice(k * LANES, (k + 1) * LANES)
        e = r2e[0, :, s] * far_e
        F2[0, k] = e
        F2[13, k] = e
        for x in range(4):
            a, b = r2c1[x, :, s], r2c2[x, :, s] * far_c
            F2[x + 1, k] = jnp.where(odd_c, a, b)
            F2[x + 5, k] = f2[x, :, s]
            F2[x + 9, k] = jnp.where(odd_c, b, a)
    m2 = jnp.ones((16, LANES), f32)
    for x in range(5):
        prolonged(T2.at[x], [u3[x, :, k * LANES : (k + 1) * LANES] for k in range(n3)], 8)
    for w in range(10):
        m = plane_mask(m2, 2 * i + w - 4, 2 * leaves)
        f, around_f = around(F2, base + w + 1, True)
        for k in range(n2):
            W2[w, k] = (C1 * f[k] + C2 * around_f[k] + T2[w // 2, k // 2]) * m

    def sweep2(old, new, lo, hi):
        for w in range(lo, hi):
            m = plane_mask(m2, 2 * i + w - 4, 2 * leaves)
            u, around_u = around(old, w, True)
            for k in range(n2):
                new[w, k] = (C0 * u[k] + D * (F2[base + w + 1, k] + around_u[k])) * m

    sweep2(W2, X2, 1, 9)
    sweep2(X2, W2, 2, 8)

    for c in range(6):
        for k in range(n2):
            T1[c, k] = zero
    my1 = row_mask(24, j * (NY // 2) - 8, count_y // 2)

    for c in range(6):
        cols = [pltpu.roll(W2[c + 2, k], (18 - 4 * j) % 16, 0)[0:8] for k in range(n2)]
        prolonged(T1.at[c], cols, 8, 4)
    for c in range(6):
        for p in (0, 1):
            x = 2 * c + p + 1
            m = plane_mask(my1, i * (NX // 2) + x - 5, count_x // 2)
            for k in range(n1):
                V1[x, k] = P1[x, k] + T1[c, k // 2] * m

    def sweep1(old, new, lo, hi):
        def body(x):
            m = plane_mask(my1, i * (NX // 2) + x - 5, count_x // 2)
            u, around_u = around(old, x)
            for k in range(n1):
                new[x, k] = (C0 * u[k] + D * (F1[x, k] + around_u[k])) * m

        each(lo, hi, body, (hi - lo) // 2)

    sweep1(V1, X1, 2, 12)
    sweep1(X1, V1, 3, 11)


    my0 = row_mask(24, j * NY - 4, count_y)

    def start0(c):
        prolonged(T0.at[c], [V1[c + 3, k, 6:18, :] for k in range(n1)], 12)

    each(0, 8, start0, 4)

    def smooth0(x):
        m = plane_mask(my0, i * NX + x - 4, count_x)
        for k in range(nz):
            V0[x, k] = P0[x, k] + T0[x // 2, k // 2] * m

    each(1, 15, smooth0, 4)

    def sweep0(old, new, lo, hi):
        def body(x):
            m = plane_mask(my0, i * NX + x - 4, count_x)
            u, around_u = around(old, x)
            for k in range(nz):
                new[x, k] = (C0 * u[k] + D * (F0[x, k] + around_u[k])) * m

        each(lo, hi, body, 4)

    sweep0(V0, X0, 2, 14)
    sweep0(X0, V0, 3, 13)

    def put(out, x, cols):
        for k, v in enumerate(regroup(cols)):
            out[x, :, k * LANES : (k + 1) * LANES] = v

    def rest(x):
        u = [V0[x + 4, k, 4:20, :] for k in range(nz)]
        before, after = along_z(u)
        res = []
        for k in range(nz):
            near = V0[x + 5, k, 4:20, :] + V0[x + 3, k, 4:20, :] + (V0[x + 4, k, 5:21, :] + V0[x + 4, k, 3:19, :])
            res.append(F0[x + 4, k, 4:20, :] - 6.0 * u[k] + (near + (before[k] + after[k])))
        put(resid, x, res)

    copies = []

    def away(t, a, b, x):
        copies.append(pltpu.make_async_copy(a.at[pl.ds(x, 4)], b.at[pl.ds(x, 4)], done.at[t, x // 4]))
        copies[-1].start()

    each(0, NX, lambda x: put(press, x, [V0[x + 4, k, 4:20, :] for k in range(nz)]), 4)
    for x in (0, 4):
        away(0, press, press_out, x)
    each(0, NX, rest, 4)
    for x in (0, 4):
        away(1, resid, resid_out, x)
    for copy in copies:
        copy.wait()


def call(kernel, outs, scratch, *args, here=(), away=False, mib=4):
    vmem, hbm = pl.BlockSpec(), pl.BlockSpec(memory_space=pltpu.HBM)
    return pl.pallas_call(
        kernel,
        out_shape=[jax.ShapeDtypeStruct(s, f32) for s in outs],
        in_specs=[hbm if n in here else vmem for n in range(len(args))],
        out_specs=[hbm if away else vmem for _ in outs],
        scratch_shapes=[pltpu.VMEM(s, f32) if isinstance(s, tuple) else s for s in scratch],
        compiler_params=pltpu.CompilerParams(vmem_limit_bytes=mib * 1024 * 1024),
    )(*args)


def swaps(leaves, subs):
    def table(partner):
        return [(i * subs + j, (lambda t: t[0] * subs + t[1])(partner(i, j))) for i in range(leaves) for j in range(subs)]

    def odd(n):
        return ((n + 1) ^ 1) - 1

    def inner(n, count):
        return 0 <= n < count

    a = table(lambda i, j: (i ^ 1, j))
    b = table(lambda i, j: (odd(i), j) if inner(odd(i), leaves) else (i, j ^ 1))
    s1 = table(lambda i, j: (i, j ^ 1))
    s2 = table(lambda i, j: (i, odd(j)) if inner(odd(j), subs) else (i ^ 1, j))
    c1 = table(lambda i, j: (i ^ 2, j))
    c2 = table(lambda i, j: (2 * odd(i // 2) + i % 2, j) if inner(odd(i // 2), leaves // 2) else (i ^ 1, j))

    def two_on(i):
        t = 2 * (i // 2 + (2 if i % 2 else -2)) + 1 - i % 2
        return t if inner(t, leaves) else None

    e = table(lambda i, j: (two_on(i), j) if two_on(i) is not None else (i ^ 2, j))
    return a, b, s1, s2, c1, c2, e


def shards(dims, volume_fraction, interface_mask):
    leaves, subs = dims
    depth = volume_fraction.shape[2]
    nz = depth // LANES
    pa, pb, ps1, ps2, pc1, pc2, pe = swaps(leaves, subs)
    move = lambda v, table: lax.ppermute(v, AXES, table)
    n1, n2, n3 = nz // 2, nz // 4, nz // 8

    plane, rows = (1, NY, depth), (NX, depth)
    to_a, to_b, to_1, to_2 = call(functools.partial(edges, dims), [plane, plane, rows, rows], [], volume_fraction)
    halos = move(to_a, pa), move(to_b, pb), move(to_1, ps1), move(to_2, ps2)
    shape = (NX, nz, NY, LANES)
    scratch = [pltpu.VMEM((NX, NY, depth), jnp.int32), pltpu.SemaphoreType.DMA]
    heights, slope = call(columns, [shape, shape], scratch, volume_fraction, interface_mask, here=(1,))
    (src,) = call(functools.partial(source, dims), [(NX, NY, depth)], [], heights, slope, *halos)
    big, m2a, m2b, own2 = call(
        functools.partial(descent, dims),
        [(7, NY, depth)] + [(2, 8, depth // 4)] * 3,
        [
            (6, 8, depth // 4),
            (16, nz, 24, LANES),
            (16, nz, 24, LANES),
            (8, nz, 24, LANES),
            (14, n1, 16, LANES),
            (14, n1, 16, LANES),
            (6, n1, 16, LANES),
        ],
        src,
        mib=10,
    )
    r2a, r2b, ra = move(m2a, pa), move(m2b, pb), move(big, pa)
    out, to_b = call(
        functools.partial(middle, dims), [(2 * subs, 2, 8, depth // 4), (7, NY, depth)], [], own2, r2a, r2b, src, big, ra
    )
    rb = move(to_b, pb)
    group = [list(range(k, k + 2 * subs)) for k in range(0, leaves * subs, 2 * subs)]
    got = lax.all_to_all(out, AXES, 0, 0, axis_index_groups=group)
    got, rb = lax.optimization_barrier((got, rb))
    far = move(rb[4:7], pa)
    chips = leaves // 2
    f2, edge, out = call(
        functools.partial(chip2, dims),
        [(4, 16, depth // 4), (1, 16, depth // 4), (chips, 4, 8, depth // 8)],
        [(10, n2, 16, LANES), (10, n2, 16, LANES), (4, n2, 16, LANES)],
        got,
    )
    f1x, s1, s2 = call(
        functools.partial(rows_out, dims),
        [(14, 16, depth // 2), (15, 8, depth), (15, 8, depth)],
        [],
        src,
        big,
        ra,
        rb,
        far,
    )
    out, s1, s2 = lax.optimization_barrier((out, s1, s2))
    rs1, rs2 = move(s1, ps1), move(s2, ps2)
    group = [[(2 * c + k) * subs + s for c in range(chips)] for k in (0, 1) for s in range(subs)]
    got = lax.all_to_all(out, AXES, 0, 0, axis_index_groups=group)
    r2c1, r2c2, r2e = move(f2, pc1), move(f2, pc2), move(edge, pe)
    shape0, shape1 = (16, nz, 24, LANES), (14, n1, 24, LANES)
    F0, P0, F1, P1 = call(functools.partial(ready, dims), [shape0, shape0, shape1, shape1], [], src, ra, rb, f1x, rs1, rs2, mib=10)
    (u3,) = call(functools.partial(coarsest, dims), [(5, 8, depth // 8)], [(leaves + 18, 8, LANES)], got)
    return call(
        functools.partial(ascent, dims),
        [(NX, NY, depth), (NX, NY, depth)],
        [
            (14, n2, 16, LANES),
            (5, n3, 16, LANES),
            (10, n2, 16, LANES),
            (10, n2, 16, LANES),
            (6, n2, 24, LANES),
            shape1,
            shape1,
            (8, n1, 24, LANES),
            shape0,
            shape0,
            (NX, NY, depth),
            (NX, NY, depth),
            pltpu.SemaphoreType.DMA((2, NX // 4)),
        ],
        u3,
        f2,
        r2c1,
        r2c2,
        r2e,
        F0,
        P0,
        F1,
        P1,
        away=True,
        mib=16,
    )


def solution(mesh):
    spec = P("leaf", "sub", None)
    dims = (mesh.shape["leaf"], mesh.shape["sub"])
    body = functools.partial(shards, dims)
    return jax.shard_map(body, mesh=mesh, in_specs=(spec, spec), out_specs=(spec, spec), check_vma=False)
```

```python
import functools

import jax
import jax.numpy as jnp
from jax import lax
from jax.experimental import pallas as pl
from jax.experimental.pallas import tpu as pltpu
from jax.sharding import PartitionSpec as P

D = 0.8 / 6.0
C1 = 2.0 * D - 6.0 * D * D
C2 = D * D
C0 = 1.0 - 6.0 * D
NX, NY = 8, 16
LANES = 128
AXES = ("leaf", "sub")
f32 = jnp.float32


def lanes(rows):
    return lax.broadcasted_iota(jnp.int32, (rows, LANES), 1)


def rows_of(rows):
    return lax.broadcasted_iota(jnp.int32, (rows, LANES), 0)


def lane_before(col):
    lane = lanes(col.shape[0])
    wrapped = jnp.where(lane == 0, 0.0, pltpu.roll(col, 9, 1))
    return jnp.where(lane < 8, wrapped, pltpu.roll(col, 8, 1))


def lane_after(col):
    lane = lanes(col.shape[0])
    wrapped = jnp.where(lane == LANES - 1, 0.0, pltpu.roll(col, LANES - 9, 1))
    return jnp.where(lane >= LANES - 8, wrapped, pltpu.roll(col, LANES - 8, 1))


def along_z(cols):
    return [lane_before(cols[-1])] + cols[:-1], cols[1:] + [lane_after(cols[0])]


def regroup(cols):
    cols = list(cols)
    lane = lanes(cols[0].shape[0])
    for s in (1, 2, 4):
        low, beside = (lane & s) == 0, lane ^ s
        for a in range(8):
            b = a | s
            if a != b:
                moved = jnp.where(low, cols[b], cols[a])
                moved = jnp.take_along_axis(moved, beside, axis=1, mode="promise_in_bounds")
                cols[a], cols[b] = jnp.where(low, cols[a], moved), jnp.where(low, moved, cols[b])
    return cols


def around(ref, x, whole=False):
    n, rows = ref.shape[1], ref.shape[2]
    cols = [ref[x, k] for k in range(n)]
    before, after = along_z(cols)
    out = []
    for k, c in enumerate(cols):
        up, down = pltpu.roll(c, rows - 1, 0), pltpu.roll(c, 1, 0)
        if whole:
            row = rows_of(rows)
            up, down = jnp.where(row == rows - 1, 0.0, up), jnp.where(row == 0, 0.0, down)
        out.append((ref[x + 1, k] + ref[x - 1, k]) + (up + down) + (before[k] + after[k]))
    return cols, out


def restricted(tmp, rows):
    sums = [tmp[k, pl.ds(0, rows, 2), :] + tmp[k, pl.ds(1, rows, 2), :] for k in range(tmp.shape[0])]
    return [0.5 * (sums[2 * m] + sums[2 * m + 1]) for m in range(tmp.shape[0] // 2)]


def prolonged(tmp, cols, rows, at=0):
    for m, c in enumerate(cols):
        tmp[m, pl.ds(at, rows, 2), :] = c
        tmp[m, pl.ds(at + 1, rows, 2), :] = c


def inside(pos, count):
    return jnp.logical_and(pos >= 0, pos < count)


def row_mask(rows, start, count):
    pos = rows_of(rows) + start
    return jnp.where(inside(pos, count), 1.0, 0.0).astype(f32)


def plane_mask(mask, x, count):
    return mask * jnp.where(inside(x, count), 1.0, 0.0).astype(f32)


def each(lo, hi, body, together=1):
    steps = (hi - lo) // together

    def step(s, carry):
        for t in range(together):
            body(lo + s * together + t)
        return carry

    lax.fori_loop(0, steps, step, 0)
    for x in range(lo + steps * together, hi):
        body(x)


def taps(cols):
    n = len(cols)
    more = [lane_before(c) for c in cols[-3:]] + cols + [lane_after(c) for c in cols[:3]]
    out = [((more[k] + more[k + 1]) + (more[k + 2] + more[k + 3])) + ((more[k + 4] + more[k + 5]) + more[k + 6]) for k in range(n)]
    return out, more[2 : n + 2], more[4 : n + 4]


def split(value):
    return regroup(value[:, k * LANES : (k + 1) * LANES] for k in range(value.shape[1] // LANES))


def place(leaves, subs):
    i, j = lax.axis_index("leaf"), lax.axis_index("sub")
    odd_i, odd_j = i % 2 == 1, j % 2 == 1
    far_i = jnp.where(odd_i, i < leaves - 1, i > 0)
    far_j = jnp.where(odd_j, j < subs - 1, j > 0)
    return i, j, odd_i, odd_j, far_i, far_j


def edges(dims, vf, to_a, to_b, to_1, to_2):
    _, _, odd_i, odd_j, _, _ = place(*dims)
    to_a[0] = vf[jnp.where(odd_i, 0, NX - 1)]
    to_b[0] = vf[jnp.where(odd_i, NX - 1, 0)]
    for x in range(NX):
        first, last = vf[x, 0:1, :], vf[x, NY - 1 : NY, :]
        to_1[x : x + 1, :] = jnp.where(odd_j, first, last)
        to_2[x : x + 1, :] = jnp.where(odd_j, last, first)


def columns(vf, H, G):
    nz = vf.shape[2] // LANES

    def level0(x):
        h, before, after = taps(split(vf[x]))
        for k in range(nz):
            H[x, k] = h[k]
            G[x, k] = 0.5 * (after[k] - before[k])

    each(0, NX, level0, 4)


def masked(G, mask, out):
    def body(x):
        m = split(mask[x].astype(f32))
        for k in range(len(m)):
            out[x, k] = G[x, k] * m[k]

    each(0, NX, body, 8)


def source(dims, H, G, ra, rb, rs1, rs2, src):
    _, _, odd_i, odd_j, far_i, far_j = place(*dims)
    nz = H.shape[1]
    far_x = jnp.where(far_i, 1.0, 0.0).astype(f32)
    far_y = jnp.where(far_j, 1.0, 0.0).astype(f32)
    ha, _, _ = taps(split(ra[0]))
    hb, _, _ = taps(split(rb[0]))
    hs1, _, _ = taps(split(rs1[...]))
    hs2, _, _ = taps(split(rs2[...]))
    row = rows_of(NY)
    for k in range(nz):
        b = hb[k] * far_x
        below, above = jnp.where(odd_i, ha[k], b), jnp.where(odd_i, b, ha[k])
        low = jnp.where(odd_j, hs1[k], hs2[k] * far_y)
        high = jnp.where(odd_j, hs2[k] * far_y, hs1[k])
        for x in range(NX):
            h = H[x, k]
            up = jnp.where(row == NY - 1, high[x : x + 1, :], pltpu.roll(h, NY - 1, 0))
            down = jnp.where(row == 0, low[x : x + 1, :], pltpu.roll(h, 1, 0))
            ahead = H[x + 1, k] if x < NX - 1 else above
            behind = H[x - 1, k] if x > 0 else below
            sx, sy = 0.5 * (ahead - behind), 0.5 * (up - down)
            bend = ahead - 2.0 * h + behind + (up - 2.0 * h + down)
            inv = lax.rsqrt(1.0 + sx * sx + sy * sy)
            src[x, :, k * LANES : (k + 1) * LANES] = G[x, k] * (bend * (inv * inv * inv))


def descent(dims, src, big, m2b, own2, F1c, F0, U0, T0, F1, U1, T1):
    leaves, subs = dims
    i, j, odd_i, odd_j, far_i, far_j = place(leaves, subs)
    nz = src.shape[2] // LANES
    zero = jnp.zeros((16, LANES), f32)
    zero24 = jnp.zeros((24, LANES), f32)
    for x in range(16):
        for k in range(nz):
            if 4 <= x < 12:
                F0[x, k, 0:4, :] = zero24[0:4]
                F0[x, k, 4:20, :] = src[x - 4, :, k * LANES : (k + 1) * LANES]
                F0[x, k, 20:24, :] = zero24[0:4]
            else:
                F0[x, k] = zero24

    count_x, count_y = leaves * NX, subs * NY
    my0 = row_mask(24, j * NY - 4, count_y)
    for x in (1, 2, 13, 14):
        for k in range(nz):
            U0[x, k] = zero24

    def smooth0(x):
        m = plane_mask(my0, i * NX + x - 4, count_x)
        f, around_f = around(F0, x)
        for k in range(nz):
            U0[x, k] = (C1 * f[k] + C2 * around_f[k]) * m

    each(3, 13, smooth0, 5)

    for x in range(0, 14):
        if x < 4 or x >= 10:
            for k in range(nz // 2):
                F1[x, k] = zero

    def restrict0(c):
        total = [zero24] * nz
        for p in (0, 1):
            x = 2 * c + p
            m = plane_mask(my0, i * NX + x - 4, count_x)
            u, around_u = around(U0, x)
            total = [total[k] + (F0[x, k] - 6.0 * u[k] + around_u[k]) * m for k in range(nz)]
        for k in range(nz):
            T0[c, k] = total[k]
        for k, v in enumerate(restricted(T0.at[c], 12)):
            F1[c + 3, k, 0:2, :] = zero[0:2]
            F1[c + 3, k, 2:14, :] = v
            F1[c + 3, k, 14:16, :] = zero[0:2]

    each(1, 7, restrict0, 2)

    n1 = nz // 2
    my1 = row_mask(16, j * (NY // 2) - 4, count_y // 2)
    for x in (0, 1, 2, 11, 12, 13):
        for k in range(n1):
            U1[x, k] = zero

    def smooth1(x):
        m = plane_mask(my1, i * (NX // 2) + x - 5, count_x // 2)
        f, around_f = around(F1, x)
        for k in range(n1):
            U1[x, k] = (C1 * f[k] + C2 * around_f[k]) * m

    each(3, 11, smooth1, 4)

    def restrict1(c):
        total = [zero] * n1
        for p in (0, 1):
            x = 2 * c + 1 + p
            m = plane_mask(my1, i * (NX // 2) + x - 5, count_x // 2)
            u, around_u = around(U1, x)
            total = [total[k] + (F1[x, k] - 6.0 * u[k] + around_u[k]) * m for k in range(n1)]
        for k in range(n1):
            T1[c, k] = total[k]
        for k, v in enumerate(restricted(T1.at[c], 8)):
            F1c[c, :, k * LANES : (k + 1) * LANES] = v

    each(0, 6, restrict1, 3)

    at = jnp.where(odd_i, 0, 4)
    for x in (0, 1):
        big[7, 0:8, x * 2 * LANES : (x + 1) * 2 * LANES] = F1c[at + x]
    m2b[...] = F1c[pl.ds(4 - at, 2)]
    own2[...] = F1c[2:4]
    big[0:4] = src[pl.ds(at, 4)]
    for p in range(3):
        for k in range(n1):
            for h in (0, 1):
                big[4 + p, :, (h * n1 + k) * LANES : (h * n1 + k + 1) * LANES] = F1[4 + p + 3 * h, k]


def half_planes(ref, p):
    n = ref.shape[2] // 2
    return ref[4 + p % 3, :, (p // 3) * n : (p // 3 + 1) * n]


def middle(dims, own2, r2b, src, big, ra, out, to_b):
    _, _, odd_i, _, far_i, _ = place(*dims)
    n = src.shape[2] // 2
    for x in (0, 1):
        v = own2[x] + ra[7, 0:8, x * 2 * LANES : (x + 1) * 2 * LANES] + jnp.where(far_i, r2b[x], 0.0)
        for k in range(out.shape[0]):
            out[k, x] = v
    to_b[0:4] = src[pl.ds(jnp.where(odd_i, 4, 0), 4)]
    more = {
        0: jnp.where(odd_i, half_planes(ra, 4), 0.0),
        1: jnp.where(odd_i, half_planes(ra, 5), 0.0),
        4: jnp.where(odd_i, 0.0, half_planes(ra, 0)),
        5: jnp.where(odd_i, 0.0, half_planes(ra, 1)),
    }
    for p in range(6):
        v = half_planes(big, p)
        to_b[4 + p % 3, :, (p // 3) * n : (p // 3 + 1) * n] = v + more[p] if p in more else v


def chip2(dims, got, f2, edge, out, F2, U2, T2):
    leaves, subs = dims
    i = lax.axis_index("leaf")
    odd_i, c = i % 2 == 1, i // 2
    n2 = f2.shape[2] // LANES
    row = rows_of(8)
    zero = jnp.zeros((16, LANES), f32)
    for x in (0, 1, 2, 7, 8, 9):
        for k in range(n2):
            F2[x, k] = zero
    for x in (0, 1, 8, 9):
        for k in range(n2):
            U2[x, k] = zero
    for x in range(4):
        for k in range(n2):
            s = slice(k * LANES, (k + 1) * LANES)
            t = [got[4 * (x // 2) + j, x % 2, :, s] for j in range(4)]
            one, two = pltpu.roll(t[1], 2, 0), pltpu.roll(t[2], 6, 0)
            lo = jnp.where(row < 6, pltpu.roll(t[0], 6, 0), two) + jnp.where(row >= 2, one, 0.0)
            hi = jnp.where(row >= 2, pltpu.roll(t[3], 2, 0), one) + jnp.where(row < 6, two, 0.0)
            f2[x, 0:8, s] = lo
            f2[x, 8:16, s] = hi
            F2[x + 3, k, 0:8, :] = lo
            F2[x + 3, k, 8:16, :] = hi
    edge[0] = f2[jnp.where(odd_i, 3, 0)]
    m2 = jnp.ones((16, LANES), f32)
    for x in range(2, 8):
        m = plane_mask(m2, 4 * c + x - 3, 2 * leaves)
        f, around_f = around(F2, x, True)
        for k in range(n2):
            U2[x, k] = (C1 * f[k] + C2 * around_f[k]) * m
    for q in range(4):
        total = [zero] * n2
        for x in (2 * q + 1, 2 * q + 2):
            m = plane_mask(m2, 4 * c + x - 3, 2 * leaves)
            u, around_u = around(U2, x, True)
            total = [total[k] + (F2[x, k] - 6.0 * u[k] + around_u[k]) * m for k in range(n2)]
        for k in range(n2):
            T2[q, k] = total[k]
    for q in range(4):
        for k, v in enumerate(restricted(T2.at[q], 8)):
            for t in range(out.shape[0]):
                out[t, q, :, k * LANES : (k + 1) * LANES] = in_order(v)


def rows_out(dims, src, big, ra, rb, far, f1x, s1, s2):
    _, _, odd_i, odd_j, far_i, _ = place(*dims)
    i = lax.axis_index("leaf")
    n = src.shape[2] // 2
    a = [half_planes(ra, p) for p in range(6)]
    b = [jnp.where(far_i, half_planes(rb, p), 0.0) for p in range(6)]
    before = [jnp.where(odd_i, a[p], b[p]) for p in range(6)]
    after = [jnp.where(odd_i, b[p], a[p]) for p in range(6)]
    far_two = jnp.where(odd_i, i > 1, i < dims[0] - 2)
    d = [jnp.where(far_two, far[p % 3, :, (p // 3) * n : (p // 3 + 1) * n], 0.0) for p in (0, 1, 4, 5)]
    before2 = [jnp.where(odd_i, d[2 + h], 0.0) for h in (0, 1)]
    after2 = [jnp.where(odd_i, 0.0, d[h]) for h in (0, 1)]
    own = [half_planes(big, p) for p in range(6)]
    planes = {}

    def add(x, v):
        planes[x] = planes[x] + v if x in planes else v

    for p in range(6):
        add(p - 1, own[p])
        add(p - 5, before[p])
        add(p + 3, after[p])
    for h in (0, 1):
        add(-5 + h, before2[h])
        add(7 + h, after2[h])
    for x in range(14):
        f1x[x] = planes[x - 5]

    def fine(x):
        if 4 <= x < 12:
            return src[x - 4]
        if x < 4:
            return jnp.where(odd_i, ra[x], jnp.where(far_i, rb[x], 0.0))
        return jnp.where(odd_i, jnp.where(far_i, rb[x - 12], 0.0), ra[x - 12])

    for x in range(8):
        u, v = fine(x), fine(x + 8)
        for out, up in ((s1, odd_j == False), (s2, odd_j)):
            out[x, 0:4, :] = jnp.where(up, u[12:16], u[0:4])
            out[x, 4:8, :] = jnp.where(up, v[12:16], v[0:4])
    for x in range(14):
        v = planes[x - 5]
        s = slice((x // 7) * n, (x // 7 + 1) * n)
        last, first = v[5:13], v[3:11]
        s1[8 + x % 7, :, s] = jnp.where(odd_j, first, last)
        s2[8 + x % 7, :, s] = jnp.where(odd_j, last, first)


def in_order(col):
    lane = lanes(col.shape[0])
    return jnp.take_along_axis(col, 8 * (lane % 16) + lane // 16, axis=1, mode="promise_in_bounds")


def as_kept(col):
    lane = lanes(col.shape[0])
    return jnp.take_along_axis(col, 16 * (lane % 8) + lane // 8, axis=1, mode="promise_in_bounds")


def coarsest(dims, got, out, G3):
    leaves = dims[0]
    chips = got.shape[0]
    i = lax.axis_index("leaf")
    zero = jnp.zeros((8, LANES), f32)
    for x in range(9):
        G3[x] = zero
        G3[leaves + 9 + x] = zero
    for c in range(chips):
        a, b = got[c, 1], got[c, 2]
        if c > 0:
            a = a + got[c - 1, 3]
        if c < chips - 1:
            b = b + got[c + 1, 0]
        G3[2 * c + 9], G3[2 * c + 10] = a, b
    lane, row = lanes(8), rows_of(8)
    ends = [lane == 0, lane == LANES - 1, row == 0, row == 7]
    f = [D * G3[i + w] for w in range(19)]
    keep = [jnp.where(inside(i + w - 9, leaves), 1.0, 0.0).astype(f32) for w in range(19)]
    u = list(f)
    for s in range(1, 8):
        new = list(u)
        for w in range(s, 19 - s):
            c = u[w]
            z = jnp.where(ends[0], 0.0, pltpu.roll(c, 1, 1)) + jnp.where(ends[1], 0.0, pltpu.roll(c, LANES - 1, 1))
            y = jnp.where(ends[2], 0.0, pltpu.roll(c, 1, 0)) + jnp.where(ends[3], 0.0, pltpu.roll(c, 7, 0))
            new[w] = (C0 * c + (f[w] + D * ((u[w + 1] + u[w - 1]) + (y + z)))) * keep[w]
        u = new
    for x in range(5):
        out[x] = as_kept(u[7 + x])


def ready(dims, src, ra, rb, f1x, rs1, rs2, F0, P0, F1, P1):
    leaves, subs = dims
    i, j, odd_i, odd_j, far_i, far_j = place(leaves, subs)
    count_x, count_y = leaves * NX, subs * NY
    nz = src.shape[2] // LANES
    n1 = nz // 2
    zero = jnp.zeros((24, LANES), f32)
    far_x = jnp.where(far_i, 1.0, 0.0).astype(f32)

    low_j = jnp.where(j > 0, 1.0, 0.0).astype(f32)
    high_j = jnp.where(j < subs - 1, 1.0, 0.0).astype(f32)

    def fill1(x):
        part, at = x // 7, 8 + x % 7
        for k in range(n1):
            s = slice(k * LANES, (k + 1) * LANES)
            F1[x, k] = zero
            F1[x, k, 4:20, :] = f1x[x, :, s]
            s = slice((part * n1 + k) * LANES, (part * n1 + k + 1) * LANES)
            lo = jnp.where(odd_j, rs1[at, :, s], rs2[at, :, s]) * low_j
            hi = jnp.where(odd_j, rs2[at, :, s], rs1[at, :, s]) * high_j
            F1[x, k, 1:9, :] = F1[x, k, 1:9, :] + lo
            F1[x, k, 15:23, :] = F1[x, k, 15:23, :] + hi

    for x in range(14):
        fill1(x)
    my1 = row_mask(24, j * (NY // 2) - 8, count_y // 2)

    def smooth1(x):
        m = plane_mask(my1, i * (NX // 2) + x - 5, count_x // 2)
        f, around_f = around(F1, x)
        for k in range(n1):
            P1[x, k] = (C1 * f[k] + C2 * around_f[k]) * m

    each(1, 13, smooth1, 4)

    def fill0(x):
        if 4 <= x < 12:
            v = src[x - 4]
        elif x < 4:
            v = jnp.where(odd_i, ra[x], rb[x] * far_x)
        else:
            v = jnp.where(odd_i, rb[x - 12] * far_x, ra[x - 12])
        a, b = rs1[x % 8], rs2[x % 8]
        h = 4 * (x // 8)
        lo = jnp.where(odd_j, a[h : h + 4], b[h : h + 4]) * low_j
        hi = jnp.where(odd_j, b[h : h + 4], a[h : h + 4]) * high_j
        for k in range(nz):
            s = slice(k * LANES, (k + 1) * LANES)
            F0[x, k, 0:4, :] = lo[:, s]
            F0[x, k, 4:20, :] = v[:, s]
            F0[x, k, 20:24, :] = hi[:, s]

    for x in range(16):
        fill0(x)
    my0 = row_mask(24, j * NY - 4, count_y)

    def smooth0(x):
        m = plane_mask(my0, i * NX + x - 4, count_x)
        f, around_f = around(F0, x)
        for k in range(nz):
            P0[x, k] = (C1 * f[k] + C2 * around_f[k]) * m

    each(1, 15, smooth0, 4)


def ascent(dims, u3, f2, r2c1, r2c2, r2e, F0, P0, F1, P1, press_out, resid_out, F2, T2, W2, X2, T1, V1, X1, T0, V0, X0, press, resid, done):
    leaves, subs = dims
    i, j, odd_i, odd_j, far_i, far_j = place(leaves, subs)
    count_x, count_y = leaves * NX, subs * NY
    nz = F0.shape[1]
    n1, n2, n3 = nz // 2, nz // 4, nz // 8
    zero = jnp.zeros((24, LANES), f32)

    c, chips = i // 2, leaves // 2
    odd_c = c % 2 == 1
    far_c = jnp.where(jnp.where(odd_c, c < chips - 1, c > 0), 1.0, 0.0).astype(f32)
    far_e = jnp.where(jnp.where(odd_i, c < chips - 2, c > 1), 1.0, 0.0).astype(f32)
    base = jnp.where(odd_i, 2, 0)
    for k in range(n2):
        s = slice(k * LANES, (k + 1) * LANES)
        e = r2e[0, :, s] * far_e
        F2[0, k] = e
        F2[13, k] = e
        for x in range(4):
            a, b = r2c1[x, :, s], r2c2[x, :, s] * far_c
            F2[x + 1, k] = jnp.where(odd_c, a, b)
            F2[x + 5, k] = f2[x, :, s]
            F2[x + 9, k] = jnp.where(odd_c, b, a)
    m2 = jnp.ones((16, LANES), f32)
    for x in range(5):
        prolonged(T2.at[x], [u3[x, :, k * LANES : (k + 1) * LANES] for k in range(n3)], 8)
    for w in range(10):
        m = plane_mask(m2, 2 * i + w - 4, 2 * leaves)
        f, around_f = around(F2, base + w + 1, True)
        for k in range(n2):
            W2[w, k] = (C1 * f[k] + C2 * around_f[k] + T2[w // 2, k // 2]) * m

    def sweep2(old, new, lo, hi):
        for w in range(lo, hi):
            m = plane_mask(m2, 2 * i + w - 4, 2 * leaves)
            u, around_u = around(old, w, True)
            for k in range(n2):
                new[w, k] = (C0 * u[k] + D * (F2[base + w + 1, k] + around_u[k])) * m

    sweep2(W2, X2, 1, 9)
    sweep2(X2, W2, 2, 8)

    for c in range(6):
        for k in range(n2):
            T1[c, k] = zero
    my1 = row_mask(24, j * (NY // 2) - 8, count_y // 2)

    for c in range(6):
        cols = [pltpu.roll(W2[c + 2, k], (18 - 4 * j) % 16, 0)[0:8] for k in range(n2)]
        prolonged(T1.at[c], cols, 8, 4)
    for c in range(6):
        for p in (0, 1):
            x = 2 * c + p + 1
            m = plane_mask(my1, i * (NX // 2) + x - 5, count_x // 2)
            for k in range(n1):
                V1[x, k] = P1[x, k] + T1[c, k // 2] * m

    def sweep1(old, new, lo, hi):
        def body(x):
            m = plane_mask(my1, i * (NX // 2) + x - 5, count_x // 2)
            u, around_u = around(old, x)
            for k in range(n1):
                new[x, k] = (C0 * u[k] + D * (F1[x, k] + around_u[k])) * m

        each(lo, hi, body, (hi - lo) // 2)

    sweep1(V1, X1, 2, 12)
    sweep1(X1, V1, 3, 11)


    my0 = row_mask(24, j * NY - 4, count_y)

    def start0(c):
        prolonged(T0.at[c], [V1[c + 3, k, 6:18, :] for k in range(n1)], 12)

    each(0, 8, start0, 4)

    def smooth0(x):
        m = plane_mask(my0, i * NX + x - 4, count_x)
        for k in range(nz):
            V0[x, k] = P0[x, k] + T0[x // 2, k // 2] * m

    each(1, 15, smooth0, 4)

    def sweep0(old, new, lo, hi):
        def body(x):
            m = plane_mask(my0, i * NX + x - 4, count_x)
            u, around_u = around(old, x)
            for k in range(nz):
                new[x, k] = (C0 * u[k] + D * (F0[x, k] + around_u[k])) * m

        each(lo, hi, body, 4)

    sweep0(V0, X0, 2, 14)
    sweep0(X0, V0, 3, 13)

    def put(out, x, cols):
        for k, v in enumerate(regroup(cols)):
            out[x, :, k * LANES : (k + 1) * LANES] = v

    def rest(x):
        u = [V0[x + 4, k, 4:20, :] for k in range(nz)]
        before, after = along_z(u)
        res = []
        for k in range(nz):
            near = V0[x + 5, k, 4:20, :] + V0[x + 3, k, 4:20, :] + (V0[x + 4, k, 5:21, :] + V0[x + 4, k, 3:19, :])
            res.append(F0[x + 4, k, 4:20, :] - 6.0 * u[k] + (near + (before[k] + after[k])))
        put(resid, x, res)

    def away(t, a, b, s):
        return pltpu.make_async_copy(a.at[pl.ds(4 * s, 4)], b.at[pl.ds(4 * s, 4)], done.at[t, s])

    def give(s):
        for x in range(4):
            put(press, 4 * s + x, [V0[4 * s + x + 4, k, 4:20, :] for k in range(nz)])
        away(0, press, press_out, s).start()

    def give_rest(s):
        for x in range(4):
            rest(4 * s + x)
        away(1, resid, resid_out, s).start()

    each(0, NX // 4, give)
    each(0, NX // 4, give_rest)
    for s in range(NX // 4):
        away(0, press, press_out, s).wait()
        away(1, resid, resid_out, s).wait()


def call(kernel, outs, scratch, *args, away=False, mib=4, us=0.0):
    cost = pl.CostEstimate(flops=0, transcendentals=0, bytes_accessed=int(us * 3.6e6)) if us else None
    return pl.pallas_call(
        kernel,
        out_shape=[jax.ShapeDtypeStruct(s, f32) for s in outs],
        out_specs=[pl.BlockSpec(memory_space=pltpu.HBM) if away else pl.BlockSpec() for _ in outs],
        scratch_shapes=[pltpu.VMEM(s, f32) if isinstance(s, tuple) else s for s in scratch],
        compiler_params=pltpu.CompilerParams(vmem_limit_bytes=mib * 1024 * 1024),
        cost_estimate=cost,
    )(*args)


def swaps(leaves, subs):
    def table(partner):
        return [(i * subs + j, (lambda t: t[0] * subs + t[1])(partner(i, j))) for i in range(leaves) for j in range(subs)]

    def odd(n):
        return ((n + 1) ^ 1) - 1

    def inner(n, count):
        return 0 <= n < count

    a = table(lambda i, j: (i ^ 1, j))
    b = table(lambda i, j: (odd(i), j) if inner(odd(i), leaves) else (i, j ^ 1))
    s1 = table(lambda i, j: (i, j ^ 1))
    s2 = table(lambda i, j: (i, odd(j)) if inner(odd(j), subs) else (i ^ 1, j))
    c1 = table(lambda i, j: (i ^ 2, j))
    c2 = table(lambda i, j: (2 * odd(i // 2) + i % 2, j) if inner(odd(i // 2), leaves // 2) else (i ^ 1, j))

    def two_on(i):
        t = 2 * (i // 2 + (2 if i % 2 else -2)) + 1 - i % 2
        return t if inner(t, leaves) else None

    e = table(lambda i, j: (two_on(i), j) if two_on(i) is not None else (i ^ 2, j))
    return a, b, s1, s2, c1, c2, e


def shards(dims, volume_fraction, interface_mask):
    leaves, subs = dims
    depth = volume_fraction.shape[2]
    nz = depth // LANES
    pa, pb, ps1, ps2, pc1, pc2, pe = swaps(leaves, subs)
    move = lambda v, table: lax.ppermute(v, AXES, table)
    n1, n2, n3 = nz // 2, nz // 4, nz // 8

    plane, rows = (1, NY, depth), (NX, depth)
    to_a, to_b, to_1, to_2 = call(functools.partial(edges, dims), [plane, plane, rows, rows], [], volume_fraction)
    halos = move(to_a, pa), move(to_b, pb), move(to_1, ps1), move(to_2, ps2)
    shape = (NX, nz, NY, LANES)
    heights, slope = call(columns, [shape, shape], [], volume_fraction, us=1.5)
    (slope,) = call(masked, [shape], [], slope, interface_mask)
    (src,) = call(functools.partial(source, dims), [(NX, NY, depth)], [], heights, slope, *halos)
    big, m2b, own2 = call(
        functools.partial(descent, dims),
        [(8, NY, depth)] + [(2, 8, depth // 4)] * 2,
        [
            (6, 8, depth // 4),
            (16, nz, 24, LANES),
            (16, nz, 24, LANES),
            (8, nz, 24, LANES),
            (14, n1, 16, LANES),
            (14, n1, 16, LANES),
            (6, n1, 16, LANES),
        ],
        src,
        mib=10,
    )
    r2b, ra = move(m2b, pb), move(big, pa)
    out, to_b = call(
        functools.partial(middle, dims), [(2 * subs, 2, 8, depth // 4), (7, NY, depth)], [], own2, r2b, src, big, ra
    )
    rb = move(to_b, pb)
    group = [list(range(k, k + 2 * subs)) for k in range(0, leaves * subs, 2 * subs)]
    got = lax.all_to_all(out, AXES, 0, 0, axis_index_groups=group)
    got, rb = lax.optimization_barrier((got, rb))
    far = move(rb[4:7], pa)
    chips = leaves // 2
    f2, edge, out = call(
        functools.partial(chip2, dims),
        [(4, 16, depth // 4), (1, 16, depth // 4), (chips, 4, 8, depth // 8)],
        [(10, n2, 16, LANES), (10, n2, 16, LANES), (4, n2, 16, LANES)],
        got,
    )
    f1x, s1, s2 = call(
        functools.partial(rows_out, dims),
        [(14, 16, depth // 2), (15, 8, depth), (15, 8, depth)],
        [],
        src,
        big,
        ra,
        rb,
        far,
    )
    out, s1, s2 = lax.optimization_barrier((out, s1, s2))
    rs1, rs2 = move(s1, ps1), move(s2, ps2)
    group = [[(2 * c + k) * subs + s for c in range(chips)] for k in (0, 1) for s in range(subs)]
    got = lax.all_to_all(out, AXES, 0, 0, axis_index_groups=group)
    r2c1, r2c2, r2e = move(f2, pc1), move(f2, pc2), move(edge, pe)
    shape0, shape1 = (16, nz, 24, LANES), (14, n1, 24, LANES)
    F0, P0, F1, P1 = call(functools.partial(ready, dims), [shape0, shape0, shape1, shape1], [], src, ra, rb, f1x, rs1, rs2, mib=10)
    (u3,) = call(functools.partial(coarsest, dims), [(5, 8, depth // 8)], [(leaves + 18, 8, LANES)], got)
    return call(
        functools.partial(ascent, dims),
        [(NX, NY, depth), (NX, NY, depth)],
        [
            (14, n2, 16, LANES),
            (5, n3, 16, LANES),
            (10, n2, 16, LANES),
            (10, n2, 16, LANES),
            (6, n2, 24, LANES),
            shape1,
            shape1,
            (8, n1, 24, LANES),
            shape0,
            shape0,
            (NX, NY, depth),
            (NX, NY, depth),
            pltpu.SemaphoreType.DMA((2, NX // 4)),
        ],
        u3,
        f2,
        r2c1,
        r2c2,
        r2e,
        F0,
        P0,
        F1,
        P1,
        away=True,
        mib=16,
    )


def solution(mesh):
    spec = P("leaf", "sub", None)
    dims = (mesh.shape["leaf"], mesh.shape["sub"])
    body = functools.partial(shards, dims)
    return jax.shard_map(body, mesh=mesh, in_specs=(spec, spec), out_specs=(spec, spec), check_vma=False)
```

```python
import functools

import jax
import jax.numpy as jnp
from jax import lax
from jax.experimental import pallas as pl
from jax.experimental.pallas import tpu as pltpu
from jax.sharding import PartitionSpec as P

D = 0.8 / 6.0
C1 = 2.0 * D - 6.0 * D * D
C2 = D * D
C0 = 1.0 - 6.0 * D
NX, NY = 8, 16
LANES = 128
AXES = ("leaf", "sub")
f32 = jnp.float32


def lanes(rows):
    return lax.broadcasted_iota(jnp.int32, (rows, LANES), 1)


def rows_of(rows):
    return lax.broadcasted_iota(jnp.int32, (rows, LANES), 0)


def lane_before(col):
    lane = lanes(col.shape[0])
    wrapped = jnp.where(lane == 0, 0.0, pltpu.roll(col, 9, 1))
    return jnp.where(lane < 8, wrapped, pltpu.roll(col, 8, 1))


def lane_after(col):
    lane = lanes(col.shape[0])
    wrapped = jnp.where(lane == LANES - 1, 0.0, pltpu.roll(col, LANES - 9, 1))
    return jnp.where(lane >= LANES - 8, wrapped, pltpu.roll(col, LANES - 8, 1))


def along_z(cols):
    return [lane_before(cols[-1])] + cols[:-1], cols[1:] + [lane_after(cols[0])]


def regroup(cols):
    cols = list(cols)
    lane = lanes(cols[0].shape[0])
    for s in (1, 2, 4):
        low, beside = (lane & s) == 0, lane ^ s
        for a in range(8):
            b = a | s
            if a != b:
                moved = jnp.where(low, cols[b], cols[a])
                moved = jnp.take_along_axis(moved, beside, axis=1, mode="promise_in_bounds")
                cols[a], cols[b] = jnp.where(low, cols[a], moved), jnp.where(low, moved, cols[b])
    return cols


def around(ref, x, whole=False):
    n, rows = ref.shape[1], ref.shape[2]
    cols = [ref[x, k] for k in range(n)]
    before, after = along_z(cols)
    out = []
    for k, c in enumerate(cols):
        up, down = pltpu.roll(c, rows - 1, 0), pltpu.roll(c, 1, 0)
        if whole:
            row = rows_of(rows)
            up, down = jnp.where(row == rows - 1, 0.0, up), jnp.where(row == 0, 0.0, down)
        out.append((ref[x + 1, k] + ref[x - 1, k]) + (up + down) + (before[k] + after[k]))
    return cols, out


def restricted(tmp, rows):
    sums = [tmp[k, pl.ds(0, rows, 2), :] + tmp[k, pl.ds(1, rows, 2), :] for k in range(tmp.shape[0])]
    return [0.5 * (sums[2 * m] + sums[2 * m + 1]) for m in range(tmp.shape[0] // 2)]


def prolonged(tmp, cols, rows, at=0):
    for m, c in enumerate(cols):
        tmp[m, pl.ds(at, rows, 2), :] = c
        tmp[m, pl.ds(at + 1, rows, 2), :] = c


def inside(pos, count):
    return jnp.logical_and(pos >= 0, pos < count)


def row_mask(rows, start, count):
    pos = rows_of(rows) + start
    return jnp.where(inside(pos, count), 1.0, 0.0).astype(f32)


def plane_mask(mask, x, count):
    return mask * jnp.where(inside(x, count), 1.0, 0.0).astype(f32)


def each(lo, hi, body, together=1):
    steps = (hi - lo) // together

    def step(s, carry):
        for t in range(together):
            body(lo + s * together + t)
        return carry

    lax.fori_loop(0, steps, step, 0)
    for x in range(lo + steps * together, hi):
        body(x)


def taps(cols):
    n = len(cols)
    more = [lane_before(c) for c in cols[-3:]] + cols + [lane_after(c) for c in cols[:3]]
    out = [((more[k] + more[k + 1]) + (more[k + 2] + more[k + 3])) + ((more[k + 4] + more[k + 5]) + more[k + 6]) for k in range(n)]
    return out, more[2 : n + 2], more[4 : n + 4]


def split(value):
    return regroup(value[:, k * LANES : (k + 1) * LANES] for k in range(value.shape[1] // LANES))


def place(leaves, subs):
    i, j = lax.axis_index("leaf"), lax.axis_index("sub")
    odd_i, odd_j = i % 2 == 1, j % 2 == 1
    far_i = jnp.where(odd_i, i < leaves - 1, i > 0)
    far_j = jnp.where(odd_j, j < subs - 1, j > 0)
    return i, j, odd_i, odd_j, far_i, far_j


def edges(dims, vf, to_a, to_b, to_1, to_2):
    _, _, odd_i, odd_j, _, _ = place(*dims)
    to_a[0] = vf[jnp.where(odd_i, 0, NX - 1)]
    to_b[0] = vf[jnp.where(odd_i, NX - 1, 0)]
    first = jnp.concatenate([vf[x, 0:1, :] for x in range(NX)], axis=0)
    last = jnp.concatenate([vf[x, NY - 1 : NY, :] for x in range(NX)], axis=0)
    to_1[...] = jnp.where(odd_j, first, last)
    to_2[...] = jnp.where(odd_j, last, first)


def columns(vf, H, G):
    nz = vf.shape[2] // LANES

    def level0(x):
        h, before, after = taps(split(vf[x]))
        for k in range(nz):
            H[x, k] = h[k]
            G[x, k] = 0.5 * (after[k] - before[k])

    each(0, NX, level0, 4)


def masked(G, mask, out):
    def body(x):
        m = split(mask[x].astype(f32))
        for k in range(len(m)):
            out[x, k] = G[x, k] * m[k]

    each(0, NX, body, 8)


def source(dims, H, G, ra, rb, rs1, rs2, src):
    _, _, odd_i, odd_j, far_i, far_j = place(*dims)
    nz = H.shape[1]
    far_x = jnp.where(far_i, 1.0, 0.0).astype(f32)
    far_y = jnp.where(far_j, 1.0, 0.0).astype(f32)
    ha, _, _ = taps(split(ra[0]))
    hb, _, _ = taps(split(rb[0]))
    hs1, _, _ = taps(split(rs1[...]))
    hs2, _, _ = taps(split(rs2[...]))
    row = rows_of(NY)
    for k in range(nz):
        b = hb[k] * far_x
        below, above = jnp.where(odd_i, ha[k], b), jnp.where(odd_i, b, ha[k])
        low = jnp.where(odd_j, hs1[k], hs2[k] * far_y)
        high = jnp.where(odd_j, hs2[k] * far_y, hs1[k])
        for x in range(NX):
            h = H[x, k]
            up = jnp.where(row == NY - 1, high[x : x + 1, :], pltpu.roll(h, NY - 1, 0))
            down = jnp.where(row == 0, low[x : x + 1, :], pltpu.roll(h, 1, 0))
            ahead = H[x + 1, k] if x < NX - 1 else above
            behind = H[x - 1, k] if x > 0 else below
            sx, sy = 0.5 * (ahead - behind), 0.5 * (up - down)
            bend = ahead - 2.0 * h + behind + (up - 2.0 * h + down)
            inv = lax.rsqrt(1.0 + sx * sx + sy * sy)
            src[x, :, k * LANES : (k + 1) * LANES] = G[x, k] * (bend * (inv * inv * inv))


def descent(dims, src, big, m2b, own2, F1c, F0, U0, T0, F1, U1, T1):
    leaves, subs = dims
    i, j, odd_i, odd_j, far_i, far_j = place(leaves, subs)
    nz = src.shape[2] // LANES
    zero = jnp.zeros((16, LANES), f32)
    zero24 = jnp.zeros((24, LANES), f32)
    for x in range(16):
        for k in range(nz):
            if 4 <= x < 12:
                own = src[x - 4, :, k * LANES : (k + 1) * LANES]
                F0[x, k] = jnp.concatenate([zero[0:4], own, zero[0:4]], axis=0)
            else:
                F0[x, k] = zero24

    count_x, count_y = leaves * NX, subs * NY
    my0 = row_mask(24, j * NY - 4, count_y)
    for x in (1, 2, 13, 14):
        for k in range(nz):
            U0[x, k] = zero24

    def smooth0(x):
        m = plane_mask(my0, i * NX + x - 4, count_x)
        f, around_f = around(F0, x)
        for k in range(nz):
            U0[x, k] = (C1 * f[k] + C2 * around_f[k]) * m

    each(3, 13, smooth0, 10)

    for x in range(0, 14):
        if x < 4 or x >= 10:
            for k in range(nz // 2):
                F1[x, k] = zero

    def restrict0(c):
        total = [zero24] * nz
        for p in (0, 1):
            x = 2 * c + p
            m = plane_mask(my0, i * NX + x - 4, count_x)
            u, around_u = around(U0, x)
            total = [total[k] + (F0[x, k] - 6.0 * u[k] + around_u[k]) * m for k in range(nz)]
        for k in range(nz):
            T0[c, k, 0:24, :] = total[k]
        for k, v in enumerate(restricted(T0.at[c], 12)):
            F1[c + 3, k] = jnp.concatenate([zero[0:2], v, zero[0:2]], axis=0)

    each(1, 7, restrict0, 6)

    n1 = nz // 2
    my1 = row_mask(16, j * (NY // 2) - 4, count_y // 2)
    for x in (0, 1, 2, 11, 12, 13):
        for k in range(n1):
            U1[x, k] = zero

    def smooth1(x):
        m = plane_mask(my1, i * (NX // 2) + x - 5, count_x // 2)
        f, around_f = around(F1, x)
        for k in range(n1):
            U1[x, k] = (C1 * f[k] + C2 * around_f[k]) * m

    each(3, 11, smooth1, 8)

    def restrict1(c):
        total = [zero] * n1
        for p in (0, 1):
            x = 2 * c + 1 + p
            m = plane_mask(my1, i * (NX // 2) + x - 5, count_x // 2)
            u, around_u = around(U1, x)
            total = [total[k] + (F1[x, k] - 6.0 * u[k] + around_u[k]) * m for k in range(n1)]
        for k in range(n1):
            T1[c, k] = total[k]
        for k, v in enumerate(restricted(T1.at[c], 8)):
            F1c[c, :, k * LANES : (k + 1) * LANES] = v

    each(0, 6, restrict1, 6)

    at = jnp.where(odd_i, 0, 4)
    for x in (0, 1):
        big[7, 0:8, x * 2 * LANES : (x + 1) * 2 * LANES] = F1c[at + x]
    m2b[...] = F1c[pl.ds(4 - at, 2)]
    own2[...] = F1c[2:4]
    big[0:4] = src[pl.ds(at, 4)]
    for p in range(3):
        for k in range(n1):
            for h in (0, 1):
                big[4 + p, :, (h * n1 + k) * LANES : (h * n1 + k + 1) * LANES] = F1[4 + p + 3 * h, k]


def half_planes(ref, p):
    n = ref.shape[2] // 2
    return ref[4 + p % 3, :, (p // 3) * n : (p // 3 + 1) * n]


def middle(dims, own2, r2b, src, big, ra, out, to_b):
    _, _, odd_i, _, far_i, _ = place(*dims)
    n = src.shape[2] // 2
    for x in (0, 1):
        v = own2[x] + ra[7, 0:8, x * 2 * LANES : (x + 1) * 2 * LANES] + jnp.where(far_i, r2b[x], 0.0)
        for k in range(out.shape[0]):
            out[k, x] = v
    to_b[0:4] = src[pl.ds(jnp.where(odd_i, 4, 0), 4)]
    more = {
        0: jnp.where(odd_i, half_planes(ra, 4), 0.0),
        1: jnp.where(odd_i, half_planes(ra, 5), 0.0),
        4: jnp.where(odd_i, 0.0, half_planes(ra, 0)),
        5: jnp.where(odd_i, 0.0, half_planes(ra, 1)),
    }
    for p in range(6):
        v = half_planes(big, p)
        to_b[4 + p % 3, :, (p // 3) * n : (p // 3 + 1) * n] = v + more[p] if p in more else v


def chip2(dims, got, f2, edge, out, F2, U2, T2):
    leaves, subs = dims
    i = lax.axis_index("leaf")
    odd_i, c = i % 2 == 1, i // 2
    n2 = f2.shape[2] // LANES
    row = rows_of(8)
    zero = jnp.zeros((16, LANES), f32)
    for x in (0, 1, 2, 7, 8, 9):
        for k in range(n2):
            F2[x, k] = zero
    for x in (0, 1, 8, 9):
        for k in range(n2):
            U2[x, k] = zero
    for x in range(4):
        for k in range(n2):
            s = slice(k * LANES, (k + 1) * LANES)
            t = [got[4 * (x // 2) + j, x % 2, :, s] for j in range(4)]
            one, two = pltpu.roll(t[1], 2, 0), pltpu.roll(t[2], 6, 0)
            lo = jnp.where(row < 6, pltpu.roll(t[0], 6, 0), two) + jnp.where(row >= 2, one, 0.0)
            hi = jnp.where(row >= 2, pltpu.roll(t[3], 2, 0), one) + jnp.where(row < 6, two, 0.0)
            f2[x, 0:8, s] = lo
            f2[x, 8:16, s] = hi
            F2[x + 3, k, 0:8, :] = lo
            F2[x + 3, k, 8:16, :] = hi
    edge[0] = f2[jnp.where(odd_i, 3, 0)]
    m2 = jnp.ones((16, LANES), f32)
    for x in range(2, 8):
        m = plane_mask(m2, 4 * c + x - 3, 2 * leaves)
        f, around_f = around(F2, x, True)
        for k in range(n2):
            U2[x, k] = (C1 * f[k] + C2 * around_f[k]) * m
    for q in range(4):
        total = [zero] * n2
        for x in (2 * q + 1, 2 * q + 2):
            m = plane_mask(m2, 4 * c + x - 3, 2 * leaves)
            u, around_u = around(U2, x, True)
            total = [total[k] + (F2[x, k] - 6.0 * u[k] + around_u[k]) * m for k in range(n2)]
        for k in range(n2):
            T2[q, k] = total[k]
    for q in range(4):
        for k, v in enumerate(restricted(T2.at[q], 8)):
            for t in range(out.shape[0]):
                out[t, q, :, k * LANES : (k + 1) * LANES] = in_order(v)


def rows_out(dims, src, big, ra, rb, far, f1x, s1, s2):
    _, _, odd_i, odd_j, far_i, _ = place(*dims)
    i = lax.axis_index("leaf")
    n = src.shape[2] // 2
    a = [half_planes(ra, p) for p in range(6)]
    b = [jnp.where(far_i, half_planes(rb, p), 0.0) for p in range(6)]
    before = [jnp.where(odd_i, a[p], b[p]) for p in range(6)]
    after = [jnp.where(odd_i, b[p], a[p]) for p in range(6)]
    far_two = jnp.where(odd_i, i > 1, i < dims[0] - 2)
    d = [jnp.where(far_two, far[p % 3, :, (p // 3) * n : (p // 3 + 1) * n], 0.0) for p in (0, 1, 4, 5)]
    before2 = [jnp.where(odd_i, d[2 + h], 0.0) for h in (0, 1)]
    after2 = [jnp.where(odd_i, 0.0, d[h]) for h in (0, 1)]
    own = [half_planes(big, p) for p in range(6)]
    planes = {}

    def add(x, v):
        planes[x] = planes[x] + v if x in planes else v

    for p in range(6):
        add(p - 1, own[p])
        add(p - 5, before[p])
        add(p + 3, after[p])
    for h in (0, 1):
        add(-5 + h, before2[h])
        add(7 + h, after2[h])
    for x in range(14):
        f1x[x] = planes[x - 5]

    def fine(x):
        if 4 <= x < 12:
            return src[x - 4]
        if x < 4:
            return jnp.where(odd_i, ra[x], jnp.where(far_i, rb[x], 0.0))
        return jnp.where(odd_i, jnp.where(far_i, rb[x - 12], 0.0), ra[x - 12])

    for x in range(8):
        u, v = fine(x), fine(x + 8)
        for out, up in ((s1, odd_j == False), (s2, odd_j)):
            out[x] = jnp.concatenate([jnp.where(up, u[12:16], u[0:4]), jnp.where(up, v[12:16], v[0:4])], axis=0)
    for x in range(14):
        v = planes[x - 5]
        s = slice((x // 7) * n, (x // 7 + 1) * n)
        last, first = v[5:13], v[3:11]
        s1[8 + x % 7, :, s] = jnp.where(odd_j, first, last)
        s2[8 + x % 7, :, s] = jnp.where(odd_j, last, first)


def in_order(col):
    lane = lanes(col.shape[0])
    return jnp.take_along_axis(col, 8 * (lane % 16) + lane // 16, axis=1, mode="promise_in_bounds")


def as_kept(col):
    lane = lanes(col.shape[0])
    return jnp.take_along_axis(col, 16 * (lane % 8) + lane // 8, axis=1, mode="promise_in_bounds")


def coarsest(dims, got, out, G3):
    leaves = dims[0]
    chips = got.shape[0]
    i = lax.axis_index("leaf")
    zero = jnp.zeros((8, LANES), f32)
    for x in range(9):
        G3[x] = zero
        G3[leaves + 9 + x] = zero
    for c in range(chips):
        a, b = got[c, 1], got[c, 2]
        if c > 0:
            a = a + got[c - 1, 3]
        if c < chips - 1:
            b = b + got[c + 1, 0]
        G3[2 * c + 9], G3[2 * c + 10] = a, b
    lane, row = lanes(8), rows_of(8)
    ends = [lane == 0, lane == LANES - 1, row == 0, row == 7]
    f = [D * G3[i + w] for w in range(19)]
    keep = [jnp.where(inside(i + w - 9, leaves), 1.0, 0.0).astype(f32) for w in range(19)]
    u = list(f)
    for s in range(1, 8):
        new = list(u)
        for w in range(s, 19 - s):
            c = u[w]
            z = jnp.where(ends[0], 0.0, pltpu.roll(c, 1, 1)) + jnp.where(ends[1], 0.0, pltpu.roll(c, LANES - 1, 1))
            y = jnp.where(ends[2], 0.0, pltpu.roll(c, 1, 0)) + jnp.where(ends[3], 0.0, pltpu.roll(c, 7, 0))
            new[w] = (C0 * c + (f[w] + D * ((u[w + 1] + u[w - 1]) + (y + z)))) * keep[w]
        u = new
    for x in range(5):
        out[x] = as_kept(u[7 + x])


def ready(dims, src, ra, rb, f1x, rs1, rs2, F0, P0, F1, P1):
    leaves, subs = dims
    i, j, odd_i, odd_j, far_i, far_j = place(leaves, subs)
    count_x, count_y = leaves * NX, subs * NY
    nz = src.shape[2] // LANES
    n1 = nz // 2
    zero = jnp.zeros((24, LANES), f32)
    far_x = jnp.where(far_i, 1.0, 0.0).astype(f32)

    low_j = jnp.where(j > 0, 1.0, 0.0).astype(f32)
    high_j = jnp.where(j < subs - 1, 1.0, 0.0).astype(f32)

    def fill1(x):
        part, at = x // 7, 8 + x % 7
        for k in range(n1):
            s = slice(k * LANES, (k + 1) * LANES)
            F1[x, k] = zero
            F1[x, k, 4:20, :] = f1x[x, :, s]
            s = slice((part * n1 + k) * LANES, (part * n1 + k + 1) * LANES)
            lo = jnp.where(odd_j, rs1[at, :, s], rs2[at, :, s]) * low_j
            hi = jnp.where(odd_j, rs2[at, :, s], rs1[at, :, s]) * high_j
            F1[x, k, 1:9, :] = F1[x, k, 1:9, :] + lo
            F1[x, k, 15:23, :] = F1[x, k, 15:23, :] + hi

    for x in range(14):
        fill1(x)
    my1 = row_mask(24, j * (NY // 2) - 8, count_y // 2)

    def smooth1(x):
        m = plane_mask(my1, i * (NX // 2) + x - 5, count_x // 2)
        f, around_f = around(F1, x)
        for k in range(n1):
            P1[x, k] = (C1 * f[k] + C2 * around_f[k]) * m

    each(1, 13, smooth1, 12)

    def fill0(x):
        if 4 <= x < 12:
            v = src[x - 4]
        elif x < 4:
            v = jnp.where(odd_i, ra[x], rb[x] * far_x)
        else:
            v = jnp.where(odd_i, rb[x - 12] * far_x, ra[x - 12])
        a, b = rs1[x % 8], rs2[x % 8]
        h = 4 * (x // 8)
        lo = jnp.where(odd_j, a[h : h + 4], b[h : h + 4]) * low_j
        hi = jnp.where(odd_j, b[h : h + 4], a[h : h + 4]) * high_j
        for k in range(nz):
            s = slice(k * LANES, (k + 1) * LANES)
            F0[x, k] = jnp.concatenate([lo[:, s], v[:, s], hi[:, s]], axis=0)

    for x in range(16):
        fill0(x)
    my0 = row_mask(24, j * NY - 4, count_y)

    def smooth0(x):
        m = plane_mask(my0, i * NX + x - 4, count_x)
        f, around_f = around(F0, x)
        for k in range(nz):
            P0[x, k] = (C1 * f[k] + C2 * around_f[k]) * m

    each(1, 15, smooth0, 7)


def ascent(dims, u3, f2, r2c1, r2c2, r2e, F0, P0, F1, P1, press_out, resid_out, F2, T2, W2, X2, T1, V1, X1, T0, V0, X0, press, resid, done):
    leaves, subs = dims
    i, j, odd_i, odd_j, far_i, far_j = place(leaves, subs)
    count_x, count_y = leaves * NX, subs * NY
    nz = F0.shape[1]
    n1, n2, n3 = nz // 2, nz // 4, nz // 8
    zero = jnp.zeros((24, LANES), f32)

    c, chips = i // 2, leaves // 2
    odd_c = c % 2 == 1
    far_c = jnp.where(jnp.where(odd_c, c < chips - 1, c > 0), 1.0, 0.0).astype(f32)
    far_e = jnp.where(jnp.where(odd_i, c < chips - 2, c > 1), 1.0, 0.0).astype(f32)
    base = jnp.where(odd_i, 2, 0)
    for k in range(n2):
        s = slice(k * LANES, (k + 1) * LANES)
        e = r2e[0, :, s] * far_e
        F2[0, k] = e
        F2[13, k] = e
        for x in range(4):
            a, b = r2c1[x, :, s], r2c2[x, :, s] * far_c
            F2[x + 1, k] = jnp.where(odd_c, a, b)
            F2[x + 5, k] = f2[x, :, s]
            F2[x + 9, k] = jnp.where(odd_c, b, a)
    m2 = jnp.ones((16, LANES), f32)
    for x in range(5):
        prolonged(T2.at[x], [u3[x, :, k * LANES : (k + 1) * LANES] for k in range(n3)], 8)
    for w in range(10):
        m = plane_mask(m2, 2 * i + w - 4, 2 * leaves)
        f, around_f = around(F2, base + w + 1, True)
        for k in range(n2):
            W2[w, k] = (C1 * f[k] + C2 * around_f[k] + T2[w // 2, k // 2]) * m

    def sweep2(old, new, lo, hi):
        for w in range(lo, hi):
            m = plane_mask(m2, 2 * i + w - 4, 2 * leaves)
            u, around_u = around(old, w, True)
            for k in range(n2):
                new[w, k] = (C0 * u[k] + D * (F2[base + w + 1, k] + around_u[k])) * m

    sweep2(W2, X2, 1, 9)
    sweep2(X2, W2, 2, 8)

    for c in range(6):
        for k in range(n2):
            T1[c, k] = zero
    my1 = row_mask(24, j * (NY // 2) - 8, count_y // 2)

    for c in range(6):
        cols = [pltpu.roll(W2[c + 2, k], (18 - 4 * j) % 16, 0)[0:8] for k in range(n2)]
        prolonged(T1.at[c], cols, 8, 4)
    for c in range(6):
        for p in (0, 1):
            x = 2 * c + p + 1
            m = plane_mask(my1, i * (NX // 2) + x - 5, count_x // 2)
            for k in range(n1):
                V1[x, k] = P1[x, k] + T1[c, k // 2] * m

    def sweep1(old, new, lo, hi):
        def body(x):
            m = plane_mask(my1, i * (NX // 2) + x - 5, count_x // 2)
            u, around_u = around(old, x)
            for k in range(n1):
                new[x, k] = (C0 * u[k] + D * (F1[x, k] + around_u[k])) * m

        each(lo, hi, body, hi - lo)

    sweep1(V1, X1, 2, 12)
    sweep1(X1, V1, 3, 11)


    my0 = row_mask(24, j * NY - 4, count_y)

    def start0(c):
        prolonged(T0.at[c], [V1[c + 3, k, 6:18, :] for k in range(n1)], 12)

    each(0, 8, start0, 4)

    def smooth0(x):
        m = plane_mask(my0, i * NX + x - 4, count_x)
        for k in range(nz):
            V0[x, k] = P0[x, k] + T0[x // 2, k // 2, 0:24, :] * m

    each(1, 15, smooth0, 4)

    def sweep0(old, new, lo, hi):
        def body(x):
            m = plane_mask(my0, i * NX + x - 4, count_x)
            u, around_u = around(old, x)
            for k in range(nz):
                new[x, k] = (C0 * u[k] + D * (F0[x, k] + around_u[k])) * m

        each(lo, hi, body, 4)

    sweep0(V0, X0, 2, 14)
    sweep0(X0, V0, 3, 13)

    def put(out, x, cols):
        for k, v in enumerate(regroup(cols)):
            out[x, :, k * LANES : (k + 1) * LANES] = v

    def rest(x):
        u = [V0[x + 4, k, 4:20, :] for k in range(nz)]
        before, after = along_z(u)
        res = []
        for k in range(nz):
            near = V0[x + 5, k, 4:20, :] + V0[x + 3, k, 4:20, :] + (V0[x + 4, k, 5:21, :] + V0[x + 4, k, 3:19, :])
            res.append(F0[x + 4, k, 4:20, :] - 6.0 * u[k] + (near + (before[k] + after[k])))
        put(resid, x, res)

    def away(t, a, b, s):
        return pltpu.make_async_copy(a.at[pl.ds(4 * s, 4)], b.at[pl.ds(4 * s, 4)], done.at[t, s])

    def give(s):
        for x in range(4):
            put(press, 4 * s + x, [V0[4 * s + x + 4, k, 4:20, :] for k in range(nz)])
        away(0, press, press_out, s).start()

    def give_rest(s):
        for x in range(4):
            rest(4 * s + x)
        away(1, resid, resid_out, s).start()

    each(0, NX // 4, give)
    each(0, NX // 4, give_rest)
    for s in range(NX // 4):
        away(0, press, press_out, s).wait()
        away(1, resid, resid_out, s).wait()


def call(kernel, outs, scratch, *args, away=False, mib=4, us=0.0):
    cost = pl.CostEstimate(flops=0, transcendentals=0, bytes_accessed=int(us * 3.6e6)) if us else None
    return pl.pallas_call(
        kernel,
        out_shape=[jax.ShapeDtypeStruct(s, f32) for s in outs],
        out_specs=[pl.BlockSpec(memory_space=pltpu.HBM) if away else pl.BlockSpec() for _ in outs],
        scratch_shapes=[pltpu.VMEM(s, f32) if isinstance(s, tuple) else s for s in scratch],
        compiler_params=pltpu.CompilerParams(vmem_limit_bytes=mib * 1024 * 1024),
        cost_estimate=cost,
    )(*args)


def swaps(leaves, subs):
    def table(partner):
        return [(i * subs + j, (lambda t: t[0] * subs + t[1])(partner(i, j))) for i in range(leaves) for j in range(subs)]

    def odd(n):
        return ((n + 1) ^ 1) - 1

    def inner(n, count):
        return 0 <= n < count

    a = table(lambda i, j: (i ^ 1, j))
    b = table(lambda i, j: (odd(i), j) if inner(odd(i), leaves) else (i, j ^ 1))
    s1 = table(lambda i, j: (i, j ^ 1))
    s2 = table(lambda i, j: (i, odd(j)) if inner(odd(j), subs) else (i ^ 1, j))
    c1 = table(lambda i, j: (i ^ 2, j))
    c2 = table(lambda i, j: (2 * odd(i // 2) + i % 2, j) if inner(odd(i // 2), leaves // 2) else (i ^ 1, j))

    def two_on(i):
        t = 2 * (i // 2 + (2 if i % 2 else -2)) + 1 - i % 2
        return t if inner(t, leaves) else None

    e = table(lambda i, j: (two_on(i), j) if two_on(i) is not None else (i ^ 2, j))
    return a, b, s1, s2, c1, c2, e


def shards(dims, volume_fraction, interface_mask):
    leaves, subs = dims
    depth = volume_fraction.shape[2]
    nz = depth // LANES
    pa, pb, ps1, ps2, pc1, pc2, pe = swaps(leaves, subs)
    move = lambda v, table: lax.ppermute(v, AXES, table)
    n1, n2, n3 = nz // 2, nz // 4, nz // 8

    plane, rows = (1, NY, depth), (NX, depth)
    to_a, to_b, to_1, to_2 = call(functools.partial(edges, dims), [plane, plane, rows, rows], [], volume_fraction)
    halos = move(to_a, pa), move(to_b, pb), move(to_1, ps1), move(to_2, ps2)
    shape = (NX, nz, NY, LANES)
    heights, slope = call(columns, [shape, shape], [], volume_fraction, us=1.5)
    (slope,) = call(masked, [shape], [], slope, interface_mask)
    (src,) = call(functools.partial(source, dims), [(NX, NY, depth)], [], heights, slope, *halos)
    big, m2b, own2 = call(
        functools.partial(descent, dims),
        [(8, NY, depth)] + [(2, 8, depth // 4)] * 2,
        [
            (6, 8, depth // 4),
            (16, nz, 24, LANES),
            (16, nz, 24, LANES),
            (8, nz, 32, LANES),
            (14, n1, 16, LANES),
            (14, n1, 16, LANES),
            (6, n1, 16, LANES),
        ],
        src,
        mib=10,
    )
    r2b, ra = move(m2b, pb), move(big, pa)
    out, to_b = call(
        functools.partial(middle, dims), [(2 * subs, 2, 8, depth // 4), (7, NY, depth)], [], own2, r2b, src, big, ra
    )
    rb = move(to_b, pb)
    group = [list(range(k, k + 2 * subs)) for k in range(0, leaves * subs, 2 * subs)]
    got = lax.all_to_all(out, AXES, 0, 0, axis_index_groups=group)
    got, rb = lax.optimization_barrier((got, rb))
    far = move(rb[4:7], pa)
    chips = leaves // 2
    f2, edge, out = call(
        functools.partial(chip2, dims),
        [(4, 16, depth // 4), (1, 16, depth // 4), (chips, 4, 8, depth // 8)],
        [(10, n2, 16, LANES), (10, n2, 16, LANES), (4, n2, 16, LANES)],
        got,
    )
    f1x, s1, s2 = call(
        functools.partial(rows_out, dims),
        [(14, 16, depth // 2), (15, 8, depth), (15, 8, depth)],
        [],
        src,
        big,
        ra,
        rb,
        far,
    )
    out, s1, s2 = lax.optimization_barrier((out, s1, s2))
    rs1, rs2 = move(s1, ps1), move(s2, ps2)
    group = [[(2 * c + k) * subs + s for c in range(chips)] for k in (0, 1) for s in range(subs)]
    got = lax.all_to_all(out, AXES, 0, 0, axis_index_groups=group)
    r2c1, r2c2, r2e = move(f2, pc1), move(f2, pc2), move(edge, pe)
    shape0, shape1 = (16, nz, 24, LANES), (14, n1, 24, LANES)
    F0, P0, F1, P1 = call(functools.partial(ready, dims), [shape0, shape0, shape1, shape1], [], src, ra, rb, f1x, rs1, rs2, mib=10)
    (u3,) = call(functools.partial(coarsest, dims), [(5, 8, depth // 8)], [(leaves + 18, 8, LANES)], got)
    return call(
        functools.partial(ascent, dims),
        [(NX, NY, depth), (NX, NY, depth)],
        [
            (14, n2, 16, LANES),
            (5, n3, 16, LANES),
            (10, n2, 16, LANES),
            (10, n2, 16, LANES),
            (6, n2, 24, LANES),
            shape1,
            shape1,
            (8, n1, 32, LANES),
            shape0,
            shape0,
            (NX, NY, depth),
            (NX, NY, depth),
            pltpu.SemaphoreType.DMA((2, NX // 4)),
        ],
        u3,
        f2,
        r2c1,
        r2c2,
        r2e,
        F0,
        P0,
        F1,
        P1,
        away=True,
        mib=16,
    )


def solution(mesh):
    spec = P("leaf", "sub", None)
    dims = (mesh.shape["leaf"], mesh.shape["sub"])
    body = functools.partial(shards, dims)
    return jax.shard_map(body, mesh=mesh, in_specs=(spec, spec), out_specs=(spec, spec), check_vma=False)
```

```python
import functools

import jax
import jax.numpy as jnp
from jax import lax
from jax.experimental import pallas as pl
from jax.experimental.pallas import tpu as pltpu
from jax.sharding import PartitionSpec as P

D = 0.8 / 6.0
C1 = 2.0 * D - 6.0 * D * D
C2 = D * D
C0 = 1.0 - 6.0 * D
NX, NY = 8, 16
LANES = 128
AXES = ("leaf", "sub")
f32 = jnp.float32


def lanes(rows):
    return lax.broadcasted_iota(jnp.int32, (rows, LANES), 1)


def rows_of(rows):
    return lax.broadcasted_iota(jnp.int32, (rows, LANES), 0)


def lane_before(col):
    lane = lanes(col.shape[0])
    wrapped = jnp.where(lane == 0, 0.0, pltpu.roll(col, 9, 1))
    return jnp.where(lane < 8, wrapped, pltpu.roll(col, 8, 1))


def lane_after(col):
    lane = lanes(col.shape[0])
    wrapped = jnp.where(lane == LANES - 1, 0.0, pltpu.roll(col, LANES - 9, 1))
    return jnp.where(lane >= LANES - 8, wrapped, pltpu.roll(col, LANES - 8, 1))


def along_z(cols):
    return [lane_before(cols[-1])] + cols[:-1], cols[1:] + [lane_after(cols[0])]


def regroup(cols):
    cols = list(cols)
    lane = lanes(cols[0].shape[0])
    for s in (1, 2, 4):
        low, beside = (lane & s) == 0, lane ^ s
        for a in range(8):
            b = a | s
            if a != b:
                moved = jnp.where(low, cols[b], cols[a])
                moved = jnp.take_along_axis(moved, beside, axis=1, mode="promise_in_bounds")
                cols[a], cols[b] = jnp.where(low, cols[a], moved), jnp.where(low, moved, cols[b])
    return cols


def around(ref, x, whole=False):
    n, rows = ref.shape[1], ref.shape[2]
    cols = [ref[x, k] for k in range(n)]
    before, after = along_z(cols)
    out = []
    for k, c in enumerate(cols):
        up, down = pltpu.roll(c, rows - 1, 0), pltpu.roll(c, 1, 0)
        if whole:
            row = rows_of(rows)
            up, down = jnp.where(row == rows - 1, 0.0, up), jnp.where(row == 0, 0.0, down)
        out.append((ref[x + 1, k] + ref[x - 1, k]) + (up + down) + (before[k] + after[k]))
    return cols, out


def restricted(tmp, rows):
    sums = [tmp[k, pl.ds(0, rows, 2), :] + tmp[k, pl.ds(1, rows, 2), :] for k in range(tmp.shape[0])]
    return [0.5 * (sums[2 * m] + sums[2 * m + 1]) for m in range(tmp.shape[0] // 2)]


def prolonged(tmp, cols, rows, at=0):
    for m, c in enumerate(cols):
        tmp[m, pl.ds(at, rows, 2), :] = c
        tmp[m, pl.ds(at + 1, rows, 2), :] = c


def inside(pos, count):
    return jnp.logical_and(pos >= 0, pos < count)


def row_mask(rows, start, count):
    pos = rows_of(rows) + start
    return jnp.where(inside(pos, count), 1.0, 0.0).astype(f32)


def plane_mask(mask, x, count):
    return mask * jnp.where(inside(x, count), 1.0, 0.0).astype(f32)


def each(lo, hi, body, together=1):
    steps = (hi - lo) // together

    def step(s, carry):
        for t in range(together):
            body(lo + s * together + t)
        return carry

    lax.fori_loop(0, steps, step, 0)
    for x in range(lo + steps * together, hi):
        body(x)


def taps(cols):
    n = len(cols)
    more = [lane_before(c) for c in cols[-3:]] + cols + [lane_after(c) for c in cols[:3]]
    out = [((more[k] + more[k + 1]) + (more[k + 2] + more[k + 3])) + ((more[k + 4] + more[k + 5]) + more[k + 6]) for k in range(n)]
    return out, more[2 : n + 2], more[4 : n + 4]


def split(value):
    return regroup(value[:, k * LANES : (k + 1) * LANES] for k in range(value.shape[1] // LANES))


def place(leaves, subs):
    i, j = lax.axis_index("leaf"), lax.axis_index("sub")
    odd_i, odd_j = i % 2 == 1, j % 2 == 1
    far_i = jnp.where(odd_i, i < leaves - 1, i > 0)
    far_j = jnp.where(odd_j, j < subs - 1, j > 0)
    return i, j, odd_i, odd_j, far_i, far_j


def edges(dims, vf, to_a, to_b, to_1, to_2):
    _, _, odd_i, odd_j, _, _ = place(*dims)
    to_a[0] = vf[jnp.where(odd_i, 0, NX - 1)]
    to_b[0] = vf[jnp.where(odd_i, NX - 1, 0)]
    first = jnp.concatenate([vf[x, 0:1, :] for x in range(NX)], axis=0)
    last = jnp.concatenate([vf[x, NY - 1 : NY, :] for x in range(NX)], axis=0)
    to_1[...] = jnp.where(odd_j, first, last)
    to_2[...] = jnp.where(odd_j, last, first)


def columns(vf, H, G):
    nz = vf.shape[2] // LANES

    def level0(x):
        h, before, after = taps(split(vf[x]))
        for k in range(nz):
            H[x, k] = h[k]
            G[x, k] = 0.5 * (after[k] - before[k])

    each(0, NX, level0, 8)


def masked(G, mask, out):
    def body(x):
        m = split(mask[x].astype(f32))
        for k in range(len(m)):
            out[x, k] = G[x, k] * m[k]

    each(0, NX, body, 8)


def source(dims, H, G, ra, rb, rs1, rs2, src):
    _, _, odd_i, odd_j, far_i, far_j = place(*dims)
    nz = H.shape[1]
    far_x = jnp.where(far_i, 1.0, 0.0).astype(f32)
    far_y = jnp.where(far_j, 1.0, 0.0).astype(f32)
    ha, _, _ = taps(split(ra[0]))
    hb, _, _ = taps(split(rb[0]))
    hs1, _, _ = taps(split(rs1[...]))
    hs2, _, _ = taps(split(rs2[...]))
    row = rows_of(NY)
    for k in range(nz):
        b = hb[k] * far_x
        below, above = jnp.where(odd_i, ha[k], b), jnp.where(odd_i, b, ha[k])
        low = jnp.where(odd_j, hs1[k], hs2[k] * far_y)
        high = jnp.where(odd_j, hs2[k] * far_y, hs1[k])
        for x in range(NX):
            h = H[x, k]
            up = jnp.where(row == NY - 1, high[x : x + 1, :], pltpu.roll(h, NY - 1, 0))
            down = jnp.where(row == 0, low[x : x + 1, :], pltpu.roll(h, 1, 0))
            ahead = H[x + 1, k] if x < NX - 1 else above
            behind = H[x - 1, k] if x > 0 else below
            sx, sy = 0.5 * (ahead - behind), 0.5 * (up - down)
            bend = ahead - 2.0 * h + behind + (up - 2.0 * h + down)
            inv = lax.rsqrt(1.0 + sx * sx + sy * sy)
            src[x, :, k * LANES : (k + 1) * LANES] = G[x, k] * (bend * (inv * inv * inv))


def descent(dims, src, big, m2b, own2, F1c, F0, U0, T0, F1, U1, T1):
    leaves, subs = dims
    i, j, odd_i, odd_j, far_i, far_j = place(leaves, subs)
    nz = src.shape[2] // LANES
    zero = jnp.zeros((16, LANES), f32)
    zero24 = jnp.zeros((24, LANES), f32)
    for x in range(16):
        for k in range(nz):
            if 4 <= x < 12:
                own = src[x - 4, :, k * LANES : (k + 1) * LANES]
                F0[x, k] = jnp.concatenate([zero[0:4], own, zero[0:4]], axis=0)
            else:
                F0[x, k] = zero24

    count_x, count_y = leaves * NX, subs * NY
    my0 = row_mask(24, j * NY - 4, count_y)
    for x in (1, 2, 13, 14):
        for k in range(nz):
            U0[x, k] = zero24

    def smooth0(x):
        m = plane_mask(my0, i * NX + x - 4, count_x)
        f, around_f = around(F0, x)
        for k in range(nz):
            U0[x, k] = (C1 * f[k] + C2 * around_f[k]) * m

    each(3, 13, smooth0, 10)

    for x in range(0, 14):
        if x < 4 or x >= 10:
            for k in range(nz // 2):
                F1[x, k] = zero

    def restrict0(c):
        total = [zero24] * nz
        for p in (0, 1):
            x = 2 * c + p
            m = plane_mask(my0, i * NX + x - 4, count_x)
            u, around_u = around(U0, x)
            total = [total[k] + (F0[x, k] - 6.0 * u[k] + around_u[k]) * m for k in range(nz)]
        for k in range(nz):
            T0[c, k, 0:24, :] = total[k]
        for k, v in enumerate(restricted(T0.at[c], 12)):
            F1[c + 3, k] = jnp.concatenate([zero[0:2], v, zero[0:2]], axis=0)

    each(1, 7, restrict0, 6)

    n1 = nz // 2
    my1 = row_mask(16, j * (NY // 2) - 4, count_y // 2)
    for x in (0, 1, 2, 11, 12, 13):
        for k in range(n1):
            U1[x, k] = zero

    def smooth1(x):
        m = plane_mask(my1, i * (NX // 2) + x - 5, count_x // 2)
        f, around_f = around(F1, x)
        for k in range(n1):
            U1[x, k] = (C1 * f[k] + C2 * around_f[k]) * m

    each(3, 11, smooth1, 8)

    def restrict1(c):
        total = [zero] * n1
        for p in (0, 1):
            x = 2 * c + 1 + p
            m = plane_mask(my1, i * (NX // 2) + x - 5, count_x // 2)
            u, around_u = around(U1, x)
            total = [total[k] + (F1[x, k] - 6.0 * u[k] + around_u[k]) * m for k in range(n1)]
        for k in range(n1):
            T1[c, k] = total[k]
        for k, v in enumerate(restricted(T1.at[c], 8)):
            F1c[c, :, k * LANES : (k + 1) * LANES] = v

    each(0, 6, restrict1, 6)

    at = jnp.where(odd_i, 0, 4)
    for x in (0, 1):
        big[7, 0:8, x * 2 * LANES : (x + 1) * 2 * LANES] = F1c[at + x]
    m2b[...] = F1c[pl.ds(4 - at, 2)]
    own2[...] = F1c[2:4]
    big[0:4] = src[pl.ds(at, 4)]
    for p in range(3):
        for k in range(n1):
            for h in (0, 1):
                big[4 + p, :, (h * n1 + k) * LANES : (h * n1 + k + 1) * LANES] = F1[4 + p + 3 * h, k]


def half_planes(ref, p):
    n = ref.shape[2] // 2
    return ref[4 + p % 3, :, (p // 3) * n : (p // 3 + 1) * n]


def middle(dims, own2, r2b, src, big, ra, out, to_b):
    _, _, odd_i, _, far_i, _ = place(*dims)
    n = src.shape[2] // 2
    for x in (0, 1):
        v = own2[x] + ra[7, 0:8, x * 2 * LANES : (x + 1) * 2 * LANES] + jnp.where(far_i, r2b[x], 0.0)
        for k in range(out.shape[0]):
            out[k, x] = v
    to_b[0:4] = src[pl.ds(jnp.where(odd_i, 4, 0), 4)]
    more = {
        0: jnp.where(odd_i, half_planes(ra, 4), 0.0),
        1: jnp.where(odd_i, half_planes(ra, 5), 0.0),
        4: jnp.where(odd_i, 0.0, half_planes(ra, 0)),
        5: jnp.where(odd_i, 0.0, half_planes(ra, 1)),
    }
    for p in range(6):
        v = half_planes(big, p)
        to_b[4 + p % 3, :, (p // 3) * n : (p // 3 + 1) * n] = v + more[p] if p in more else v


def chip2(dims, got, f2, edge, out, F2, U2, T2):
    leaves, subs = dims
    i = lax.axis_index("leaf")
    odd_i, c = i % 2 == 1, i // 2
    n2 = f2.shape[2] // LANES
    row = rows_of(8)
    zero = jnp.zeros((16, LANES), f32)
    for x in (0, 1, 2, 7, 8, 9):
        for k in range(n2):
            F2[x, k] = zero
    for x in (0, 1, 8, 9):
        for k in range(n2):
            U2[x, k] = zero
    for x in range(4):
        for k in range(n2):
            s = slice(k * LANES, (k + 1) * LANES)
            t = [got[4 * (x // 2) + j, x % 2, :, s] for j in range(4)]
            one, two = pltpu.roll(t[1], 2, 0), pltpu.roll(t[2], 6, 0)
            lo = jnp.where(row < 6, pltpu.roll(t[0], 6, 0), two) + jnp.where(row >= 2, one, 0.0)
            hi = jnp.where(row >= 2, pltpu.roll(t[3], 2, 0), one) + jnp.where(row < 6, two, 0.0)
            f2[x, 0:8, s] = lo
            f2[x, 8:16, s] = hi
            F2[x + 3, k, 0:8, :] = lo
            F2[x + 3, k, 8:16, :] = hi
    edge[0] = f2[jnp.where(odd_i, 3, 0)]
    m2 = jnp.ones((16, LANES), f32)
    for x in range(2, 8):
        m = plane_mask(m2, 4 * c + x - 3, 2 * leaves)
        f, around_f = around(F2, x, True)
        for k in range(n2):
            U2[x, k] = (C1 * f[k] + C2 * around_f[k]) * m
    for q in range(4):
        total = [zero] * n2
        for x in (2 * q + 1, 2 * q + 2):
            m = plane_mask(m2, 4 * c + x - 3, 2 * leaves)
            u, around_u = around(U2, x, True)
            total = [total[k] + (F2[x, k] - 6.0 * u[k] + around_u[k]) * m for k in range(n2)]
        for k in range(n2):
            T2[q, k] = total[k]
    for q in range(4):
        for k, v in enumerate(restricted(T2.at[q], 8)):
            for t in range(out.shape[0]):
                out[t, q, :, k * LANES : (k + 1) * LANES] = in_order(v)


def rows_out(dims, src, big, ra, rb, far, f1x, s1, s2):
    _, _, odd_i, odd_j, far_i, _ = place(*dims)
    i = lax.axis_index("leaf")
    n = src.shape[2] // 2
    a = [half_planes(ra, p) for p in range(6)]
    b = [jnp.where(far_i, half_planes(rb, p), 0.0) for p in range(6)]
    before = [jnp.where(odd_i, a[p], b[p]) for p in range(6)]
    after = [jnp.where(odd_i, b[p], a[p]) for p in range(6)]
    far_two = jnp.where(odd_i, i > 1, i < dims[0] - 2)
    d = [jnp.where(far_two, far[p % 3, :, (p // 3) * n : (p // 3 + 1) * n], 0.0) for p in (0, 1, 4, 5)]
    before2 = [jnp.where(odd_i, d[2 + h], 0.0) for h in (0, 1)]
    after2 = [jnp.where(odd_i, 0.0, d[h]) for h in (0, 1)]
    own = [half_planes(big, p) for p in range(6)]
    planes = {}

    def add(x, v):
        planes[x] = planes[x] + v if x in planes else v

    for p in range(6):
        add(p - 1, own[p])
        add(p - 5, before[p])
        add(p + 3, after[p])
    for h in (0, 1):
        add(-5 + h, before2[h])
        add(7 + h, after2[h])
    for x in range(14):
        f1x[x] = planes[x - 5]

    def fine(x):
        if 4 <= x < 12:
            return src[x - 4]
        if x < 4:
            return jnp.where(odd_i, ra[x], jnp.where(far_i, rb[x], 0.0))
        return jnp.where(odd_i, jnp.where(far_i, rb[x - 12], 0.0), ra[x - 12])

    for x in range(8):
        u, v = fine(x), fine(x + 8)
        for out, up in ((s1, odd_j == False), (s2, odd_j)):
            out[x] = jnp.concatenate([jnp.where(up, u[12:16], u[0:4]), jnp.where(up, v[12:16], v[0:4])], axis=0)
    for x in range(14):
        v = planes[x - 5]
        s = slice((x // 7) * n, (x // 7 + 1) * n)
        last, first = v[5:13], v[3:11]
        s1[8 + x % 7, :, s] = jnp.where(odd_j, first, last)
        s2[8 + x % 7, :, s] = jnp.where(odd_j, last, first)


def in_order(col):
    lane = lanes(col.shape[0])
    return jnp.take_along_axis(col, 8 * (lane % 16) + lane // 16, axis=1, mode="promise_in_bounds")


def as_kept(col):
    lane = lanes(col.shape[0])
    return jnp.take_along_axis(col, 16 * (lane % 8) + lane // 8, axis=1, mode="promise_in_bounds")


def coarsest(dims, got, out, G3):
    leaves = dims[0]
    chips = got.shape[0]
    i = lax.axis_index("leaf")
    zero = jnp.zeros((8, LANES), f32)
    for x in range(9):
        G3[x] = zero
        G3[leaves + 9 + x] = zero
    for c in range(chips):
        a, b = got[c, 1], got[c, 2]
        if c > 0:
            a = a + got[c - 1, 3]
        if c < chips - 1:
            b = b + got[c + 1, 0]
        G3[2 * c + 9], G3[2 * c + 10] = a, b
    lane, row = lanes(8), rows_of(8)
    ends = [lane == 0, lane == LANES - 1, row == 0, row == 7]
    f = [D * G3[i + w] for w in range(19)]
    keep = [jnp.where(inside(i + w - 9, leaves), 1.0, 0.0).astype(f32) for w in range(19)]
    u = list(f)
    for s in range(1, 8):
        new = list(u)
        for w in range(s, 19 - s):
            c = u[w]
            z = jnp.where(ends[0], 0.0, pltpu.roll(c, 1, 1)) + jnp.where(ends[1], 0.0, pltpu.roll(c, LANES - 1, 1))
            y = jnp.where(ends[2], 0.0, pltpu.roll(c, 1, 0)) + jnp.where(ends[3], 0.0, pltpu.roll(c, 7, 0))
            new[w] = (C0 * c + (f[w] + D * ((u[w + 1] + u[w - 1]) + (y + z)))) * keep[w]
        u = new
    for x in range(5):
        out[x] = as_kept(u[7 + x])


def ready(dims, src, ra, rb, f1x, rs1, rs2, F0, P0, F1, P1):
    leaves, subs = dims
    i, j, odd_i, odd_j, far_i, far_j = place(leaves, subs)
    count_x, count_y = leaves * NX, subs * NY
    nz = src.shape[2] // LANES
    n1 = nz // 2
    zero = jnp.zeros((24, LANES), f32)
    far_x = jnp.where(far_i, 1.0, 0.0).astype(f32)

    low_j = jnp.where(j > 0, 1.0, 0.0).astype(f32)
    high_j = jnp.where(j < subs - 1, 1.0, 0.0).astype(f32)

    def fill1(x):
        part, at = x // 7, 8 + x % 7
        for k in range(n1):
            s = slice(k * LANES, (k + 1) * LANES)
            F1[x, k] = zero
            F1[x, k, 4:20, :] = f1x[x, :, s]
            s = slice((part * n1 + k) * LANES, (part * n1 + k + 1) * LANES)
            lo = jnp.where(odd_j, rs1[at, :, s], rs2[at, :, s]) * low_j
            hi = jnp.where(odd_j, rs2[at, :, s], rs1[at, :, s]) * high_j
            F1[x, k, 1:9, :] = F1[x, k, 1:9, :] + lo
            F1[x, k, 15:23, :] = F1[x, k, 15:23, :] + hi

    for x in range(14):
        fill1(x)
    my1 = row_mask(24, j * (NY // 2) - 8, count_y // 2)

    def smooth1(x):
        m = plane_mask(my1, i * (NX // 2) + x - 5, count_x // 2)
        f, around_f = around(F1, x)
        for k in range(n1):
            P1[x, k] = (C1 * f[k] + C2 * around_f[k]) * m

    each(1, 13, smooth1, 12)

    def fill0(x):
        if 4 <= x < 12:
            v = src[x - 4]
        elif x < 4:
            v = jnp.where(odd_i, ra[x], rb[x] * far_x)
        else:
            v = jnp.where(odd_i, rb[x - 12] * far_x, ra[x - 12])
        a, b = rs1[x % 8], rs2[x % 8]
        h = 4 * (x // 8)
        lo = jnp.where(odd_j, a[h : h + 4], b[h : h + 4]) * low_j
        hi = jnp.where(odd_j, b[h : h + 4], a[h : h + 4]) * high_j
        for k in range(nz):
            s = slice(k * LANES, (k + 1) * LANES)
            F0[x, k] = jnp.concatenate([lo[:, s], v[:, s], hi[:, s]], axis=0)

    for x in range(16):
        fill0(x)
    my0 = row_mask(24, j * NY - 4, count_y)

    def smooth0(x):
        m = plane_mask(my0, i * NX + x - 4, count_x)
        f, around_f = around(F0, x)
        for k in range(nz):
            P0[x, k] = (C1 * f[k] + C2 * around_f[k]) * m

    each(1, 15, smooth0, 7)


def ascent(dims, u3, f2, r2c1, r2c2, r2e, F0, P0, F1, P1, press_out, resid_out, F2, T2, W2, X2, T1, V1, X1, T0, V0, X0, press, resid, done):
    leaves, subs = dims
    i, j, odd_i, odd_j, far_i, far_j = place(leaves, subs)
    count_x, count_y = leaves * NX, subs * NY
    nz = F0.shape[1]
    n1, n2, n3 = nz // 2, nz // 4, nz // 8
    zero = jnp.zeros((24, LANES), f32)

    c, chips = i // 2, leaves // 2
    odd_c = c % 2 == 1
    far_c = jnp.where(jnp.where(odd_c, c < chips - 1, c > 0), 1.0, 0.0).astype(f32)
    far_e = jnp.where(jnp.where(odd_i, c < chips - 2, c > 1), 1.0, 0.0).astype(f32)
    base = jnp.where(odd_i, 2, 0)
    for k in range(n2):
        s = slice(k * LANES, (k + 1) * LANES)
        e = r2e[0, :, s] * far_e
        F2[0, k] = e
        F2[13, k] = e
        for x in range(4):
            a, b = r2c1[x, :, s], r2c2[x, :, s] * far_c
            F2[x + 1, k] = jnp.where(odd_c, a, b)
            F2[x + 5, k] = f2[x, :, s]
            F2[x + 9, k] = jnp.where(odd_c, b, a)
    m2 = jnp.ones((16, LANES), f32)
    for x in range(5):
        prolonged(T2.at[x], [u3[x, :, k * LANES : (k + 1) * LANES] for k in range(n3)], 8)
    for w in range(10):
        m = plane_mask(m2, 2 * i + w - 4, 2 * leaves)
        f, around_f = around(F2, base + w + 1, True)
        for k in range(n2):
            W2[w, k] = (C1 * f[k] + C2 * around_f[k] + T2[w // 2, k // 2]) * m

    def sweep2(old, new, lo, hi):
        for w in range(lo, hi):
            m = plane_mask(m2, 2 * i + w - 4, 2 * leaves)
            u, around_u = around(old, w, True)
            for k in range(n2):
                new[w, k] = (C0 * u[k] + D * (F2[base + w + 1, k] + around_u[k])) * m

    sweep2(W2, X2, 1, 9)
    sweep2(X2, W2, 2, 8)

    for c in range(6):
        for k in range(n2):
            T1[c, k] = zero
    my1 = row_mask(24, j * (NY // 2) - 8, count_y // 2)

    for c in range(6):
        cols = [pltpu.roll(W2[c + 2, k], (18 - 4 * j) % 16, 0)[0:8] for k in range(n2)]
        prolonged(T1.at[c], cols, 8, 4)
    for c in range(6):
        for p in (0, 1):
            x = 2 * c + p + 1
            m = plane_mask(my1, i * (NX // 2) + x - 5, count_x // 2)
            for k in range(n1):
                V1[x, k] = P1[x, k] + T1[c, k // 2] * m

    def sweep1(old, new, lo, hi):
        def body(x):
            m = plane_mask(my1, i * (NX // 2) + x - 5, count_x // 2)
            u, around_u = around(old, x)
            for k in range(n1):
                new[x, k] = (C0 * u[k] + D * (F1[x, k] + around_u[k])) * m

        each(lo, hi, body, hi - lo)

    sweep1(V1, X1, 2, 12)
    sweep1(X1, V1, 3, 11)


    my0 = row_mask(24, j * NY - 4, count_y)

    def start0(c):
        prolonged(T0.at[c], [V1[c + 3, k, 6:18, :] for k in range(n1)], 12)

    each(0, 8, start0, 4)

    def smooth0(x):
        m = plane_mask(my0, i * NX + x - 4, count_x)
        for k in range(nz):
            V0[x, k] = P0[x, k] + T0[x // 2, k // 2, 0:24, :] * m

    each(1, 15, smooth0, 4)

    def sweep0(old, new, lo, hi):
        def body(x):
            m = plane_mask(my0, i * NX + x - 4, count_x)
            u, around_u = around(old, x)
            for k in range(nz):
                new[x, k] = (C0 * u[k] + D * (F0[x, k] + around_u[k])) * m

        each(lo, hi, body, (hi - lo) // 2)

    sweep0(V0, X0, 2, 14)
    sweep0(X0, V0, 3, 13)

    def put(out, x, cols):
        for k, v in enumerate(regroup(cols)):
            out[x, :, k * LANES : (k + 1) * LANES] = v

    def rest(x):
        u = [V0[x + 4, k, 4:20, :] for k in range(nz)]
        before, after = along_z(u)
        res = []
        for k in range(nz):
            near = V0[x + 5, k, 4:20, :] + V0[x + 3, k, 4:20, :] + (V0[x + 4, k, 5:21, :] + V0[x + 4, k, 3:19, :])
            res.append(F0[x + 4, k, 4:20, :] - 6.0 * u[k] + (near + (before[k] + after[k])))
        put(resid, x, res)

    def away(t, a, b, s):
        return pltpu.make_async_copy(a.at[pl.ds(4 * s, 4)], b.at[pl.ds(4 * s, 4)], done.at[t, s])

    def give(s):
        for x in range(4):
            put(press, 4 * s + x, [V0[4 * s + x + 4, k, 4:20, :] for k in range(nz)])
        away(0, press, press_out, s).start()

    def give_rest(s):
        for x in range(4):
            rest(4 * s + x)
        away(1, resid, resid_out, s).start()

    each(0, NX // 4, give)
    each(0, NX // 4, give_rest)
    for s in range(NX // 4):
        away(0, press, press_out, s).wait()
        away(1, resid, resid_out, s).wait()


def call(kernel, outs, scratch, *args, away=False, mib=4, us=0.0):
    cost = pl.CostEstimate(flops=0, transcendentals=0, bytes_accessed=int(us * 3.6e6)) if us else None
    return pl.pallas_call(
        kernel,
        out_shape=[jax.ShapeDtypeStruct(s, f32) for s in outs],
        out_specs=[pl.BlockSpec(memory_space=pltpu.HBM) if away else pl.BlockSpec() for _ in outs],
        scratch_shapes=[pltpu.VMEM(s, f32) if isinstance(s, tuple) else s for s in scratch],
        compiler_params=pltpu.CompilerParams(vmem_limit_bytes=mib * 1024 * 1024),
        cost_estimate=cost,
    )(*args)


def swaps(leaves, subs):
    def table(partner):
        return [(i * subs + j, (lambda t: t[0] * subs + t[1])(partner(i, j))) for i in range(leaves) for j in range(subs)]

    def odd(n):
        return ((n + 1) ^ 1) - 1

    def inner(n, count):
        return 0 <= n < count

    a = table(lambda i, j: (i ^ 1, j))
    b = table(lambda i, j: (odd(i), j) if inner(odd(i), leaves) else (i, j ^ 1))
    s1 = table(lambda i, j: (i, j ^ 1))
    s2 = table(lambda i, j: (i, odd(j)) if inner(odd(j), subs) else (i ^ 1, j))
    c1 = table(lambda i, j: (i ^ 2, j))
    c2 = table(lambda i, j: (2 * odd(i // 2) + i % 2, j) if inner(odd(i // 2), leaves // 2) else (i ^ 1, j))

    def two_on(i):
        t = 2 * (i // 2 + (2 if i % 2 else -2)) + 1 - i % 2
        return t if inner(t, leaves) else None

    e = table(lambda i, j: (two_on(i), j) if two_on(i) is not None else (i ^ 2, j))
    return a, b, s1, s2, c1, c2, e


def shards(dims, volume_fraction, interface_mask):
    leaves, subs = dims
    depth = volume_fraction.shape[2]
    nz = depth // LANES
    pa, pb, ps1, ps2, pc1, pc2, pe = swaps(leaves, subs)
    move = lambda v, table: lax.ppermute(v, AXES, table)
    n1, n2, n3 = nz // 2, nz // 4, nz // 8

    plane, rows = (1, NY, depth), (NX, depth)
    to_a, to_b, to_1, to_2 = call(functools.partial(edges, dims), [plane, plane, rows, rows], [], volume_fraction)
    halos = move(to_a, pa), move(to_b, pb), move(to_1, ps1), move(to_2, ps2)
    shape = (NX, nz, NY, LANES)
    heights, slope = call(columns, [shape, shape], [], volume_fraction, us=1.5)
    (slope,) = call(masked, [shape], [], slope, interface_mask)
    (src,) = call(functools.partial(source, dims), [(NX, NY, depth)], [], heights, slope, *halos)
    big, m2b, own2 = call(
        functools.partial(descent, dims),
        [(8, NY, depth)] + [(2, 8, depth // 4)] * 2,
        [
            (6, 8, depth // 4),
            (16, nz, 24, LANES),
            (16, nz, 24, LANES),
            (8, nz, 32, LANES),
            (14, n1, 16, LANES),
            (14, n1, 16, LANES),
            (6, n1, 16, LANES),
        ],
        src,
        mib=10,
    )
    r2b, ra = move(m2b, pb), move(big, pa)
    out, to_b = call(
        functools.partial(middle, dims), [(2 * subs, 2, 8, depth // 4), (7, NY, depth)], [], own2, r2b, src, big, ra
    )
    rb = move(to_b, pb)
    group = [list(range(k, k + 2 * subs)) for k in range(0, leaves * subs, 2 * subs)]
    got = lax.all_to_all(out, AXES, 0, 0, axis_index_groups=group)
    got, rb = lax.optimization_barrier((got, rb))
    far = move(rb[4:7], pa)
    chips = leaves // 2
    f2, edge, out = call(
        functools.partial(chip2, dims),
        [(4, 16, depth // 4), (1, 16, depth // 4), (chips, 4, 8, depth // 8)],
        [(10, n2, 16, LANES), (10, n2, 16, LANES), (4, n2, 16, LANES)],
        got,
    )
    f1x, s1, s2 = call(
        functools.partial(rows_out, dims),
        [(14, 16, depth // 2), (15, 8, depth), (15, 8, depth)],
        [],
        src,
        big,
        ra,
        rb,
        far,
    )
    out, s1, s2 = lax.optimization_barrier((out, s1, s2))
    rs1, rs2 = move(s1, ps1), move(s2, ps2)
    group = [[(2 * c + k) * subs + s for c in range(chips)] for k in (0, 1) for s in range(subs)]
    got = lax.all_to_all(out, AXES, 0, 0, axis_index_groups=group)
    r2c1, r2c2, r2e = move(f2, pc1), move(f2, pc2), move(edge, pe)
    shape0, shape1 = (16, nz, 24, LANES), (14, n1, 24, LANES)
    F0, P0, F1, P1 = call(functools.partial(ready, dims), [shape0, shape0, shape1, shape1], [], src, ra, rb, f1x, rs1, rs2, mib=10)
    (u3,) = call(functools.partial(coarsest, dims), [(5, 8, depth // 8)], [(leaves + 18, 8, LANES)], got)
    return call(
        functools.partial(ascent, dims),
        [(NX, NY, depth), (NX, NY, depth)],
        [
            (14, n2, 16, LANES),
            (5, n3, 16, LANES),
            (10, n2, 16, LANES),
            (10, n2, 16, LANES),
            (6, n2, 24, LANES),
            shape1,
            shape1,
            (8, n1, 32, LANES),
            shape0,
            shape0,
            (NX, NY, depth),
            (NX, NY, depth),
            pltpu.SemaphoreType.DMA((2, NX // 4)),
        ],
        u3,
        f2,
        r2c1,
        r2c2,
        r2e,
        F0,
        P0,
        F1,
        P1,
        away=True,
        mib=16,
    )


def solution(mesh):
    spec = P("leaf", "sub", None)
    dims = (mesh.shape["leaf"], mesh.shape["sub"])
    body = functools.partial(shards, dims)
    return jax.shard_map(body, mesh=mesh, in_specs=(spec, spec), out_specs=(spec, spec), check_vma=False)
```

```python
import functools

import jax
import jax.numpy as jnp
from jax import lax
from jax.experimental import pallas as pl
from jax.experimental.pallas import tpu as pltpu
from jax.sharding import PartitionSpec as P

D = 0.8 / 6.0
C1 = 2.0 * D - 6.0 * D * D
C2 = D * D
C0 = 1.0 - 6.0 * D
NX, NY = 8, 16
LANES = 128
AXES = ("leaf", "sub")
f32 = jnp.float32


def lanes(rows):
    return lax.broadcasted_iota(jnp.int32, (rows, LANES), 1)


def rows_of(rows):
    return lax.broadcasted_iota(jnp.int32, (rows, LANES), 0)


def lane_before(col):
    lane = lanes(col.shape[0])
    wrapped = jnp.where(lane == 0, 0.0, pltpu.roll(col, 9, 1))
    return jnp.where(lane < 8, wrapped, pltpu.roll(col, 8, 1))


def lane_after(col):
    lane = lanes(col.shape[0])
    wrapped = jnp.where(lane == LANES - 1, 0.0, pltpu.roll(col, LANES - 9, 1))
    return jnp.where(lane >= LANES - 8, wrapped, pltpu.roll(col, LANES - 8, 1))


def along_z(cols):
    return [lane_before(cols[-1])] + cols[:-1], cols[1:] + [lane_after(cols[0])]


def regroup(cols):
    cols = list(cols)
    lane = lanes(cols[0].shape[0])
    for s in (1, 2, 4):
        low, beside = (lane & s) == 0, lane ^ s
        for a in range(8):
            b = a | s
            if a != b:
                moved = jnp.where(low, cols[b], cols[a])
                moved = jnp.take_along_axis(moved, beside, axis=1, mode="promise_in_bounds")
                cols[a], cols[b] = jnp.where(low, cols[a], moved), jnp.where(low, moved, cols[b])
    return cols


def around(ref, x, whole=False):
    n, rows = ref.shape[1], ref.shape[2]
    cols = [ref[x, k] for k in range(n)]
    before, after = along_z(cols)
    out = []
    for k, c in enumerate(cols):
        up, down = pltpu.roll(c, rows - 1, 0), pltpu.roll(c, 1, 0)
        if whole:
            row = rows_of(rows)
            up, down = jnp.where(row == rows - 1, 0.0, up), jnp.where(row == 0, 0.0, down)
        out.append((ref[x + 1, k] + ref[x - 1, k]) + (up + down) + (before[k] + after[k]))
    return cols, out


def restricted(tmp, rows):
    sums = [tmp[k, pl.ds(0, rows, 2), :] + tmp[k, pl.ds(1, rows, 2), :] for k in range(tmp.shape[0])]
    return [0.5 * (sums[2 * m] + sums[2 * m + 1]) for m in range(tmp.shape[0] // 2)]


def prolonged(tmp, cols, rows, at=0):
    for m, c in enumerate(cols):
        tmp[m, pl.ds(at, rows, 2), :] = c
        tmp[m, pl.ds(at + 1, rows, 2), :] = c


def inside(pos, count):
    return jnp.logical_and(pos >= 0, pos < count)


def row_mask(rows, start, count):
    pos = rows_of(rows) + start
    return jnp.where(inside(pos, count), 1.0, 0.0).astype(f32)


def plane_mask(mask, x, count):
    return mask * jnp.where(inside(x, count), 1.0, 0.0).astype(f32)


def each(lo, hi, body, together=1):
    steps = (hi - lo) // together

    def step(s, carry):
        for t in range(together):
            body(lo + s * together + t)
        return carry

    lax.fori_loop(0, steps, step, 0)
    for x in range(lo + steps * together, hi):
        body(x)


def taps(cols):
    n = len(cols)
    more = [lane_before(c) for c in cols[-3:]] + cols + [lane_after(c) for c in cols[:3]]
    out = [((more[k] + more[k + 1]) + (more[k + 2] + more[k + 3])) + ((more[k + 4] + more[k + 5]) + more[k + 6]) for k in range(n)]
    return out, more[2 : n + 2], more[4 : n + 4]


def split(value):
    return regroup(value[:, k * LANES : (k + 1) * LANES] for k in range(value.shape[1] // LANES))


def place(leaves, subs):
    i, j = lax.axis_index("leaf"), lax.axis_index("sub")
    odd_i, odd_j = i % 2 == 1, j % 2 == 1
    far_i = jnp.where(odd_i, i < leaves - 1, i > 0)
    far_j = jnp.where(odd_j, j < subs - 1, j > 0)
    return i, j, odd_i, odd_j, far_i, far_j


def edges(dims, vf, to_a, to_b, to_1, to_2):
    _, _, odd_i, odd_j, _, _ = place(*dims)
    to_a[0] = vf[jnp.where(odd_i, 0, NX - 1)]
    to_b[0] = vf[jnp.where(odd_i, NX - 1, 0)]
    first = jnp.concatenate([vf[x, 0:1, :] for x in range(NX)], axis=0)
    last = jnp.concatenate([vf[x, NY - 1 : NY, :] for x in range(NX)], axis=0)
    to_1[...] = jnp.where(odd_j, first, last)
    to_2[...] = jnp.where(odd_j, last, first)


def columns(vf, H, G):
    nz = vf.shape[2] // LANES

    def level0(x):
        h, before, after = taps(split(vf[x]))
        for k in range(nz):
            H[x, k] = h[k]
            G[x, k] = 0.5 * (after[k] - before[k])

    each(0, NX, level0, 4)


def masked(G, mask, out):
    def body(x):
        m = split(mask[x].astype(f32))
        for k in range(len(m)):
            out[x, k] = G[x, k] * m[k]

    each(0, NX, body, 8)


def source(dims, H, G, ra, rb, rs1, rs2, src):
    _, _, odd_i, odd_j, far_i, far_j = place(*dims)
    nz = H.shape[1]
    far_x = jnp.where(far_i, 1.0, 0.0).astype(f32)
    far_y = jnp.where(far_j, 1.0, 0.0).astype(f32)
    ha, _, _ = taps(split(ra[0]))
    hb, _, _ = taps(split(rb[0]))
    hs1, _, _ = taps(split(rs1[...]))
    hs2, _, _ = taps(split(rs2[...]))
    row = rows_of(NY)
    for k in range(nz):
        b = hb[k] * far_x
        below, above = jnp.where(odd_i, ha[k], b), jnp.where(odd_i, b, ha[k])
        low = jnp.where(odd_j, hs1[k], hs2[k] * far_y)
        high = jnp.where(odd_j, hs2[k] * far_y, hs1[k])
        for x in range(NX):
            h = H[x, k]
            up = jnp.where(row == NY - 1, high[x : x + 1, :], pltpu.roll(h, NY - 1, 0))
            down = jnp.where(row == 0, low[x : x + 1, :], pltpu.roll(h, 1, 0))
            ahead = H[x + 1, k] if x < NX - 1 else above
            behind = H[x - 1, k] if x > 0 else below
            sx, sy = 0.5 * (ahead - behind), 0.5 * (up - down)
            bend = ahead - 2.0 * h + behind + (up - 2.0 * h + down)
            inv = lax.rsqrt(1.0 + sx * sx + sy * sy)
            src[x, :, k * LANES : (k + 1) * LANES] = G[x, k] * (bend * (inv * inv * inv))


def descent(dims, src, big, m2b, own2, F1c, F0, U0, T0, F1, U1, T1):
    leaves, subs = dims
    i, j, odd_i, odd_j, far_i, far_j = place(leaves, subs)
    nz = src.shape[2] // LANES
    zero = jnp.zeros((16, LANES), f32)
    zero24 = jnp.zeros((24, LANES), f32)
    for x in range(16):
        for k in range(nz):
            if 4 <= x < 12:
                own = src[x - 4, :, k * LANES : (k + 1) * LANES]
                F0[x, k] = jnp.concatenate([zero[0:4], own, zero[0:4]], axis=0)
            else:
                F0[x, k] = zero24

    count_x, count_y = leaves * NX, subs * NY
    my0 = row_mask(24, j * NY - 4, count_y)
    for x in (1, 2, 13, 14):
        for k in range(nz):
            U0[x, k] = zero24

    def smooth0(x):
        m = plane_mask(my0, i * NX + x - 4, count_x)
        f, around_f = around(F0, x)
        for k in range(nz):
            U0[x, k] = (C1 * f[k] + C2 * around_f[k]) * m

    each(3, 13, smooth0, 10)

    for x in range(0, 14):
        if x < 4 or x >= 10:
            for k in range(nz // 2):
                F1[x, k] = zero

    def restrict0(c):
        total = [zero24] * nz
        for p in (0, 1):
            x = 2 * c + p
            m = plane_mask(my0, i * NX + x - 4, count_x)
            u, around_u = around(U0, x)
            total = [total[k] + (F0[x, k] - 6.0 * u[k] + around_u[k]) * m for k in range(nz)]
        for k in range(nz):
            T0[c, k, 0:24, :] = total[k]
        for k, v in enumerate(restricted(T0.at[c], 12)):
            F1[c + 3, k] = jnp.concatenate([zero[0:2], v, zero[0:2]], axis=0)

    each(1, 7, restrict0, 6)

    n1 = nz // 2
    my1 = row_mask(16, j * (NY // 2) - 4, count_y // 2)
    for x in (0, 1, 2, 11, 12, 13):
        for k in range(n1):
            U1[x, k] = zero

    def smooth1(x):
        m = plane_mask(my1, i * (NX // 2) + x - 5, count_x // 2)
        f, around_f = around(F1, x)
        for k in range(n1):
            U1[x, k] = (C1 * f[k] + C2 * around_f[k]) * m

    each(3, 11, smooth1, 8)

    def restrict1(c):
        total = [zero] * n1
        for p in (0, 1):
            x = 2 * c + 1 + p
            m = plane_mask(my1, i * (NX // 2) + x - 5, count_x // 2)
            u, around_u = around(U1, x)
            total = [total[k] + (F1[x, k] - 6.0 * u[k] + around_u[k]) * m for k in range(n1)]
        for k in range(n1):
            T1[c, k] = total[k]
        for k, v in enumerate(restricted(T1.at[c], 8)):
            F1c[c, :, k * LANES : (k + 1) * LANES] = v

    each(0, 6, restrict1, 6)

    at = jnp.where(odd_i, 0, 4)
    for x in (0, 1):
        big[7, 0:8, x * 2 * LANES : (x + 1) * 2 * LANES] = F1c[at + x]
    m2b[...] = F1c[pl.ds(4 - at, 2)]
    own2[...] = F1c[2:4]
    big[0:4] = src[pl.ds(at, 4)]
    for p in range(3):
        for k in range(n1):
            for h in (0, 1):
                big[4 + p, :, (h * n1 + k) * LANES : (h * n1 + k + 1) * LANES] = F1[4 + p + 3 * h, k]


def half_planes(ref, p):
    n = ref.shape[2] // 2
    return ref[4 + p % 3, :, (p // 3) * n : (p // 3 + 1) * n]


def middle(dims, own2, r2b, src, big, ra, out, to_b):
    _, _, odd_i, _, far_i, _ = place(*dims)
    n = src.shape[2] // 2
    for x in (0, 1):
        v = own2[x] + ra[7, 0:8, x * 2 * LANES : (x + 1) * 2 * LANES] + jnp.where(far_i, r2b[x], 0.0)
        for k in range(out.shape[0]):
            out[k, x] = v
    to_b[0:4] = src[pl.ds(jnp.where(odd_i, 4, 0), 4)]
    more = {
        0: jnp.where(odd_i, half_planes(ra, 4), 0.0),
        1: jnp.where(odd_i, half_planes(ra, 5), 0.0),
        4: jnp.where(odd_i, 0.0, half_planes(ra, 0)),
        5: jnp.where(odd_i, 0.0, half_planes(ra, 1)),
    }
    for p in range(6):
        v = half_planes(big, p)
        to_b[4 + p % 3, :, (p // 3) * n : (p // 3 + 1) * n] = v + more[p] if p in more else v


def chip2(dims, got, f2, edge, out, F2, U2, T2):
    leaves, subs = dims
    i = lax.axis_index("leaf")
    odd_i, c = i % 2 == 1, i // 2
    n2 = f2.shape[2] // LANES
    row = rows_of(8)
    zero = jnp.zeros((16, LANES), f32)
    for x in (0, 1, 2, 7, 8, 9):
        for k in range(n2):
            F2[x, k] = zero
    for x in (0, 1, 8, 9):
        for k in range(n2):
            U2[x, k] = zero
    for x in range(4):
        for k in range(n2):
            s = slice(k * LANES, (k + 1) * LANES)
            t = [got[4 * (x // 2) + j, x % 2, :, s] for j in range(4)]
            one, two = pltpu.roll(t[1], 2, 0), pltpu.roll(t[2], 6, 0)
            lo = jnp.where(row < 6, pltpu.roll(t[0], 6, 0), two) + jnp.where(row >= 2, one, 0.0)
            hi = jnp.where(row >= 2, pltpu.roll(t[3], 2, 0), one) + jnp.where(row < 6, two, 0.0)
            f2[x, 0:8, s] = lo
            f2[x, 8:16, s] = hi
            F2[x + 3, k, 0:8, :] = lo
            F2[x + 3, k, 8:16, :] = hi
    edge[0] = f2[jnp.where(odd_i, 3, 0)]
    m2 = jnp.ones((16, LANES), f32)
    for x in range(2, 8):
        m = plane_mask(m2, 4 * c + x - 3, 2 * leaves)
        f, around_f = around(F2, x, True)
        for k in range(n2):
            U2[x, k] = (C1 * f[k] + C2 * around_f[k]) * m
    for q in range(4):
        total = [zero] * n2
        for x in (2 * q + 1, 2 * q + 2):
            m = plane_mask(m2, 4 * c + x - 3, 2 * leaves)
            u, around_u = around(U2, x, True)
            total = [total[k] + (F2[x, k] - 6.0 * u[k] + around_u[k]) * m for k in range(n2)]
        for k in range(n2):
            T2[q, k] = total[k]
    for q in range(4):
        for k, v in enumerate(restricted(T2.at[q], 8)):
            for t in range(out.shape[0]):
                out[t, q, :, k * LANES : (k + 1) * LANES] = in_order(v)


def rows_out(dims, src, big, ra, rb, far, f1x, s1, s2):
    _, _, odd_i, odd_j, far_i, _ = place(*dims)
    i = lax.axis_index("leaf")
    n = src.shape[2] // 2
    a = [half_planes(ra, p) for p in range(6)]
    b = [jnp.where(far_i, half_planes(rb, p), 0.0) for p in range(6)]
    before = [jnp.where(odd_i, a[p], b[p]) for p in range(6)]
    after = [jnp.where(odd_i, b[p], a[p]) for p in range(6)]
    far_two = jnp.where(odd_i, i > 1, i < dims[0] - 2)
    d = [jnp.where(far_two, far[p % 3, :, (p // 3) * n : (p // 3 + 1) * n], 0.0) for p in (0, 1, 4, 5)]
    before2 = [jnp.where(odd_i, d[2 + h], 0.0) for h in (0, 1)]
    after2 = [jnp.where(odd_i, 0.0, d[h]) for h in (0, 1)]
    own = [half_planes(big, p) for p in range(6)]
    planes = {}

    def add(x, v):
        planes[x] = planes[x] + v if x in planes else v

    for p in range(6):
        add(p - 1, own[p])
        add(p - 5, before[p])
        add(p + 3, after[p])
    for h in (0, 1):
        add(-5 + h, before2[h])
        add(7 + h, after2[h])
    for x in range(14):
        f1x[x] = planes[x - 5]

    def fine(x):
        if 4 <= x < 12:
            return src[x - 4]
        if x < 4:
            return jnp.where(odd_i, ra[x], jnp.where(far_i, rb[x], 0.0))
        return jnp.where(odd_i, jnp.where(far_i, rb[x - 12], 0.0), ra[x - 12])

    for x in range(8):
        u, v = fine(x), fine(x + 8)
        for out, up in ((s1, odd_j == False), (s2, odd_j)):
            out[x] = jnp.concatenate([jnp.where(up, u[12:16], u[0:4]), jnp.where(up, v[12:16], v[0:4])], axis=0)
    for x in range(14):
        v = planes[x - 5]
        s = slice((x // 7) * n, (x // 7 + 1) * n)
        last, first = v[5:13], v[3:11]
        s1[8 + x % 7, :, s] = jnp.where(odd_j, first, last)
        s2[8 + x % 7, :, s] = jnp.where(odd_j, last, first)


def in_order(col):
    lane = lanes(col.shape[0])
    return jnp.take_along_axis(col, 8 * (lane % 16) + lane // 16, axis=1, mode="promise_in_bounds")


def as_kept(col):
    lane = lanes(col.shape[0])
    return jnp.take_along_axis(col, 16 * (lane % 8) + lane // 8, axis=1, mode="promise_in_bounds")


def coarsest(dims, got, out, G3):
    leaves = dims[0]
    chips = got.shape[0]
    i = lax.axis_index("leaf")
    zero = jnp.zeros((8, LANES), f32)
    for x in range(9):
        G3[x] = zero
        G3[leaves + 9 + x] = zero
    for c in range(chips):
        a, b = got[c, 1], got[c, 2]
        if c > 0:
            a = a + got[c - 1, 3]
        if c < chips - 1:
            b = b + got[c + 1, 0]
        G3[2 * c + 9], G3[2 * c + 10] = a, b
    lane, row = lanes(8), rows_of(8)
    ends = [lane == 0, lane == LANES - 1, row == 0, row == 7]
    f = [D * G3[i + w] for w in range(19)]
    keep = [jnp.where(inside(i + w - 9, leaves), 1.0, 0.0).astype(f32) for w in range(19)]
    u = list(f)
    for s in range(1, 8):
        new = list(u)
        for w in range(s, 19 - s):
            c = u[w]
            z = jnp.where(ends[0], 0.0, pltpu.roll(c, 1, 1)) + jnp.where(ends[1], 0.0, pltpu.roll(c, LANES - 1, 1))
            y = jnp.where(ends[2], 0.0, pltpu.roll(c, 1, 0)) + jnp.where(ends[3], 0.0, pltpu.roll(c, 7, 0))
            new[w] = (C0 * c + (f[w] + D * ((u[w + 1] + u[w - 1]) + (y + z)))) * keep[w]
        u = new
    for x in range(5):
        out[x] = as_kept(u[7 + x])


def ready(dims, src, ra, rb, f1x, rs1, rs2, F0, P0, F1, P1):
    leaves, subs = dims
    i, j, odd_i, odd_j, far_i, far_j = place(leaves, subs)
    count_x, count_y = leaves * NX, subs * NY
    nz = src.shape[2] // LANES
    n1 = nz // 2
    zero = jnp.zeros((24, LANES), f32)
    far_x = jnp.where(far_i, 1.0, 0.0).astype(f32)

    low_j = jnp.where(j > 0, 1.0, 0.0).astype(f32)
    high_j = jnp.where(j < subs - 1, 1.0, 0.0).astype(f32)

    def fill1(x):
        part, at = x // 7, 8 + x % 7
        for k in range(n1):
            s = slice(k * LANES, (k + 1) * LANES)
            F1[x, k] = zero
            F1[x, k, 4:20, :] = f1x[x, :, s]
            s = slice((part * n1 + k) * LANES, (part * n1 + k + 1) * LANES)
            lo = jnp.where(odd_j, rs1[at, :, s], rs2[at, :, s]) * low_j
            hi = jnp.where(odd_j, rs2[at, :, s], rs1[at, :, s]) * high_j
            F1[x, k, 1:9, :] = F1[x, k, 1:9, :] + lo
            F1[x, k, 15:23, :] = F1[x, k, 15:23, :] + hi

    for x in range(14):
        fill1(x)
    my1 = row_mask(24, j * (NY // 2) - 8, count_y // 2)

    def smooth1(x):
        m = plane_mask(my1, i * (NX // 2) + x - 5, count_x // 2)
        f, around_f = around(F1, x)
        for k in range(n1):
            P1[x, k] = (C1 * f[k] + C2 * around_f[k]) * m

    each(1, 13, smooth1, 12)

    def fill0(x):
        if 4 <= x < 12:
            v = src[x - 4]
        elif x < 4:
            v = jnp.where(odd_i, ra[x], rb[x] * far_x)
        else:
            v = jnp.where(odd_i, rb[x - 12] * far_x, ra[x - 12])
        a, b = rs1[x % 8], rs2[x % 8]
        h = 4 * (x // 8)
        lo = jnp.where(odd_j, a[h : h + 4], b[h : h + 4]) * low_j
        hi = jnp.where(odd_j, b[h : h + 4], a[h : h + 4]) * high_j
        for k in range(nz):
            s = slice(k * LANES, (k + 1) * LANES)
            F0[x, k] = jnp.concatenate([lo[:, s], v[:, s], hi[:, s]], axis=0)

    for x in range(16):
        fill0(x)
    my0 = row_mask(24, j * NY - 4, count_y)

    def smooth0(x):
        m = plane_mask(my0, i * NX + x - 4, count_x)
        f, around_f = around(F0, x)
        for k in range(nz):
            P0[x, k] = (C1 * f[k] + C2 * around_f[k]) * m

    each(1, 15, smooth0, 14)


def ascent(dims, u3, f2, r2c1, r2c2, r2e, F0, P0, F1, P1, press_out, resid_out, F2, T2, W2, X2, T1, V1, X1, T0, V0, X0, press, resid, done):
    leaves, subs = dims
    i, j, odd_i, odd_j, far_i, far_j = place(leaves, subs)
    count_x, count_y = leaves * NX, subs * NY
    nz = F0.shape[1]
    n1, n2, n3 = nz // 2, nz // 4, nz // 8
    zero = jnp.zeros((24, LANES), f32)

    c, chips = i // 2, leaves // 2
    odd_c = c % 2 == 1
    far_c = jnp.where(jnp.where(odd_c, c < chips - 1, c > 0), 1.0, 0.0).astype(f32)
    far_e = jnp.where(jnp.where(odd_i, c < chips - 2, c > 1), 1.0, 0.0).astype(f32)
    base = jnp.where(odd_i, 2, 0)
    for k in range(n2):
        s = slice(k * LANES, (k + 1) * LANES)
        e = r2e[0, :, s] * far_e
        F2[0, k] = e
        F2[13, k] = e
        for x in range(4):
            a, b = r2c1[x, :, s], r2c2[x, :, s] * far_c
            F2[x + 1, k] = jnp.where(odd_c, a, b)
            F2[x + 5, k] = f2[x, :, s]
            F2[x + 9, k] = jnp.where(odd_c, b, a)
    m2 = jnp.ones((16, LANES), f32)
    for x in range(5):
        prolonged(T2.at[x], [u3[x, :, k * LANES : (k + 1) * LANES] for k in range(n3)], 8)
    for w in range(10):
        m = plane_mask(m2, 2 * i + w - 4, 2 * leaves)
        f, around_f = around(F2, base + w + 1, True)
        for k in range(n2):
            W2[w, k] = (C1 * f[k] + C2 * around_f[k] + T2[w // 2, k // 2]) * m

    def sweep2(old, new, lo, hi):
        for w in range(lo, hi):
            m = plane_mask(m2, 2 * i + w - 4, 2 * leaves)
            u, around_u = around(old, w, True)
            for k in range(n2):
                new[w, k] = (C0 * u[k] + D * (F2[base + w + 1, k] + around_u[k])) * m

    sweep2(W2, X2, 1, 9)
    sweep2(X2, W2, 2, 8)

    for c in range(6):
        for k in range(n2):
            T1[c, k] = zero
    my1 = row_mask(24, j * (NY // 2) - 8, count_y // 2)

    for c in range(6):
        cols = [pltpu.roll(W2[c + 2, k], (18 - 4 * j) % 16, 0)[0:8] for k in range(n2)]
        prolonged(T1.at[c], cols, 8, 4)
    for c in range(6):
        for p in (0, 1):
            x = 2 * c + p + 1
            m = plane_mask(my1, i * (NX // 2) + x - 5, count_x // 2)
            for k in range(n1):
                V1[x, k] = P1[x, k] + T1[c, k // 2] * m

    def sweep1(old, new, lo, hi):
        def body(x):
            m = plane_mask(my1, i * (NX // 2) + x - 5, count_x // 2)
            u, around_u = around(old, x)
            for k in range(n1):
                new[x, k] = (C0 * u[k] + D * (F1[x, k] + around_u[k])) * m

        each(lo, hi, body, hi - lo)

    sweep1(V1, X1, 2, 12)
    sweep1(X1, V1, 3, 11)


    my0 = row_mask(24, j * NY - 4, count_y)

    def start0(c):
        prolonged(T0.at[c], [V1[c + 3, k, 6:18, :] for k in range(n1)], 12)

    each(0, 8, start0, 4)

    def smooth0(x):
        m = plane_mask(my0, i * NX + x - 4, count_x)
        for k in range(nz):
            V0[x, k] = P0[x, k] + T0[x // 2, k // 2, 0:24, :] * m

    each(1, 15, smooth0, 4)

    def sweep0(old, new, lo, hi):
        def body(x):
            m = plane_mask(my0, i * NX + x - 4, count_x)
            u, around_u = around(old, x)
            for k in range(nz):
                new[x, k] = (C0 * u[k] + D * (F0[x, k] + around_u[k])) * m

        each(lo, hi, body, 4)

    sweep0(V0, X0, 2, 14)
    sweep0(X0, V0, 3, 13)

    def put(out, x, cols):
        for k, v in enumerate(regroup(cols)):
            out[x, :, k * LANES : (k + 1) * LANES] = v

    def rest(x):
        u = [V0[x + 4, k, 4:20, :] for k in range(nz)]
        before, after = along_z(u)
        res = []
        for k in range(nz):
            near = V0[x + 5, k, 4:20, :] + V0[x + 3, k, 4:20, :] + (V0[x + 4, k, 5:21, :] + V0[x + 4, k, 3:19, :])
            res.append(F0[x + 4, k, 4:20, :] - 6.0 * u[k] + (near + (before[k] + after[k])))
        put(resid, x, res)

    def away(t, a, b, s):
        return pltpu.make_async_copy(a.at[pl.ds(4 * s, 4)], b.at[pl.ds(4 * s, 4)], done.at[t, s])

    def give(s):
        for x in range(4):
            put(press, 4 * s + x, [V0[4 * s + x + 4, k, 4:20, :] for k in range(nz)])
        away(0, press, press_out, s).start()

    def give_rest(s):
        for x in range(4):
            rest(4 * s + x)
        away(1, resid, resid_out, s).start()

    each(0, NX // 4, give)
    each(0, NX // 4, give_rest)
    for s in range(NX // 4):
        away(0, press, press_out, s).wait()
        away(1, resid, resid_out, s).wait()


def call(kernel, outs, scratch, *args, away=False, mib=4, us=0.0):
    cost = pl.CostEstimate(flops=0, transcendentals=0, bytes_accessed=int(us * 3.6e6)) if us else None
    return pl.pallas_call(
        kernel,
        out_shape=[jax.ShapeDtypeStruct(s, f32) for s in outs],
        out_specs=[pl.BlockSpec(memory_space=pltpu.HBM) if away else pl.BlockSpec() for _ in outs],
        scratch_shapes=[pltpu.VMEM(s, f32) if isinstance(s, tuple) else s for s in scratch],
        compiler_params=pltpu.CompilerParams(vmem_limit_bytes=mib * 1024 * 1024),
        cost_estimate=cost,
    )(*args)


def swaps(leaves, subs):
    def table(partner):
        return [(i * subs + j, (lambda t: t[0] * subs + t[1])(partner(i, j))) for i in range(leaves) for j in range(subs)]

    def odd(n):
        return ((n + 1) ^ 1) - 1

    def inner(n, count):
        return 0 <= n < count

    a = table(lambda i, j: (i ^ 1, j))
    b = table(lambda i, j: (odd(i), j) if inner(odd(i), leaves) else (i, j ^ 1))
    s1 = table(lambda i, j: (i, j ^ 1))
    s2 = table(lambda i, j: (i, odd(j)) if inner(odd(j), subs) else (i ^ 1, j))
    c1 = table(lambda i, j: (i ^ 2, j))
    c2 = table(lambda i, j: (2 * odd(i // 2) + i % 2, j) if inner(odd(i // 2), leaves // 2) else (i ^ 1, j))

    def two_on(i):
        t = 2 * (i // 2 + (2 if i % 2 else -2)) + 1 - i % 2
        return t if inner(t, leaves) else None

    e = table(lambda i, j: (two_on(i), j) if two_on(i) is not None else (i ^ 2, j))
    return a, b, s1, s2, c1, c2, e


def shards(dims, volume_fraction, interface_mask):
    leaves, subs = dims
    depth = volume_fraction.shape[2]
    nz = depth // LANES
    pa, pb, ps1, ps2, pc1, pc2, pe = swaps(leaves, subs)
    move = lambda v, table: lax.ppermute(v, AXES, table)
    n1, n2, n3 = nz // 2, nz // 4, nz // 8

    plane, rows = (1, NY, depth), (NX, depth)
    to_a, to_b, to_1, to_2 = call(functools.partial(edges, dims), [plane, plane, rows, rows], [], volume_fraction)
    halos = move(to_a, pa), move(to_b, pb), move(to_1, ps1), move(to_2, ps2)
    shape = (NX, nz, NY, LANES)
    heights, slope = call(columns, [shape, shape], [], volume_fraction, us=1.5)
    (slope,) = call(masked, [shape], [], slope, interface_mask)
    (src,) = call(functools.partial(source, dims), [(NX, NY, depth)], [], heights, slope, *halos)
    big, m2b, own2 = call(
        functools.partial(descent, dims),
        [(8, NY, depth)] + [(2, 8, depth // 4)] * 2,
        [
            (6, 8, depth // 4),
            (16, nz, 24, LANES),
            (16, nz, 24, LANES),
            (8, nz, 32, LANES),
            (14, n1, 16, LANES),
            (14, n1, 16, LANES),
            (6, n1, 16, LANES),
        ],
        src,
        mib=10,
    )
    r2b, ra = move(m2b, pb), move(big, pa)
    out, to_b = call(
        functools.partial(middle, dims), [(2 * subs, 2, 8, depth // 4), (7, NY, depth)], [], own2, r2b, src, big, ra
    )
    rb = move(to_b, pb)
    group = [list(range(k, k + 2 * subs)) for k in range(0, leaves * subs, 2 * subs)]
    got = lax.all_to_all(out, AXES, 0, 0, axis_index_groups=group)
    got, rb = lax.optimization_barrier((got, rb))
    far = move(rb[4:7], pa)
    chips = leaves // 2
    f2, edge, out = call(
        functools.partial(chip2, dims),
        [(4, 16, depth // 4), (1, 16, depth // 4), (chips, 4, 8, depth // 8)],
        [(10, n2, 16, LANES), (10, n2, 16, LANES), (4, n2, 16, LANES)],
        got,
    )
    f1x, s1, s2 = call(
        functools.partial(rows_out, dims),
        [(14, 16, depth // 2), (15, 8, depth), (15, 8, depth)],
        [],
        src,
        big,
        ra,
        rb,
        far,
    )
    out, s1, s2 = lax.optimization_barrier((out, s1, s2))
    rs1, rs2 = move(s1, ps1), move(s2, ps2)
    group = [[(2 * c + k) * subs + s for c in range(chips)] for k in (0, 1) for s in range(subs)]
    got = lax.all_to_all(out, AXES, 0, 0, axis_index_groups=group)
    r2c1, r2c2, r2e = move(f2, pc1), move(f2, pc2), move(edge, pe)
    shape0, shape1 = (16, nz, 24, LANES), (14, n1, 24, LANES)
    F0, P0, F1, P1 = call(functools.partial(ready, dims), [shape0, shape0, shape1, shape1], [], src, ra, rb, f1x, rs1, rs2, mib=10)
    (u3,) = call(functools.partial(coarsest, dims), [(5, 8, depth // 8)], [(leaves + 18, 8, LANES)], got)
    return call(
        functools.partial(ascent, dims),
        [(NX, NY, depth), (NX, NY, depth)],
        [
            (14, n2, 16, LANES),
            (5, n3, 16, LANES),
            (10, n2, 16, LANES),
            (10, n2, 16, LANES),
            (6, n2, 24, LANES),
            shape1,
            shape1,
            (8, n1, 32, LANES),
            shape0,
            shape0,
            (NX, NY, depth),
            (NX, NY, depth),
            pltpu.SemaphoreType.DMA((2, NX // 4)),
        ],
        u3,
        f2,
        r2c1,
        r2c2,
        r2e,
        F0,
        P0,
        F1,
        P1,
        away=True,
        mib=16,
    )


def solution(mesh):
    spec = P("leaf", "sub", None)
    dims = (mesh.shape["leaf"], mesh.shape["sub"])
    body = functools.partial(shards, dims)
    return jax.shard_map(body, mesh=mesh, in_specs=(spec, spec), out_specs=(spec, spec), check_vma=False)
```
